32 devices in a mesh: dp: 8 (over y, x, core), tensor: 4 (over z).
Axes of the slice: x: 2, y: 2, z: 4, core: 2. Of those that a mesh axis runs over, the one named last changes fastest.
Arguments:
- tokens: bfloat16 [2048, 2048], P('dp'), may hold values from -6 to 6
- cotangent: bfloat16 [2048, 2048], P('dp'), may hold values from -6 to 6
- attn_gain: float32 [2048], replicated, may hold values from 0.5 to 1.5
- q_weight: bfloat16 [2048, 3072], P(None, 'tensor'), may hold values from -0.125 to 0.125
- kv_down: bfloat16 [2048, 512], P(None, 'tensor'), may hold values from -0.125 to 0.125
- k_rope_weight: bfloat16 [2048, 64], P(None, 'tensor'), may hold values from -0.125 to 0.125
- kv_gain: float32 [512], replicated, may hold values from 0.5 to 1.5
- kv_up: bfloat16 [512, 4096], P(None, 'tensor'), may hold values from -0.25 to 0.25
- o_weight: bfloat16 [2048, 2048], P('tensor'), may hold values from -0.5 to 0.5
- ffn_gain: float32 [2048], replicated, may hold values from 0.5 to 1.5
- router_weight: float32 [2048, 32], replicated, may hold values from -0.0625 to 0.0625
- expert_ids: int32 [2048, 6], P('dp'), may hold values from 0 to 31, all different within a row; in each aligned block of 256 rows (0 to 255, 256 to 511, ...) at most 64 rows name the same one
- expert_gate: bfloat16 [32, 2048, 1408], P('dp', None, 'tensor'), may hold values from -0.125 to 0.125
- expert_up: bfloat16 [32, 2048, 1408], P('dp', None, 'tensor'), may hold values from -0.125 to 0.125
- expert_down: bfloat16 [32, 1408, 2048], P('dp', 'tensor'), may hold values from -6 to 6
- shared_gate: bfloat16 [2048, 2816], P(None, 'tensor'), may hold values from -0.125 to 0.125
- shared_up: bfloat16 [2048, 2816], P(None, 'tensor'), may hold values from -0.125 to 0.125
- shared_down: bfloat16 [2816, 2048], P('tensor'), may hold values from -0.109375 to 0.109375
Outputs:
- output: bfloat16 [2048, 2048], P('dp')
- input_grad: float32 [2048, 2048], P(('dp', 'tensor'))
- attn_gain_grad: float32 [2048], P(('dp', 'tensor'))
- q_weight_grad: float32 [2048, 3072], P('dp', 'tensor')
- kv_down_grad: float32 [2048, 512], P('dp', 'tensor')
- k_rope_grad: float32 [2048, 64], P('dp', 'tensor')
- kv_gain_grad: float32 [512], P(('dp', 'tensor'))
- kv_up_grad: float32 [512, 4096], P('dp', 'tensor')
- o_weight_grad: float32 [2048, 2048], P('tensor', 'dp')
- ffn_gain_grad: float32 [2048], P(('dp', 'tensor'))
- router_grad: float32 [2048, 32], P(('dp', 'tensor'))
- shared_gate_grad: float32 [2048, 2816], P('dp', 'tensor')
- shared_up_grad: float32 [2048, 2816], P('dp', 'tensor')
- shared_down_grad: float32 [2816, 2048], P('tensor', 'dp')
- expert_gate_grad: float32 [32, 2048, 1408], P('dp', None, 'tensor')
- expert_up_grad: float32 [32, 2048, 1408], P('dp', None, 'tensor')
- expert_down_grad: float32 [32, 1408, 2048], P('dp', 'tensor')
The draws below stay inside these ranges and needn't reach their ends.
Inputs may be any that keep to these rules, and one draw needn't show every extreme that they name: `expert_ids`: each row names 6 different experts; among the 256 tokens of one index of dp no expert is named more than 64 times.
All inputs are finite; a program needn't handle non-finite values.
Results may differ from the reference program's by a relative error of at most 0.02.
Values may be sent and summed in bfloat16 or wider, within the bound.
No kernel may reach another device: no remote copies, remote signals or barrier semaphores. Data moves between devices by JAX's collectives and lax.ppermute only.
A program may use at most 320 MiB of HBM per device.

```python
import math
import jax
import jax.numpy as jnp
import numpy as np
from jax import lax

D = 2048
H = 16
HD = 128
RD = 64
VD = 128
KVR = 512
FF_E = 1408
FF_S = 2816
TOPK = 6
EXPERTS = 32
SEQ = 256
CAP = 64
TOK_DEV = 256
TOKENS = 2048
N_DP = 8
N_TENSOR = 4


def shard_levels(rng, shape, cuts, low, top_value):
    factor_of = 1.0
    for position, parts in cuts:
        draws = jax.random.uniform(jax.random.fold_in(jax.random.fold_in(rng, 6), position), (parts,), jnp.float32, low / len(cuts), top_value / len(cuts))
        factor_of = factor_of * jnp.repeat(jnp.exp(draws), shape[position] // parts).reshape((-1,) + (1,) * (len(shape) - 1 - position))
    return factor_of


def assign_block(stream_key, own, number, rows, number_of, top, most, slope):
    order = jax.random.permutation(stream_key, number_of)
    crowded, usual = shares(number_of, rows * top, most, slope, True), shares(number_of, rows * top, most, slope, False)
    places = jnp.arange(number_of)

    def named(sizes, turn):
        used = int((sizes > 0).sum())
        fixed = max(1, used // 4)
        moved = fixed + (places - fixed + turn * (used - fixed)) % max(1, number_of - fixed)
        return jnp.zeros((number_of,), jnp.int32).at[order[jnp.where(places < fixed, places, moved)]].set(jnp.asarray(sizes, jnp.int32))

    sizes = jnp.where(number % 4 == 0, named(crowded, number // 4), named(usual, number - number // 4 - 1))
    mixed = jax.random.permutation(jax.random.fold_in(own, 3), number_of)
    source_of, sink = mixed[0:number_of // 2 * 2:2], mixed[1:number_of // 2 * 2:2]
    room = jnp.minimum(sizes[source_of] - 1, most - sizes[sink]) // 2
    room = jnp.where((source_of == order[0]) | (sink == order[0]) | (sizes[sink] == 0), 0, jnp.maximum(room, 0))
    moved = jax.random.randint(jax.random.fold_in(own, 4), (number_of // 2,), 0, 1 << 20) % (room + 1)
    sizes = sizes.at[source_of].add(-moved).at[sink].add(moved)
    labels = jnp.searchsorted(jnp.cumsum(sizes), jnp.arange(rows * top), side="right").astype(jnp.int32)
    grid = labels.reshape(top, rows).T
    grid = grid[jax.random.permutation(jax.random.fold_in(own, 1), rows)]
    turn = jax.random.randint(jax.random.fold_in(own, 2), (rows, 1), 0, top)
    return jnp.take_along_axis(grid, (jnp.arange(top)[None, :] + turn) % top, axis=1)


def shares(count, total, limit, lean, full):
    portions = [(1 << 20) // math.isqrt(grade ** lean) + 1 for grade in range(1, count + 1)]
    largest = limit if full else min(limit, max(-(-total // count), total * portions[0] // sum(portions)))
    least = 1 if total - largest >= count - 1 else 0
    given, spare = [largest] + [least] * (count - 1), total - largest - least * (count - 1)
    while spare > 0:
        candidates = [i for i in range(1, count) if given[i] < largest] or [i for i in range(1, count) if given[i] < limit]
        whole, budget = sum([portions[i] for i in candidates]), spare
        for i in candidates:
            addition = min(limit - given[i], max(1, budget * portions[i] // whole), spare)
            given[i] = given[i] + addition
            spare = spare - addition
    return np.array(given)


def bell_draw(key, extent, scale, reach, pieces=(), kind=jnp.bfloat16):
    drawn = scale * jax.random.normal(key, extent, jnp.float32)
    if pieces:
        drawn = drawn * shard_levels(key, extent, pieces, -0.22, 0.18)
    return jnp.clip(drawn, -reach, reach).astype(kind)


def setup_inputs(seed: int = 0) -> dict:
    streams_of = jax.random.split(jax.random.key(seed), 19)
    tokens = bell_draw(streams_of[0], (TOKENS, D), 1.0, 6.0, ((0, 8),))
    cotangent = bell_draw(streams_of[1], (TOKENS, D), 1.0, 6.0, ((0, 8),))
    attn_gain = jnp.clip(1.0 + 0.1 * jax.random.normal(streams_of[2], (D,), jnp.float32), 0.5, 1.5)
    q_weight = bell_draw(streams_of[3], (D, H * (HD + RD)), D ** -0.5, 0.125, ((1, 4),))
    kv_down = bell_draw(streams_of[4], (D, KVR), D ** -0.5, 0.125, ((1, 4),))
    k_rope_weight = bell_draw(streams_of[5], (D, RD), D ** -0.5, 0.125, ((1, 4),))
    kv_gain = jnp.clip(1.0 + 0.1 * jax.random.normal(streams_of[6], (KVR,), jnp.float32), 0.5, 1.5)
    kv_up = bell_draw(streams_of[7], (KVR, H * (HD + VD)), KVR ** -0.5, 0.25, ((1, 4),))
    o_weight = bell_draw(streams_of[8], (H * VD, D), (H * VD // 16) ** -0.5, 0.5, ((0, 4),))
    ffn_gain = jnp.clip(1.0 + 0.1 * jax.random.normal(streams_of[9], (D,), jnp.float32), 0.5, 1.5)
    router_weight = bell_draw(streams_of[10], (D, EXPERTS), (4 * D) ** -0.5, 0.0625, (), jnp.float32)
    expert_ids_keys = jax.random.split(jax.random.fold_in(streams_of[11], 1), TOKENS // TOK_DEV)
    expert_ids_turns = jax.random.permutation(jax.random.fold_in(streams_of[11], 3), TOKENS // TOK_DEV)
    expert_ids = jax.vmap(lambda own, number: assign_block(jax.random.fold_in(streams_of[11], 2), own, number, TOK_DEV, EXPERTS, TOPK, CAP, 2))(expert_ids_keys, expert_ids_turns).reshape((TOKENS, TOPK))
    expert_gate = bell_draw(streams_of[12], (EXPERTS, D, FF_E), D ** -0.5, 0.125, ((0, 8), (2, 4)))
    expert_up = bell_draw(streams_of[13], (EXPERTS, D, FF_E), D ** -0.5, 0.125, ((0, 8), (2, 4)))
    expert_down = bell_draw(streams_of[14], (EXPERTS, FF_E, D), (max(1, FF_E // 1024)) ** -0.5, 6.0, ((0, 8), (1, 4)))
    shared_gate = bell_draw(streams_of[15], (D, FF_S), D ** -0.5, 0.125, ((1, 4),))
    shared_up = bell_draw(streams_of[16], (D, FF_S), D ** -0.5, 0.125, ((1, 4),))
    shared_down = bell_draw(streams_of[17], (FF_S, D), FF_S ** -0.5, 0.109375, ((0, 4),))
    return dict(tokens=tokens, cotangent=cotangent, attn_gain=attn_gain, q_weight=q_weight, kv_down=kv_down, k_rope_weight=k_rope_weight, kv_gain=kv_gain, kv_up=kv_up, o_weight=o_weight, ffn_gain=ffn_gain, router_weight=router_weight, expert_ids=expert_ids, expert_gate=expert_gate, expert_up=expert_up, expert_down=expert_down, shared_gate=shared_gate, shared_up=shared_up, shared_down=shared_down)


EPSILON = 1e-06

def rope_tables(length, width):
    half_width = width // 2
    frequency = 10000.0 ** (-jnp.arange(half_width, dtype=jnp.float32) * (2.0 / width))
    angles = jnp.arange(length, dtype=jnp.float32)[:, None] * frequency[None, :]
    return (jnp.cos(angles), jnp.sin(angles))

def rotate(vector, cosine, sine_tab):
    half_width = vector.shape[-1] // 2
    lower_half = vector[..., :half_width]
    upper_half = vector[..., half_width:]
    return jnp.concatenate([lower_half * cosine - upper_half * sine_tab, upper_half * cosine + lower_half * sine_tab], axis=-1)

def unrotate(vector, cosine, sine_tab):
    half_width = vector.shape[-1] // 2
    lower_half = vector[..., :half_width]
    upper_half = vector[..., half_width:]
    return jnp.concatenate([lower_half * cosine + upper_half * sine_tab, upper_half * cosine - lower_half * sine_tab], axis=-1)

def rms_norm(values, gains):
    inv_rms = lax.rsqrt(lax.optimization_barrier(jnp.mean(values * values, axis=-1, keepdims=True)) + EPSILON)
    return (values * inv_rms * gains, inv_rms)

def rms_back(cotan, values, inv_rms, gains):
    weighted = cotan * gains
    inner_mean = lax.optimization_barrier(jnp.mean(weighted * values, axis=-1, keepdims=True))
    value_grad = inv_rms * weighted - values * (inv_rms * inv_rms * inv_rms) * inner_mean
    gain_grad = lax.optimization_barrier(jnp.sum(cotan * values * inv_rms, axis=0))
    return (value_grad, gain_grad)

def causal_scores(query_rot, key_full, factor):
    scores = jnp.einsum('nqhd,nkhd->nhqk', query_rot.astype(jnp.float32), key_full.astype(jnp.float32)) * factor
    length = query_rot.shape[1]
    causal = jnp.arange(length)[:, None] >= jnp.arange(length)[None, :]
    return jnp.where(causal, scores, -1e+30)

def reference(tokens, cotangent, attn_gain, q_weight, kv_down, k_rope_weight, kv_gain, kv_up, o_weight, ffn_gain, router_weight, expert_ids, expert_gate, expert_up, expert_down, shared_gate, shared_up, shared_down):
    seq_count = TOKENS // SEQ
    factor = (HD + RD) ** (-0.5)
    block_width = FF_E // N_TENSOR
    cosine, sine_tab = rope_tables(SEQ, RD)
    head_cos = cosine[:, None, :]
    head_sin = sine_tab[:, None, :]
    tokens_f = tokens.astype(jnp.float32)
    normed_f, inv_first = rms_norm(tokens_f, attn_gain)
    normed = normed_f.astype(jnp.bfloat16)
    query_raw = jnp.dot(normed, q_weight, preferred_element_type=jnp.float32).reshape(seq_count, SEQ, H, HD + RD)
    query_rot = jnp.concatenate([query_raw[..., :HD], rotate(query_raw[..., HD:], head_cos, head_sin)], axis=-1).astype(jnp.bfloat16)
    latent = jnp.dot(normed, kv_down, preferred_element_type=jnp.float32).astype(jnp.bfloat16)
    rope_key = jnp.dot(normed, k_rope_weight, preferred_element_type=jnp.float32).astype(jnp.bfloat16)
    latent_f = latent.astype(jnp.float32)
    latent_normed_f, inv_latent = rms_norm(latent_f, kv_gain)
    latent_normed = latent_normed_f.astype(jnp.bfloat16)
    key_value = jnp.dot(latent_normed, kv_up, preferred_element_type=jnp.float32).astype(jnp.bfloat16).reshape(seq_count, SEQ, H, HD + VD)
    rope_rot = rotate(rope_key.astype(jnp.float32).reshape(seq_count, SEQ, RD), cosine, sine_tab).astype(jnp.bfloat16)
    key_full = jnp.concatenate([key_value[..., :HD], jnp.broadcast_to(rope_rot[:, :, None, :], (seq_count, SEQ, H, RD))], axis=-1)
    values = key_value[..., HD:]
    scores = causal_scores(query_rot, key_full, factor)
    top_score = lax.optimization_barrier(jnp.max(scores, axis=-1, keepdims=True))
    log_total = top_score + jnp.log(lax.optimization_barrier(jnp.sum(jnp.exp(scores - top_score), axis=-1, keepdims=True)))
    weights = jnp.exp(scores - log_total).astype(jnp.bfloat16)
    attended = jnp.einsum('nhqk,nkhd->nqhd', weights.astype(jnp.float32), values.astype(jnp.float32)).astype(jnp.bfloat16).reshape(TOKENS, H * VD)
    hidden_one = tokens_f + jnp.dot(attended, o_weight, preferred_element_type=jnp.float32)
    ffn_normed_f, inv_second = rms_norm(hidden_one, ffn_gain)
    ffn_normed = ffn_normed_f.astype(jnp.bfloat16)
    logits = jnp.dot(ffn_normed.astype(jnp.float32), router_weight, precision=lax.Precision.HIGHEST)
    router_prob = jax.nn.softmax(logits, axis=-1)
    chosen = expert_ids[:, :, None] == jnp.arange(EXPERTS, dtype=jnp.int32)[None, None, :]
    gate_vals = lax.optimization_barrier(jnp.sum(jnp.where(chosen, router_prob[:, None, :], 0.0), axis=-1))
    flat_ids = expert_ids.reshape(-1)
    routed_count = TOKENS * TOPK
    flat_hits = chosen.reshape(N_DP, TOK_DEV * TOPK, EXPERTS).astype(jnp.int32)
    earlier = (jnp.cumsum(flat_hits, axis=1) - flat_hits).reshape(routed_count, EXPERTS)
    slot_rank = lax.optimization_barrier(jnp.sum(earlier * flat_hits.reshape(routed_count, EXPERTS), axis=1)).astype(jnp.int32)
    row_index = jnp.arange(routed_count, dtype=jnp.int32)
    source_dev = row_index // (TOK_DEV * TOPK)
    table = jnp.full((EXPERTS, N_DP, CAP), routed_count, jnp.int32).at[flat_ids, source_dev, slot_rank].set(row_index).reshape(EXPERTS, N_DP * CAP)
    out_grad = cotangent.astype(jnp.float32)
    pad_normed = jnp.concatenate([ffn_normed, jnp.zeros((1, D), jnp.bfloat16)], axis=0)
    pad_grad = jnp.concatenate([out_grad, jnp.zeros((1, D), jnp.float32)], axis=0)
    pad_gate = jnp.concatenate([gate_vals.reshape(-1), jnp.zeros((1,), jnp.float32)], axis=0)

    def expert_forward(carry, inputs):
        routed_acc, gate_grad_acc = carry
        slot_rows, w_gate, w_up, w_down = inputs
        tok_index = slot_rows // TOPK
        rows_in = pad_normed[tok_index]
        gate_hidden = jnp.dot(rows_in, w_gate, preferred_element_type=jnp.float32)
        up_hidden = jnp.dot(rows_in, w_up, preferred_element_type=jnp.float32)
        activation = (jax.nn.silu(gate_hidden) * up_hidden).astype(jnp.bfloat16)
        blocks = jnp.einsum('rnh,nhd->nrd', activation.astype(jnp.float32).reshape(-1, N_TENSOR, block_width), w_down.astype(jnp.float32).reshape(N_TENSOR, block_width, D))
        routed_rows = lax.optimization_barrier(jnp.sum(lax.optimization_barrier(blocks.astype(jnp.bfloat16)).astype(jnp.float32), axis=0))
        routed_acc = routed_acc.at[tok_index].add(pad_gate[slot_rows][:, None] * routed_rows)
        gate_grad_acc = gate_grad_acc.at[slot_rows].add(lax.optimization_barrier(jnp.sum(pad_grad[tok_index] * routed_rows, axis=1)))
        return ((routed_acc, gate_grad_acc), None)
    start = (jnp.zeros((TOKENS + 1, D), jnp.float32), jnp.zeros((routed_count + 1,), jnp.float32))
    (routed_acc, gate_grad_acc), _ = lax.scan(expert_forward, start, (table, expert_gate, expert_up, expert_down))
    routed_sum = routed_acc[:TOKENS]
    gate_grad = gate_grad_acc[:routed_count].reshape(TOKENS, TOPK)
    shared_gate_h = jnp.dot(ffn_normed, shared_gate, preferred_element_type=jnp.float32)
    shared_up_h = jnp.dot(ffn_normed, shared_up, preferred_element_type=jnp.float32)
    shared_act = (jax.nn.silu(shared_gate_h) * shared_up_h).astype(jnp.bfloat16)
    shared_out = jnp.dot(shared_act, shared_down, preferred_element_type=jnp.float32)
    output = (hidden_one + routed_sum + shared_out).astype(jnp.bfloat16)

    def expert_backward(carry, inputs):
        slot_rows, w_gate, w_up, w_down = inputs
        tok_index = slot_rows // TOPK
        rows_in = pad_normed[tok_index]
        grad_in = (pad_gate[slot_rows][:, None] * pad_grad[tok_index]).astype(jnp.bfloat16)
        gate_hidden = jnp.dot(rows_in, w_gate, preferred_element_type=jnp.float32)
        up_hidden = jnp.dot(rows_in, w_up, preferred_element_type=jnp.float32)
        sigmoid_h = jax.nn.sigmoid(gate_hidden)
        silu_h = gate_hidden * sigmoid_h
        activation = (silu_h * up_hidden).astype(jnp.bfloat16)
        dact = jnp.dot(grad_in, w_down.T, preferred_element_type=jnp.float32)
        gate_delta = (dact * up_hidden * sigmoid_h * (1.0 + gate_hidden * (1.0 - sigmoid_h))).astype(jnp.bfloat16)
        up_delta = (dact * silu_h).astype(jnp.bfloat16)
        gate_w_grad = jnp.dot(rows_in.T, gate_delta, preferred_element_type=jnp.float32)
        up_w_grad = jnp.dot(rows_in.T, up_delta, preferred_element_type=jnp.float32)
        down_w_grad = jnp.dot(activation.T, grad_in, preferred_element_type=jnp.float32)
        blocks = jnp.einsum('rnh,dnh->nrd', gate_delta.astype(jnp.float32).reshape(-1, N_TENSOR, block_width), w_gate.astype(jnp.float32).reshape(D, N_TENSOR, block_width))
        blocks = blocks + jnp.einsum('rnh,dnh->nrd', up_delta.astype(jnp.float32).reshape(-1, N_TENSOR, block_width), w_up.astype(jnp.float32).reshape(D, N_TENSOR, block_width))
        back_rows = lax.optimization_barrier(jnp.sum(lax.optimization_barrier(blocks.astype(jnp.bfloat16)).astype(jnp.float32), axis=0))
        carry = carry.at[tok_index].add(back_rows)
        return (carry, (gate_w_grad, up_w_grad, down_w_grad))
    routed_dx_acc, expert_grads = lax.scan(expert_backward, jnp.zeros((TOKENS + 1, D), jnp.float32), (table, expert_gate, expert_up, expert_down))
    routed_dx = routed_dx_acc[:TOKENS]
    expert_gate_grad, expert_up_grad, expert_down_grad = expert_grads
    shared_dact = jnp.dot(cotangent, shared_down.T, preferred_element_type=jnp.float32)
    sigmoid_s = jax.nn.sigmoid(shared_gate_h)
    silu_s = shared_gate_h * sigmoid_s
    shared_gate_delta = (shared_dact * shared_up_h * sigmoid_s * (1.0 + shared_gate_h * (1.0 - sigmoid_s))).astype(jnp.bfloat16)
    shared_up_delta = (shared_dact * silu_s).astype(jnp.bfloat16)
    shared_down_grad = jnp.dot(shared_act.T, cotangent, preferred_element_type=jnp.float32)
    shared_gate_grad = jnp.dot(ffn_normed.T, shared_gate_delta, preferred_element_type=jnp.float32)
    shared_up_grad = jnp.dot(ffn_normed.T, shared_up_delta, preferred_element_type=jnp.float32)
    shared_dx = jnp.dot(shared_gate_delta, shared_gate.T, preferred_element_type=jnp.float32) + jnp.dot(shared_up_delta, shared_up.T, preferred_element_type=jnp.float32)
    prob_grad = lax.optimization_barrier(jnp.sum(jnp.where(chosen, gate_grad[:, :, None], 0.0), axis=1))
    logit_grad = (router_prob * (prob_grad - lax.optimization_barrier(jnp.sum(router_prob * prob_grad, axis=-1, keepdims=True)))).astype(jnp.bfloat16)
    router_grad = jnp.dot(ffn_normed.T, logit_grad, preferred_element_type=jnp.float32)
    ffn_normed_grad = shared_dx + routed_dx + jnp.dot(logit_grad.astype(jnp.float32), router_weight.T, precision=lax.Precision.HIGHEST)
    hidden_norm_grad, ffn_gain_grad = rms_back(ffn_normed_grad, hidden_one, inv_second, ffn_gain)
    hidden_grad = out_grad + hidden_norm_grad
    hidden_grad_b = hidden_grad.astype(jnp.bfloat16)
    o_weight_grad = jnp.dot(attended.T, hidden_grad_b, preferred_element_type=jnp.float32)
    attended_grad = jnp.dot(hidden_grad_b, o_weight.T, preferred_element_type=jnp.float32).astype(jnp.bfloat16).reshape(seq_count, SEQ, H, VD)
    attn_probs = jnp.exp(causal_scores(query_rot, key_full, factor) - log_total)
    value_grad = jnp.einsum('nhqk,nqhd->nkhd', attn_probs.astype(jnp.bfloat16).astype(jnp.float32), attended_grad.astype(jnp.float32))
    prob_dot = jnp.einsum('nqhd,nkhd->nhqk', attended_grad.astype(jnp.float32), values.astype(jnp.float32))
    score_grad = (attn_probs * (prob_dot - lax.optimization_barrier(jnp.sum(attn_probs * prob_dot, axis=-1, keepdims=True))) * factor).astype(jnp.bfloat16)
    query_grad = jnp.einsum('nhqk,nkhd->nqhd', score_grad.astype(jnp.float32), key_full.astype(jnp.float32))
    key_grad = jnp.einsum('nhqk,nqhd->nkhd', score_grad.astype(jnp.float32), query_rot.astype(jnp.float32))
    query_grad_b = jnp.concatenate([query_grad[..., :HD], unrotate(query_grad[..., HD:], head_cos, head_sin)], axis=-1).astype(jnp.bfloat16).reshape(TOKENS, H * (HD + RD))
    kv_grad = jnp.concatenate([key_grad[..., :HD], value_grad], axis=-1).astype(jnp.bfloat16).reshape(TOKENS, H * (HD + VD))
    kv_up_grad = jnp.dot(latent_normed.T, kv_grad, preferred_element_type=jnp.float32)
    latent_normed_grad = jnp.dot(kv_grad, kv_up.T, preferred_element_type=jnp.float32)
    rope_sum = unrotate(lax.optimization_barrier(jnp.sum(key_grad[..., HD:], axis=2)), cosine, sine_tab).reshape(TOKENS, RD)
    latent_grad, kv_gain_grad = rms_back(latent_normed_grad, latent_f, inv_latent, kv_gain)
    latent_grad_b = latent_grad.astype(jnp.bfloat16)
    rope_grad_b = rope_sum.astype(jnp.bfloat16)
    q_weight_grad = jnp.dot(normed.T, query_grad_b, preferred_element_type=jnp.float32)
    kv_down_grad = jnp.dot(normed.T, latent_grad_b, preferred_element_type=jnp.float32)
    k_rope_grad = jnp.dot(normed.T, rope_grad_b, preferred_element_type=jnp.float32)
    normed_grad = jnp.dot(query_grad_b, q_weight.T, preferred_element_type=jnp.float32) + jnp.dot(latent_grad_b, kv_down.T, preferred_element_type=jnp.float32) + jnp.dot(rope_grad_b, k_rope_weight.T, preferred_element_type=jnp.float32)
    input_norm_grad, attn_gain_grad = rms_back(normed_grad, tokens_f, inv_first, attn_gain)
    input_grad = hidden_grad + input_norm_grad
    return (output, input_grad, attn_gain_grad, q_weight_grad, kv_down_grad, k_rope_grad, kv_gain_grad, kv_up_grad, o_weight_grad, ffn_gain_grad, router_grad, shared_gate_grad, shared_up_grad, shared_down_grad, expert_gate_grad, expert_up_grad, expert_down_grad)
```

```python
import functools

import jax
import jax.numpy as jnp
from jax import lax
from jax.experimental import pallas as pl
from jax.experimental.pallas import tpu as pltpu
from jax.sharding import PartitionSpec as P

HD = 128
RD = 64
VD = 128
TOPK = 6
SEQ = 256
CAP = 64
LANES = 128
EPSILON = 1e-06
MIB = 1 << 20

bf16 = jnp.bfloat16
f32 = jnp.float32


def dot(a, b):
    return lax.dot_general(a, b, (((1,), (0,)), ((), ())), preferred_element_type=f32)


def dot_nt(a, b):
    return lax.dot_general(a, b, (((1,), (1,)), ((), ())), preferred_element_type=f32)


def dot_tn(a, b):
    return lax.dot_general(a, b, (((0,), (0,)), ((), ())), preferred_element_type=f32)


def rope_tables(length, width):
    half_width = width // 2
    frequency = 10000.0 ** (-jnp.arange(half_width, dtype=f32) * (2.0 / width))
    angles = jnp.arange(length, dtype=f32)[:, None] * frequency[None, :]
    return (jnp.cos(angles), jnp.sin(angles))


def rotate(vector, cosine, sine_tab):
    half_width = vector.shape[-1] // 2
    lower_half = vector[..., :half_width]
    upper_half = vector[..., half_width:]
    return jnp.concatenate(
        [lower_half * cosine - upper_half * sine_tab, upper_half * cosine + lower_half * sine_tab],
        axis=-1,
    )


def unrotate(vector, cosine, sine_tab):
    return rotate(vector, cosine, -sine_tab)


def rms_norm(values, gains):
    inv_rms = lax.rsqrt(jnp.mean(values * values, axis=-1, keepdims=True) + EPSILON)
    return (values * inv_rms * gains, inv_rms)


def rms_back(cotan, values, inv_rms, gains):
    weighted = cotan * gains
    inner_mean = jnp.mean(weighted * values, axis=-1, keepdims=True)
    value_grad = inv_rms * weighted - values * (inv_rms * inv_rms * inv_rms) * inner_mean
    gain_grad = jnp.sum(cotan * values * inv_rms, axis=0)
    return (value_grad, gain_grad)


def causal_scores(query_rot, key_full, factor):
    scores = (
        jnp.einsum("nqhd,nkhd->nhqk", query_rot, key_full, preferred_element_type=f32) * factor
    )
    length = query_rot.shape[1]
    causal = jnp.arange(length)[:, None] >= jnp.arange(length)[None, :]
    return jnp.where(causal, scores, -1e30)


def swap(array, axis, bits):
    count = lax.axis_size(axis)
    return lax.ppermute(array, axis, [(i, i ^ bits) for i in range(count)])


def block_at(array, index, size, dim):
    return lax.dynamic_slice_in_dim(array, index * size, size, dim)


def by_partner(array, axis, dim):
    count = lax.axis_size(axis)
    own = lax.axis_index(axis)
    size = array.shape[dim] // count
    return [block_at(array, own ^ r, size, dim) for r in range(count)]


def reorder(array, axis, dim):
    return jnp.concatenate(by_partner(array, axis, dim), axis=dim)


def share(array, axis):
    return [array] + [swap(array, axis, r) for r in range(1, lax.axis_size(axis))]


def share_dp(array):
    count = lax.axis_size("dp")
    same_core = [array] + [swap(array, "dp", r) for r in range(2, count, 2)]
    other_core = [swap(block, "dp", 1) for block in same_core]
    return [block for pair in zip(same_core, other_core) for block in pair]


def trade(blocks, axis):
    return [blocks[0]] + [swap(blocks[r], axis, r) for r in range(1, len(blocks))]


def total(blocks):
    return functools.reduce(jnp.add, [block.astype(f32) for block in blocks])


def pick_matrix(slots):
    toks = slots.shape[1]
    place = lax.broadcasted_iota(jnp.int32, (CAP, toks), 0)
    return jnp.concatenate(
        [
            jnp.where(place == slots[e : e + 1, :], 1.0, 0.0).astype(bf16)
            for e in range(slots.shape[0])
        ],
        axis=0,
    )


def fetch(refs, buffer, sems):
    step = pl.program_id(0)

    @pl.when(step == 0)
    def _():
        for i, ref in enumerate(refs):
            pltpu.make_async_copy(ref, buffer.at[i], sems.at[i]).start()

    pltpu.make_async_copy(refs[0], buffer.at[step], sems.at[step]).wait()
    return buffer.at[step]


def pick_grad_kernel(count, slots_ref, down_ref, *refs):
    rows_ref, dact_ref, buffer, sems = refs[count:]
    block = fetch(refs[:count], buffer, sems)
    slots = slots_ref[0]
    picked = dot(pick_matrix(slots), block[...]).astype(bf16)
    for e in range(slots.shape[0]):
        rows_ref[e] = picked[e * CAP : (e + 1) * CAP]
    dact_ref[...] = dot_nt(block[...], down_ref[...])


def pick_kernel(count, experts_all, slots_ref, router_ref, weights_ref, dact_ref, *refs):
    rows_ref, gate_ref, act_ref, delta_ref, buffer, sems = refs[count:]
    block = fetch(refs[:count], buffer, sems)
    slots = slots_ref[0]
    experts = slots.shape[0]
    picks = pick_matrix(slots)
    picked = dot(picks, block[...]).astype(bf16)
    for e in range(experts):
        rows_ref[e] = picked[e * CAP : (e + 1) * CAP]
    parts = dot_nt(router_ref[...], block[...])
    logits = parts[:experts_all] + parts[experts_all : 2 * experts_all] + parts[2 * experts_all :]
    spread = jnp.exp(logits - jnp.max(logits, axis=0, keepdims=True))
    prob = spread / jnp.sum(spread, axis=0, keepdims=True)
    for e in range(experts):
        chosen = picks[e * CAP : (e + 1) * CAP].astype(f32) * prob[e : e + 1, :]
        gate_ref[e] = jnp.broadcast_to(jnp.sum(chosen, axis=1, keepdims=True), (CAP, LANES))
    hidden = dot(block[...], weights_ref[...])
    width = hidden.shape[1] // 2
    act, gate_delta, up_delta = gated(hidden[:, :width], hidden[:, width:], dact_ref[...])
    act_ref[...] = act.astype(bf16)
    delta_ref[:, :width] = gate_delta.astype(bf16)
    delta_ref[:, width:] = up_delta.astype(bf16)


def gated(gate_h, up_h, dact):
    sigmoid_h = jax.nn.sigmoid(gate_h)
    silu_h = gate_h * sigmoid_h
    gate_delta = dact * up_h * sigmoid_h * (1.0 + gate_h * (1.0 - sigmoid_h))
    return silu_h * up_h, gate_delta, dact * silu_h


def hidden_kernel(
    first_ref,
    rows_ref,
    grads_ref,
    gate_ref,
    expert_gate_ref,
    expert_up_ref,
    expert_down_ref,
    act_ref,
    gate_delta_ref,
    up_delta_ref,
    score_ref,
):
    rows = rows_ref[0]
    gate_h = dot(rows, expert_gate_ref[0])
    up_h = dot(rows, expert_up_ref[0])
    dact = dot_nt(grads_ref[0], expert_down_ref[0])
    gate = gate_ref[0][:, :1]
    act, gate_delta, up_delta = gated(gate_h, up_h, dact)
    act_ref[0] = (act * gate).astype(bf16)
    gate_delta_ref[0] = (gate_delta * gate).astype(bf16)
    up_delta_ref[0] = (up_delta * gate).astype(bf16)
    score = jnp.sum(act * dact, axis=1, keepdims=True)
    high = score.astype(bf16).astype(f32)
    lanes = score_ref.shape[2]
    lane = lax.broadcasted_iota(jnp.int32, (rows.shape[0], lanes), 1)
    mine = first_ref[0] + pl.program_id(0)
    score_ref[0] = jnp.where(
        lane == mine, high, jnp.where(lane == mine + lanes // 2, score - high, 0.0)
    ).astype(bf16)


def return_kernel(spec, slots_ref, *refs):
    transposed, pairs, added, split = spec
    deltas, weights = refs[:pairs], refs[pairs : 2 * pairs]
    shared_ref, shared_weight_ref = refs[2 * pairs : 2 * pairs + 2]
    rest = refs[2 * pairs + 2 :]
    other_ref = rest[0] if added else None
    rest = rest[1:] if added else rest
    outs, picks, rows = rest[:-2], rest[-2], rest[-1]
    sources, slot_rows, _ = rows.shape
    experts = slot_rows // CAP
    toks = picks.shape[2]
    product = dot_nt if transposed else dot

    @pl.when(pl.program_id(0) == 0)
    def _():
        for s in range(sources):
            picks[s] = pick_matrix(slots_ref[s])

    for e in range(experts):
        back = functools.reduce(
            jnp.add, [product(d[e], w[e]) for d, w in zip(deltas, weights)]
        ).astype(bf16)
        for s in range(sources):
            rows[s, e * CAP : (e + 1) * CAP, :] = back[s * CAP : (s + 1) * CAP]
    for s in range(sources):
        summed = dot_tn(picks[s], rows[s]) + product(
            shared_ref[s * toks : (s + 1) * toks], shared_weight_ref[...]
        )
        if added:
            summed = summed + other_ref[s].astype(f32)
        if split:
            outs[s][...] = summed.astype(bf16)
        else:
            outs[0][s] = summed.astype(bf16)


def score_kernel(slots_ref, score_ref, out_ref):
    for s in range(slots_ref.shape[0]):
        rows = jnp.concatenate(
            [score_ref[e, s * CAP : (s + 1) * CAP] for e in range(score_ref.shape[0])], axis=0
        )
        out_ref[s] = dot_tn(pick_matrix(slots_ref[s]), rows).astype(bf16)


def expert_grad_kernel(
    rows_ref,
    grads_ref,
    act_ref,
    gate_delta_ref,
    up_delta_ref,
    gate_grad_ref,
    up_grad_ref,
    down_grad_ref,
):
    rows = rows_ref[0]
    gate_grad_ref[0] = dot_tn(rows, gate_delta_ref[0])
    up_grad_ref[0] = dot_tn(rows, up_delta_ref[0])
    down_grad_ref[0] = dot_tn(act_ref[0], grads_ref[0])


def shared_grad_kernel(count, delta_ref, act_ref, *refs):
    rows, grads = refs[:count], refs[count : 2 * count]
    in_ref, down_ref, row_buf, grad_buf, in_acc, down_acc, row_sems, grad_sems = refs[2 * count :]
    step = pl.program_id(0)
    row = fetch(rows, row_buf, row_sems)
    grad = fetch(grads, grad_buf, grad_sems)

    @pl.when(step == 0)
    def _():
        in_acc[...] = jnp.zeros_like(in_acc)
        down_acc[...] = jnp.zeros_like(down_acc)

    in_acc[...] += dot_tn(row[...], delta_ref[...])
    down_acc[...] += dot_tn(act_ref[...], grad[...])

    @pl.when(step == count - 1)
    def _():
        in_ref[...] = in_acc[...].astype(bf16)
        down_ref[...] = down_acc[...].astype(bf16)


ANYWHERE = pl.BlockSpec(memory_space=pl.ANY)


def whole(array):
    rank = len(array.shape)
    return pl.BlockSpec(array.shape, lambda *_: (0,) * rank)


def params(mib):
    return pltpu.CompilerParams(vmem_limit_bytes=mib * MIB)


def cost(flops, bytes_accessed, transcendentals=0):
    return pl.CostEstimate(
        flops=int(flops), bytes_accessed=int(bytes_accessed), transcendentals=int(transcendentals)
    )


def pick_grads(blocks, slots, shared_down):
    count = len(blocks)
    toks, width = blocks[0].shape
    experts = slots.shape[1]
    shared = shared_down.shape[0]
    return pl.pallas_call(
        functools.partial(pick_grad_kernel, count),
        grid=(count,),
        in_specs=[pl.BlockSpec((1, experts, toks), lambda s: (s, 0, 0)), whole(shared_down)]
        + [ANYWHERE] * count,
        out_specs=[
            pl.BlockSpec((experts, CAP, width), lambda s: (0, s, 0)),
            pl.BlockSpec((toks, shared), lambda s: (s, 0)),
        ],
        out_shape=[
            jax.ShapeDtypeStruct((experts, count * CAP, width), bf16),
            jax.ShapeDtypeStruct((count * toks, shared), f32),
        ],
        scratch_shapes=[
            pltpu.VMEM((count, toks, width), bf16),
            pltpu.SemaphoreType.DMA((count,)),
        ],
        compiler_params=params(48),
        cost_estimate=cost(
            2 * count * toks * width * (experts * CAP + shared), 4 * count * toks * width
        ),
    )(slots, shared_down, *blocks)


def pick_rows(blocks, slots, router, weights, dact, experts_all):
    count = len(blocks)
    toks, width = blocks[0].shape
    experts = slots.shape[1]
    shared = dact.shape[1]
    return pl.pallas_call(
        functools.partial(pick_kernel, count, experts_all),
        grid=(count,),
        in_specs=[
            pl.BlockSpec((1, experts, toks), lambda s: (s, 0, 0)),
            whole(router),
            whole(weights),
            pl.BlockSpec((toks, shared), lambda s: (s, 0)),
        ]
        + [ANYWHERE] * count,
        out_specs=[
            pl.BlockSpec((experts, CAP, width), lambda s: (0, s, 0)),
            pl.BlockSpec((experts, CAP, LANES), lambda s: (0, s, 0)),
            pl.BlockSpec((toks, shared), lambda s: (s, 0)),
            pl.BlockSpec((toks, 2 * shared), lambda s: (s, 0)),
        ],
        out_shape=[
            jax.ShapeDtypeStruct((experts, count * CAP, width), bf16),
            jax.ShapeDtypeStruct((experts, count * CAP, LANES), f32),
            jax.ShapeDtypeStruct((count * toks, shared), bf16),
            jax.ShapeDtypeStruct((count * toks, 2 * shared), bf16),
        ],
        scratch_shapes=[
            pltpu.VMEM((count, toks, width), bf16),
            pltpu.SemaphoreType.DMA((count,)),
        ],
        compiler_params=params(48),
        cost_estimate=cost(
            2 * count * toks * width * (experts * CAP + router.shape[0] + 2 * shared),
            4 * count * toks * width,
        ),
    )(slots, router, weights, dact, *blocks)


def expert_hidden(first, rows, grads, gate, expert_gate, expert_up, expert_down, lanes):
    experts, slot_rows, width = rows.shape
    hidden = expert_gate.shape[2]

    def per_expert(array):
        return pl.BlockSpec((1,) + array.shape[1:], lambda e: (e, 0, 0))

    narrow = jax.ShapeDtypeStruct((experts, slot_rows, hidden), bf16)
    score = jax.ShapeDtypeStruct((experts, slot_rows, lanes), bf16)
    return pl.pallas_call(
        hidden_kernel,
        grid=(experts,),
        in_specs=[pl.BlockSpec(memory_space=pltpu.SMEM)]
        + [per_expert(a) for a in (rows, grads, gate, expert_gate, expert_up, expert_down)],
        out_specs=[per_expert(narrow)] * 3 + [per_expert(score)],
        out_shape=[narrow] * 3 + [score],
        compiler_params=params(56),
        cost_estimate=cost(
            6 * experts * slot_rows * width * hidden,
            experts * (4 * slot_rows * width + 6 * hidden * width),
            experts * slot_rows * hidden,
        ),
    )(first, rows, grads, gate, expert_gate, expert_up, expert_down)


def return_rows(half, slots, deltas, weights, shared, shared_weight, transposed, start, size, other):
    experts, slot_rows, hidden = deltas[0].shape
    sources = slots.shape[0] // 2
    toks = slots.shape[2]
    chunk = min(512, size)
    steps = size // chunk
    first = start // chunk
    split = half == 1
    if transposed:
        weight_spec = pl.BlockSpec((experts, chunk, hidden), lambda n: (0, n + first, 0))
        shared_spec = pl.BlockSpec((chunk, shared.shape[1]), lambda n: (n + first, 0))
    else:
        weight_spec = pl.BlockSpec((experts, hidden, chunk), lambda n: (0, 0, n + first))
        shared_spec = pl.BlockSpec((shared.shape[1], chunk), lambda n: (0, n + first))
    many = pl.BlockSpec((sources, toks, chunk), lambda n: (0, 0, n))
    in_specs = (
        [pl.BlockSpec((sources,) + slots.shape[1:], lambda n: (half, 0, 0))]
        + [pl.BlockSpec((experts, slot_rows // 2, hidden), lambda n: (0, half, 0))] * len(deltas)
        + [weight_spec] * len(weights)
        + [pl.BlockSpec((sources * toks, shared.shape[1]), lambda n: (half, 0)), shared_spec]
    )
    operands = [slots, *deltas, *weights, shared, shared_weight]
    if other is not None:
        in_specs.append(many)
        operands.append(other)
    if split:
        out_specs = [pl.BlockSpec((toks, chunk), lambda n: (0, n))] * sources
        out_shape = [jax.ShapeDtypeStruct((toks, size), bf16)] * sources
    else:
        out_specs, out_shape = [many], [jax.ShapeDtypeStruct((sources, toks, size), bf16)]
    return pl.pallas_call(
        functools.partial(
            return_kernel, (transposed, len(deltas), other is not None, split)
        ),
        grid=(steps,),
        in_specs=in_specs,
        out_specs=out_specs,
        out_shape=out_shape,
        scratch_shapes=[
            pltpu.VMEM((sources, experts * CAP, toks), bf16),
            pltpu.VMEM((sources, experts * CAP, chunk), bf16),
        ],
        compiler_params=params(48),
        cost_estimate=cost(
            2 * experts * slot_rows // 2 * size * (hidden * len(deltas) + toks)
            + 2 * sources * toks * size * shared.shape[1],
            2 * size * (experts * hidden * len(deltas) + sources * toks),
        ),
    )(*operands)


def return_scores(slots, score):
    sources, _, toks = slots.shape
    out = jax.ShapeDtypeStruct((sources, toks, score.shape[2]), bf16)
    return pl.pallas_call(
        score_kernel,
        grid=(1,),
        in_specs=[whole(slots), whole(score)],
        out_specs=whole(out),
        out_shape=out,
        compiler_params=params(32),
    )(slots, score)


def expert_grads(rows, grads, act, gate_delta, up_delta):
    experts, slot_rows, width = rows.shape
    hidden = act.shape[2]

    def per_expert(array):
        return pl.BlockSpec((1,) + array.shape[1:], lambda e: (e, 0, 0))

    outs = [
        jax.ShapeDtypeStruct((experts, width, hidden), f32),
        jax.ShapeDtypeStruct((experts, width, hidden), f32),
        jax.ShapeDtypeStruct((experts, hidden, width), f32),
    ]
    return pl.pallas_call(
        expert_grad_kernel,
        grid=(experts,),
        in_specs=[per_expert(a) for a in (rows, grads, act, gate_delta, up_delta)],
        out_specs=[per_expert(o) for o in outs],
        out_shape=outs,
        compiler_params=params(56),
        cost_estimate=cost(
            6 * experts * slot_rows * width * hidden,
            experts * (4 * slot_rows * width + 12 * hidden * width),
        ),
    )(rows, grads, act, gate_delta, up_delta)


def shared_grads(blocks, grads, delta, act):
    count = len(blocks)
    toks, width = blocks[0].shape
    outs = [
        jax.ShapeDtypeStruct((width, delta.shape[1]), bf16),
        jax.ShapeDtypeStruct((act.shape[1], width), bf16),
    ]
    return pl.pallas_call(
        functools.partial(shared_grad_kernel, count),
        grid=(count,),
        in_specs=[
            pl.BlockSpec((toks, delta.shape[1]), lambda s: (s, 0)),
            pl.BlockSpec((toks, act.shape[1]), lambda s: (s, 0)),
        ]
        + [ANYWHERE] * (2 * count),
        out_specs=[whole(o) for o in outs],
        out_shape=outs,
        scratch_shapes=[
            pltpu.VMEM((count, toks, width), bf16),
            pltpu.VMEM((count, toks, width), bf16),
            pltpu.VMEM(outs[0].shape, f32),
            pltpu.VMEM(outs[1].shape, f32),
            pltpu.SemaphoreType.DMA((count,)),
            pltpu.SemaphoreType.DMA((count,)),
        ],
        compiler_params=params(56),
        cost_estimate=cost(
            2 * count * toks * width * (delta.shape[1] + act.shape[1]), 4 * count * toks * width
        ),
    )(delta, act, *blocks, *grads)


def on_device(
    tokens,
    cotangent,
    attn_gain,
    q_weight,
    kv_down,
    k_rope_weight,
    kv_gain,
    kv_up,
    o_weight,
    ffn_gain,
    router_weight,
    expert_ids,
    expert_gate,
    expert_up,
    expert_down,
    shared_gate,
    shared_up,
    shared_down,
):
    n_t = lax.axis_size("tensor")
    n_d = lax.axis_size("dp")
    t_index = lax.axis_index("tensor")
    d_index = lax.axis_index("dp")
    toks, width = tokens.shape
    own_toks = toks // n_t
    heads = q_weight.shape[1] // (HD + RD)
    experts_all = router_weight.shape[1]
    experts = expert_gate.shape[0]
    factor = (HD + RD) ** (-0.5)
    cosine, sine_tab = rope_tables(SEQ, RD)
    head_cos = cosine[:, None, :]
    head_sin = sine_tab[:, None, :]
    order = [r for r in range(n_d) if r % 2 == 1] + [r for r in range(n_d) if r % 2 == 0]
    lat_cols = kv_down.shape[1]
    rope_cols = k_rope_weight.shape[1]

    tokens_p = by_partner(tokens, "tensor", 0)
    tokens_own = tokens_p[0].astype(f32)
    cot_p = by_partner(cotangent, "tensor", 0)
    cot_own = cot_p[0].astype(f32)
    cot_blocks = share_dp(jnp.concatenate(cot_p, axis=0))
    ids = reorder(expert_ids, "tensor", 0)
    every = jnp.arange(experts_all, dtype=jnp.int32)
    member = jnp.any(ids.T[:, None, :] == every[None, :, None], axis=0)
    before = (jnp.arange(toks)[:, None] < jnp.arange(toks)[None, :]).astype(bf16)
    rank = dot(member.astype(bf16), before)
    slots_own = jnp.where(member, rank, -1.0).astype(bf16)
    slot_blocks = [block_at(s, d_index, experts, 0) for s in share_dp(slots_own)]
    slots = jnp.stack([slot_blocks[r] for r in order]).astype(jnp.int32)
    router_t = jnp.roll(router_weight.T, -d_index * experts, axis=0)
    router_parts = []
    rest = router_t
    for _ in range(3):
        part = lax.reduce_precision(rest, 8, 7)
        router_parts.append(part.astype(bf16))
        rest = rest - part
    router_parts = jnp.concatenate(router_parts, axis=0)
    shared_cols = shared_gate.shape[1] // n_d
    shared_pad = -(-shared_cols // LANES) * LANES - shared_cols
    shared_in = jnp.concatenate(
        [
            jnp.pad(block_at(w, d_index, shared_cols, 1), ((0, 0), (0, shared_pad)))
            for w in (shared_gate, shared_up)
        ],
        axis=1,
    )
    shared_out = jnp.pad(
        block_at(shared_down, d_index, shared_cols, 0), ((0, shared_pad), (0, 0))
    )
    grad_rows, shared_dact = pick_grads([cot_blocks[r] for r in order], slots, shared_out)

    tokens_f = tokens.astype(f32)
    normed_f, inv_first = rms_norm(tokens_f, attn_gain)
    normed = normed_f.astype(bf16)
    query_raw = dot(normed, q_weight).reshape(1, toks, heads, HD + RD)
    query_rot = jnp.concatenate(
        [query_raw[..., :HD], rotate(query_raw[..., HD:], head_cos, head_sin)], axis=-1
    ).astype(bf16)
    down_weight = jnp.concatenate([kv_down, k_rope_weight], axis=1)
    lat_blocks = reorder(
        jnp.stack(share(dot(normed, down_weight).astype(bf16), "tensor")), "tensor", 0
    )
    latent = jnp.concatenate([lat_blocks[j, :, :lat_cols] for j in range(n_t)], axis=1)
    rope_key = jnp.concatenate([lat_blocks[j, :, lat_cols:] for j in range(n_t)], axis=1)
    latent_f = latent.astype(f32)
    latent_normed_f, inv_latent = rms_norm(latent_f, kv_gain)
    latent_normed = latent_normed_f.astype(bf16)
    key_value = dot(latent_normed, kv_up).astype(bf16).reshape(1, toks, heads, HD + VD)
    rope_rot = rotate(rope_key.astype(f32), cosine, sine_tab).astype(bf16)
    key_full = jnp.concatenate(
        [
            key_value[..., :HD],
            jnp.broadcast_to(rope_rot[None, :, None, :], (1, toks, heads, RD)),
        ],
        axis=-1,
    )
    values = key_value[..., HD:]
    scores = causal_scores(query_rot, key_full, factor)
    top_score = jnp.max(scores, axis=-1, keepdims=True)
    log_total = top_score + jnp.log(jnp.sum(jnp.exp(scores - top_score), axis=-1, keepdims=True))
    weights = jnp.exp(scores - log_total).astype(bf16)
    attended = (
        jnp.einsum("nhqk,nkhd->nqhd", weights, values, preferred_element_type=f32)
        .astype(bf16)
        .reshape(toks, heads * VD)
    )
    attended_p = reorder(attended, "tensor", 0)
    attn_part = dot(attended_p, o_weight).reshape(n_t, own_toks, width)
    attn_sum = attn_part[0] + total(
        trade([attn_part[r].astype(bf16) for r in range(n_t)], "tensor")[1:]
    )
    hidden_one = tokens_own + attn_sum
    ffn_normed_f, inv_second = rms_norm(hidden_one, ffn_gain)
    ffn_own = ffn_normed_f.astype(bf16)
    blocks = share_dp(jnp.concatenate(share(ffn_own, "tensor"), axis=0))
    blocks_o = [blocks[r] for r in order]

    rows, gate, shared_act, shared_delta = pick_rows(
        blocks_o, slots, router_parts, shared_in, shared_dact, experts_all
    )
    lanes = -(-2 * experts_all // LANES) * LANES
    first = (d_index * experts).astype(jnp.int32).reshape(1)
    act, gate_delta, up_delta, score = expert_hidden(
        first, rows, grad_rows, gate, expert_gate, expert_up, expert_down, lanes
    )

    def sum_over(deltas, weights_, shared, shared_weight, transposed, start, size):
        other = return_rows(
            0, slots, deltas, weights_, shared, shared_weight, transposed, start, size, None
        )[0]
        other = swap(other, "dp", 1)
        mine = return_rows(
            1, slots, deltas, weights_, shared, shared_weight, transposed, start, size, other
        )
        return sum_blocks(mine)

    def sum_blocks(mine):
        arrived = [mine[0]] + [swap(mine[i], "dp", 2 * i) for i in range(1, len(mine))]
        parts = [
            total([a[k * own_toks : (k + 1) * own_toks] for a in arrived]).astype(bf16)
            for k in range(n_t)
        ]
        return total(trade(parts, "tensor"))

    score_sums = return_scores(slots, score)
    half = n_d // 2
    score_other = swap(score_sums[:half], "dp", 1)
    score_sum = sum_blocks(
        [(score_sums[half + i].astype(f32) + score_other[i].astype(f32)).astype(bf16) for i in range(half)]
    )
    pieces = 2
    size = width // pieces
    back_sum = jnp.concatenate(
        [
            sum_over(
                [gate_delta, up_delta],
                [expert_gate, expert_up],
                shared_delta,
                shared_in,
                True,
                i * size,
                size,
            )
            for i in range(pieces)
        ],
        axis=1,
    )
    out_sum = sum_over([act], [expert_down], shared_act, shared_out, False, 0, width)
    expert_gate_grad, expert_up_grad, expert_down_grad = expert_grads(
        rows, grad_rows, act, gate_delta, up_delta
    )
    shared_in_grad, shared_out_grad = shared_grads(
        blocks_o, [cot_blocks[r] for r in order], shared_delta, shared_act
    )
    output_own = (hidden_one + out_sum).astype(bf16)
    output = reorder(jnp.concatenate(share(output_own, "tensor"), axis=0), "tensor", 0)

    pad_cols = shared_cols + shared_pad
    in_blocks = lax.all_to_all(
        jnp.concatenate(
            [shared_in_grad[:, :shared_cols], shared_in_grad[:, pad_cols : pad_cols + shared_cols]],
            axis=1,
        ).reshape(n_d, width // n_d, 2 * shared_cols),
        "dp",
        0,
        0,
        tiled=True,
    )
    in_blocks = in_blocks.transpose(1, 0, 2).astype(f32)
    rows_d = width // n_d
    shared_gate_grad = in_blocks[:, :, :shared_cols].reshape(rows_d, n_d * shared_cols)
    shared_up_grad = in_blocks[:, :, shared_cols:].reshape(rows_d, n_d * shared_cols)
    shared_down_grad = (
        lax.all_to_all(
            shared_out_grad[:shared_cols].reshape(shared_cols, n_d, rows_d).transpose(1, 0, 2),
            "dp",
            0,
            0,
            tiled=True,
        )
        .reshape(n_d * shared_cols, rows_d)
        .astype(f32)
    )

    logits = jnp.dot(ffn_own.astype(f32), router_weight, precision=lax.Precision.HIGHEST)
    router_prob = jax.nn.softmax(logits, axis=-1)
    prob_grad = score_sum[:, :experts_all] + score_sum[:, lanes // 2 : lanes // 2 + experts_all]
    logit_grad = (
        router_prob * (prob_grad - jnp.sum(router_prob * prob_grad, axis=-1, keepdims=True))
    ).astype(bf16)
    ffn_normed_grad = back_sum + jnp.dot(
        logit_grad.astype(f32), router_weight.T, precision=lax.Precision.HIGHEST
    )
    hidden_norm_grad, ffn_gain_part = rms_back(ffn_normed_grad, hidden_one, inv_second, ffn_gain)
    hidden_grad = cot_own + hidden_norm_grad
    hidden_grad_p = jnp.concatenate(share(hidden_grad.astype(bf16), "tensor"), axis=0)
    logit_blocks = share_dp(jnp.concatenate(share(logit_grad, "tensor"), axis=0))
    device = d_index * n_t + t_index
    own_rows = width // (n_d * n_t)
    router_grad = dot_tn(
        jnp.concatenate([block_at(b, device, own_rows, 1) for b in blocks], axis=0),
        jnp.concatenate(logit_blocks, axis=0),
    )

    attended_grad = (
        reorder(dot_nt(hidden_grad_p, o_weight).astype(bf16), "tensor", 0).reshape(1, toks, heads, VD)
    )
    o_weight_grad = dot_tn(
        jnp.concatenate(share_dp(attended_p), axis=0),
        jnp.concatenate(trade(by_partner(hidden_grad_p, "dp", 1), "dp"), axis=0),
    )
    attn_probs = jnp.exp(causal_scores(query_rot, key_full, factor) - log_total)
    value_grad = jnp.einsum(
        "nhqk,nqhd->nkhd", attn_probs.astype(bf16), attended_grad, preferred_element_type=f32
    )
    prob_dot = jnp.einsum("nqhd,nkhd->nhqk", attended_grad, values, preferred_element_type=f32)
    score_grad = (
        attn_probs * (prob_dot - jnp.sum(attn_probs * prob_dot, axis=-1, keepdims=True)) * factor
    ).astype(bf16)
    query_grad = jnp.einsum("nhqk,nkhd->nqhd", score_grad, key_full, preferred_element_type=f32)
    key_grad = jnp.einsum("nhqk,nqhd->nkhd", score_grad, query_rot, preferred_element_type=f32)
    query_grad_b = (
        jnp.concatenate(
            [query_grad[..., :HD], unrotate(query_grad[..., HD:], head_cos, head_sin)], axis=-1
        )
        .astype(bf16)
        .reshape(toks, heads * (HD + RD))
    )
    kv_grad = (
        jnp.concatenate([key_grad[..., :HD], value_grad], axis=-1)
        .astype(bf16)
        .reshape(toks, heads * (HD + VD))
    )
    rope_part = unrotate(jnp.sum(key_grad[0, ..., HD:], axis=1), cosine, sine_tab)
    latent_part, kv_gain_part = rms_back(dot_nt(kv_grad, kv_up), latent_f, inv_latent, kv_gain)
    latent_trade = [
        jnp.concatenate(pair, axis=1)
        for pair in zip(by_partner(latent_part, "tensor", 1), by_partner(rope_part, "tensor", 1))
    ]
    latent_mine = latent_trade[0] + total(
        trade([b.astype(bf16) for b in latent_trade], "tensor")[1:]
    )
    narrow_p = reorder(
        jnp.concatenate([query_grad_b, latent_mine.astype(bf16)], axis=1), "tensor", 0
    )
    weight_in = jnp.concatenate([q_weight, down_weight], axis=1)
    normed_part = dot_nt(narrow_p, weight_in)
    tokens_pf = jnp.concatenate(tokens_p, axis=0).astype(f32)
    inv_first_p = reorder(inv_first, "tensor", 0)
    attn_gain_part = jnp.sum(normed_part * tokens_pf * inv_first_p, axis=0)
    normed_blocks = normed_part.reshape(n_t, own_toks, width)
    normed_grad = normed_blocks[0] + total(
        trade([normed_blocks[r].astype(bf16) for r in range(n_t)], "tensor")[1:]
    )
    input_norm_grad, _ = rms_back(normed_grad, tokens_own, inv_first_p[:own_toks], attn_gain)
    input_grad = hidden_grad + input_norm_grad

    normed_cols = trade(by_partner(reorder(normed, "tensor", 0), "dp", 1), "dp")
    in_grad = dot_tn(
        jnp.concatenate(normed_cols, axis=0), jnp.concatenate(share_dp(narrow_p), axis=0)
    )
    q_cols = q_weight.shape[1]
    q_weight_grad = in_grad[:, :q_cols]
    kv_down_grad = in_grad[:, q_cols : q_cols + lat_cols]
    k_rope_grad = in_grad[:, q_cols + lat_cols :]
    kv_up_grad = total(
        trade([b.astype(bf16) for b in by_partner(dot_tn(latent_normed, kv_grad), "dp", 0)], "dp")
    )

    gains = jnp.concatenate(
        [
            part.reshape(n_d, n_t, -1)
            for part in (attn_gain_part, ffn_gain_part, kv_gain_part)
        ],
        axis=2,
    )
    gains = total([b[:, 0] for b in trade(by_partner(gains, "tensor", 1), "tensor")])
    gains = total([b[0] for b in trade(by_partner(gains, "dp", 0), "dp")])
    attn_gain_grad = gains[:own_rows]
    ffn_gain_grad = gains[own_rows : 2 * own_rows]
    kv_gain_grad = gains[2 * own_rows :]

    return (
        output,
        input_grad,
        attn_gain_grad,
        q_weight_grad,
        kv_down_grad,
        k_rope_grad,
        kv_gain_grad,
        kv_up_grad,
        o_weight_grad,
        ffn_gain_grad,
        router_grad,
        shared_gate_grad,
        shared_up_grad,
        shared_down_grad,
        expert_gate_grad,
        expert_up_grad,
        expert_down_grad,
    )


def solution(mesh):
    in_specs = (
        P("dp", None),
        P("dp", None),
        P(),
        P(None, "tensor"),
        P(None, "tensor"),
        P(None, "tensor"),
        P(),
        P(None, "tensor"),
        P("tensor", None),
        P(),
        P(),
        P("dp", None),
        P("dp", None, "tensor"),
        P("dp", None, "tensor"),
        P("dp", "tensor", None),
        P(None, "tensor"),
        P(None, "tensor"),
        P("tensor", None),
    )
    out_specs = (
        P("dp", None),
        P(("dp", "tensor"), None),
        P(("dp", "tensor")),
        P("dp", "tensor"),
        P("dp", "tensor"),
        P("dp", "tensor"),
        P(("dp", "tensor")),
        P("dp", "tensor"),
        P("tensor", "dp"),
        P(("dp", "tensor")),
        P(("dp", "tensor"), None),
        P("dp", "tensor"),
        P("dp", "tensor"),
        P("tensor", "dp"),
        P("dp", None, "tensor"),
        P("dp", None, "tensor"),
        P("dp", "tensor", None),
    )
    return jax.shard_map(
        on_device, mesh=mesh, in_specs=in_specs, out_specs=out_specs, check_vma=False
    )
```

```python
import functools

import jax
import jax.numpy as jnp
import numpy as np
from jax import lax
from jax.experimental import pallas as pl
from jax.experimental.pallas import tpu as pltpu
from jax.sharding import PartitionSpec as P

HD = 128
RD = 64
VD = 128
TOPK = 6
SEQ = 256
CAP = 64
LANES = 128
EPSILON = 1e-06
HEAD = 256
KV = HD + VD
MIB = 1 << 20
VMEM = 60

bf16 = jnp.bfloat16
f32 = jnp.float32


def dot(a, b):
    return lax.dot_general(a, b, (((1,), (0,)), ((), ())), preferred_element_type=f32)


def dot_nt(a, b):
    return lax.dot_general(a, b, (((1,), (1,)), ((), ())), preferred_element_type=f32)


def dot_tn(a, b):
    return lax.dot_general(a, b, (((0,), (0,)), ((), ())), preferred_element_type=f32)


def rope_tables():
    frequency = np.float32(10000.0) ** (-np.arange(RD // 2, dtype=np.float32) * np.float32(2.0 / RD))
    angles = np.arange(SEQ, dtype=np.float32)[:, None] * frequency[None, :]
    blank = np.zeros((SEQ, LANES - RD), np.float32)
    cosine, sine = np.cos(angles), np.sin(angles)
    return (
        jnp.asarray(np.concatenate([cosine, cosine, blank], axis=1)),
        jnp.asarray(np.concatenate([-sine, sine, blank], axis=1)),
    )


def rotate(vector, cosines, sines):
    lane = lax.broadcasted_iota(jnp.int32, vector.shape, 1)
    swapped = jnp.where(
        lane < RD // 2, pltpu.roll(vector, LANES - RD // 2, 1), pltpu.roll(vector, RD // 2, 1)
    )
    return vector * cosines + swapped * sines


def rms_norm(values, gains):
    inv_rms = lax.rsqrt(jnp.mean(values * values, axis=-1, keepdims=True) + EPSILON)
    return (values * inv_rms * gains, inv_rms)


def rms_back(cotan, values, inv_rms, gains):
    weighted = cotan * gains
    inner_mean = jnp.mean(weighted * values, axis=-1, keepdims=True)
    value_grad = inv_rms * weighted - values * (inv_rms * inv_rms * inv_rms) * inner_mean
    gain_grad = jnp.sum(cotan * values * inv_rms, axis=0)
    return (value_grad, gain_grad)


def swap(array, axis, bits):
    count = lax.axis_size(axis)
    return lax.ppermute(array, axis, [(i, i ^ bits) for i in range(count)])


def chip_bits(core):
    bits = [2 << i for i in range((lax.axis_size("dp") // 2).bit_length() - 1)]
    return bits[::-1] if core else bits


def partner_list(core):
    partners = [0]
    for bit in chip_bits(core):
        partners = partners + [p + bit for p in partners]
    return partners


def swap_chips(array, step):
    count = lax.axis_size("dp")
    return lax.ppermute(array, "dp", [(i, i ^ chip_bits(i % 2)[step]) for i in range(count)])


def partner_order():
    core = lax.axis_index("dp") % 2
    lists = jnp.array([partner_list(0), partner_list(1)], jnp.int32)
    return jnp.concatenate([lists[1 - core] ^ 1, lists[core]])


def block_at(array, index, size, dim):
    return lax.dynamic_slice_in_dim(array, index * size, size, dim)


def by_partner(array, axis, dim):
    count = lax.axis_size(axis)
    own = lax.axis_index(axis)
    size = array.shape[dim] // count
    return [block_at(array, own ^ r, size, dim) for r in range(count)]


def reorder(array, axis, dim):
    return jnp.concatenate(by_partner(array, axis, dim), axis=dim)


def share(array, axis):
    blocks = {0: array}
    bit = lax.axis_size(axis) // 2
    while bit:
        blocks.update({r ^ bit: swap(block, axis, bit) for r, block in blocks.items()})
        bit //= 2
    return [blocks[r] for r in range(len(blocks))]


def trade(blocks, axis):
    return [blocks[0]] + [swap(blocks[r], axis, r) for r in range(1, len(blocks))]


def gather_chips(block):
    own = [block]
    for step in range(len(chip_bits(0))):
        own = own + [swap_chips(have, step) for have in own]
    return own


def both_cores(own):
    return [swap(have, "dp", 1) for have in own] + list(own)


def gather_dp(block):
    return both_cores(gather_chips(block))


def sum_chips(pairs):
    arrivals = []
    for step in reversed(range(len(chip_bits(0)))):
        got = [swap_chips(send, step) for _, send in pairs]
        arrivals.append(got)
        size = got[0].shape[0]
        sums = [keep.astype(f32) + g.astype(f32) for (keep, _), g in zip(pairs, got)]
        pairs = [(s[: size // 2], s[size // 2 :].astype(bf16)) for s in sums]
    return [s[0] for s in sums], arrivals


def sum_dp(far, near):
    here = (near.astype(f32) + swap(far, "dp", 1).astype(f32)).astype(bf16)
    half = here.shape[0] // 2
    return sum_chips([(here[:half], here[half:])])[0][0]


def total(blocks):
    return functools.reduce(jnp.add, [block.astype(f32) for block in blocks])


def after(values, *others):
    return lax.optimization_barrier((values, others))[0]


def pick_matrix(slots):
    toks = slots.shape[1]
    place = lax.broadcasted_iota(jnp.int32, (CAP, toks), 0)
    return jnp.concatenate(
        [
            jnp.where(place == slots[e : e + 1, :], 1.0, 0.0).astype(bf16)
            for e in range(slots.shape[0])
        ],
        axis=0,
    )


def fetch(refs, buffer, sems):
    step = pl.program_id(0)

    @pl.when(step == 0)
    def _():
        for i, ref in enumerate(refs):
            pltpu.make_async_copy(ref, buffer.at[i], sems.at[i]).start()

    pltpu.make_async_copy(refs[0], buffer.at[step], sems.at[step]).wait()
    return buffer.at[step]


def by_place(array, tensor, parts):
    size = array.shape[0] // parts
    return [array[pl.ds(pl.multiple_of((tensor ^ r) * size, size), size), :] for r in range(parts)]


def pick_grad_kernel(parts, src_ref, tensor_ref, slots_ref, block_ref, down_ref, rows_ref, dact_ref, placed):
    slots = slots_ref[0]
    blocks = by_place(block_ref.at[0], tensor_ref[0], parts)
    for r, block in enumerate(blocks):
        placed[r * block.shape[0] : (r + 1) * block.shape[0]] = block
    picked = dot(pick_matrix(slots), placed[...]).astype(bf16)
    for e in range(slots.shape[0]):
        rows_ref[e] = picked[e * CAP : (e + 1) * CAP]
    dact_ref[...] = dot_nt(placed[...], down_ref[...])


def pick_kernel(count, experts_all, aliased, slots_ref, router_ref, weights_ref, dact_ref, *refs):
    rows_ref, gate_ref, act_ref, delta_ref, buffer, sems = refs[count + aliased :]
    block = fetch(refs[:count], buffer, sems)
    slots = slots_ref[0]
    experts = slots.shape[0]
    picks = pick_matrix(slots)
    picked = dot(picks, block[...]).astype(bf16)
    for e in range(experts):
        rows_ref[e] = picked[e * CAP : (e + 1) * CAP]
    parts = dot_nt(router_ref[...], block[...])
    logits = parts[:experts_all] + parts[experts_all : 2 * experts_all] + parts[2 * experts_all :]
    spread = jnp.exp(logits - jnp.max(logits, axis=0, keepdims=True))
    prob = spread / jnp.sum(spread, axis=0, keepdims=True)
    for e in range(experts):
        chosen = picks[e * CAP : (e + 1) * CAP].astype(f32) * prob[e : e + 1, :]
        gate_ref[e] = jnp.broadcast_to(jnp.sum(chosen, axis=1, keepdims=True), (CAP, LANES))
    hidden = dot_nt(block[...], weights_ref[...])
    width = hidden.shape[1] // 2
    act, gate_delta, up_delta = gated(hidden[:, :width], hidden[:, width:], dact_ref[...])
    act_ref[...] = act.astype(bf16)
    delta_ref[:, :width] = gate_delta.astype(bf16)
    delta_ref[:, width:] = up_delta.astype(bf16)


def gated(gate_h, up_h, dact):
    sigmoid_h = jax.nn.sigmoid(gate_h)
    silu_h = gate_h * sigmoid_h
    gate_delta = dact * up_h * sigmoid_h * (1.0 + gate_h * (1.0 - sigmoid_h))
    return silu_h * up_h, gate_delta, dact * silu_h


def hidden_kernel(
    first_ref,
    rows_ref,
    grads_ref,
    gate_ref,
    expert_gate_ref,
    expert_up_ref,
    expert_down_ref,
    act_ref,
    gate_delta_ref,
    up_delta_ref,
    score_ref,
):
    rows = rows_ref[0]
    gate_h = dot_nt(rows, expert_gate_ref[0])
    up_h = dot_nt(rows, expert_up_ref[0])
    dact = dot_nt(grads_ref[0], expert_down_ref[0])
    gate = gate_ref[0][:, :1]
    act, gate_delta, up_delta = gated(gate_h, up_h, dact)
    act_ref[0] = (act * gate).astype(bf16)
    gate_delta_ref[0] = (gate_delta * gate).astype(bf16)
    up_delta_ref[0] = (up_delta * gate).astype(bf16)
    score = jnp.sum(act * dact, axis=1, keepdims=True)
    high = score.astype(bf16).astype(f32)
    lanes = score_ref.shape[2]
    lane = lax.broadcasted_iota(jnp.int32, (rows.shape[0], lanes), 1)
    mine = first_ref[0] + pl.program_id(0)
    score_ref[0] = jnp.where(
        lane == mine, high, jnp.where(lane == mine + lanes // 2, score - high, 0.0)
    ).astype(bf16)


def return_kernel(spec, slots_ref, *refs):
    pairs, scored, added, outputs, steps = spec
    deltas, weights = refs[:pairs], refs[pairs : 2 * pairs]
    shared_ref, shared_weight_ref = refs[2 * pairs : 2 * pairs + 2]
    rest = refs[2 * pairs + 2 :]
    score_ref, rest = (rest[0], rest[1:]) if scored else (None, rest)
    other_ref, rest = (rest[0], rest[1:]) if added else (None, rest)
    outs, picks, rows = rest[:outputs], rest[outputs], rest[outputs + 1]
    sources, _, chunk = rows.shape
    experts = slots_ref.shape[1]
    toks = picks.shape[2]
    step = pl.program_id(0)

    def store(s, columns, value):
        if added:
            value = value + other_ref[s, :, columns].astype(f32)
        out = outs[s // (sources // outputs)]
        out[s % (sources // outputs), :, columns] = value.astype(bf16)

    @pl.when(step == 0)
    def _():
        for s in range(sources):
            picks[s] = pick_matrix(slots_ref[s])
        if scored:
            for s in range(sources):
                score = jnp.concatenate(
                    [score_ref[e, s * CAP : (s + 1) * CAP] for e in range(experts)], axis=0
                )
                store(s, pl.ds(steps * chunk, score.shape[1]), dot_tn(picks[s], score))

    for e in range(experts):
        back = functools.reduce(
            jnp.add, [dot(d[e], w[e]) for d, w in zip(deltas, weights)]
        ).astype(bf16)
        for s in range(sources):
            rows[s, e * CAP : (e + 1) * CAP, :] = back[s * CAP : (s + 1) * CAP]
    columns = pl.ds(pl.multiple_of(step * chunk, chunk), chunk)
    for s in range(sources):
        summed = dot_tn(picks[s], rows[s]) + dot(
            shared_ref[s * toks : (s + 1) * toks], shared_weight_ref[...]
        )
        store(s, columns, summed)


def expert_grad_kernel(
    rows_ref,
    grads_ref,
    act_ref,
    gate_delta_ref,
    up_delta_ref,
    gate_grad_ref,
    up_grad_ref,
    down_grad_ref,
):
    rows = rows_ref[0]
    gate_grad_ref[0] = dot_tn(gate_delta_ref[0], rows)
    up_grad_ref[0] = dot_tn(up_delta_ref[0], rows)
    down_grad_ref[0] = dot_tn(act_ref[0], grads_ref[0])


def shared_grad_kernel(count, parts, src_ref, tensor_ref, delta_ref, act_ref, grad_ref, *refs):
    out_ref, buffer, placed, in_acc, down_acc, sems = refs[count:]
    step = pl.program_id(0)
    block = fetch(refs[:count], buffer, sems)
    rows = placed.shape[0] // parts
    for r, part in enumerate(by_place(grad_ref.at[0], tensor_ref[0], parts)):
        placed[r * rows : (r + 1) * rows] = part

    @pl.when(step == 0)
    def _():
        in_acc[...] = jnp.zeros_like(in_acc)
        down_acc[...] = jnp.zeros_like(down_acc)

    in_acc[...] += dot_tn(delta_ref[...], block[...])
    down_acc[...] += dot_tn(act_ref[...], placed[...])

    @pl.when(step == count - 1)
    def _():
        devices, rows, columns = out_ref.shape
        rows //= 3
        middle = in_acc.shape[0] // 2
        for j in range(devices):
            here = slice(j * columns, (j + 1) * columns)
            out_ref[j, :rows] = in_acc[:rows, here].astype(bf16)
            out_ref[j, rows : 2 * rows] = in_acc[middle : middle + rows, here].astype(bf16)
            out_ref[j, 2 * rows :] = down_acc[:rows, here].astype(bf16)


def rows_grad_kernel(src_ref, left_ref, right_ref, far_ref, near_ref):
    half, rows, _ = far_ref.shape
    for i in range(2 * half):
        start = pl.multiple_of(src_ref[i] * rows, rows)
        product = dot_tn(left_ref[:, pl.ds(start, rows)], right_ref[...]).astype(bf16)
        if i < half:
            far_ref[i] = product
        else:
            near_ref[i - half] = product


def columns_grad_kernel(parts, flat, src_ref, left_ref, logits_ref, block_ref, gain_ref, *refs):
    far_ref, near_ref, grads = refs[parts:]
    rows = left_ref.shape[0] // parts
    for r in range(parts):
        grads[r * rows : (r + 1) * rows] = refs[r][:rows]
    half, height, width = far_ref.shape
    wide, experts_all = left_ref.shape[1], logits_ref.shape[1]
    for i in range(2 * half):
        columns = pl.ds(pl.multiple_of(src_ref[i] * width, width), width)
        out = far_ref.at[i] if i < half else near_ref.at[i - half]
        out[:wide] = dot_tn(left_ref[...], grads[:, columns]).astype(bf16)
        router = dot_tn(logits_ref[...], block_ref[:, columns])
        rest = jnp.concatenate(
            [router, jnp.broadcast_to(gain_ref[:, columns], (height - wide - experts_all, width))],
            axis=0,
        )
        out[wide:] = rest.astype(bf16)


def normed_kernel(tokens_ref, gain_ref, down_ref, rope_ref, normed_ref, inv_ref, narrow_ref):
    normed, inv = rms_norm(tokens_ref[...].astype(f32), gain_ref[...])
    normed = normed.astype(bf16)
    normed_ref[...] = normed
    inv_ref[...] = inv
    cols = down_ref.shape[1]
    narrow_ref[:, :cols] = dot(normed, down_ref[...]).astype(bf16)
    narrow_ref[:, cols:] = dot_nt(normed, rope_ref[...]).astype(bf16)


def query_kernel(normed_ref, weight_ref, cosines_ref, sines_ref, query_ref):
    raw = dot(normed_ref[...], weight_ref[...])
    toks = raw.shape[0]
    for h in range(raw.shape[1] // (HD + RD)):
        start = h * (HD + RD)
        rope = jnp.concatenate(
            [raw[:, start + HD : start + HD + RD], jnp.zeros((toks, LANES - RD), f32)], axis=1
        )
        query_ref[:, h * HEAD : h * HEAD + HD] = raw[:, start : start + HD].astype(bf16)
        query_ref[:, h * HEAD + HD : (h + 1) * HEAD] = rotate(
            rope, cosines_ref[...], sines_ref[...]
        ).astype(bf16)


def causal(scores):
    later = lax.broadcasted_iota(jnp.int32, scores.shape, 1) > lax.broadcasted_iota(
        jnp.int32, scores.shape, 0
    )
    return jnp.where(later, -1e30, scores)


def attention_kernel(
    parts,
    tensor_ref,
    query_ref,
    cosines_ref,
    sines_ref,
    place_ref,
    gain_ref,
    up_ref,
    out_weight_ref,
    *refs,
):
    narrow = [ref[...] for ref in refs[:parts]]
    sums = refs[parts : 2 * parts]
    attended_ref, latent_ref, latent_normed_ref, inv_ref, kv_ref, rope_ref, lse_ref, natural = refs[
        2 * parts :
    ]
    toks = query_ref.shape[0]
    heads = query_ref.shape[1] // HEAD
    cols = up_ref.shape[0] // parts
    latent = jnp.concatenate([n[:, :cols] for n in narrow], axis=1)
    latent_ref[...] = latent
    normed, inv = rms_norm(latent.astype(f32), gain_ref[...])
    normed = normed.astype(bf16)
    latent_normed_ref[...] = normed
    inv_ref[...] = inv
    rope = dot(jnp.concatenate([n[:, cols:] for n in narrow], axis=1), place_ref[...])
    rope = rotate(rope, cosines_ref[...], sines_ref[...]).astype(bf16)
    rope_ref[...] = rope
    kv_ref[...] = dot(normed, up_ref[...]).astype(bf16)
    lane = lax.broadcasted_iota(jnp.int32, (toks, LANES), 1)
    lses = jnp.zeros((toks, LANES), f32)
    for h in range(heads):
        key = jnp.concatenate([kv_ref[:, h * KV : h * KV + HD], rope], axis=1)
        scores = causal(dot_nt(query_ref[:, h * HEAD : (h + 1) * HEAD], key) * (HD + RD) ** -0.5)
        top = jnp.max(scores, axis=1, keepdims=True)
        lse = top + jnp.log(jnp.sum(jnp.exp(scores - top), axis=1, keepdims=True))
        lses = jnp.where(lane == h, lse, lses)
        weights = jnp.exp(scores - lse).astype(bf16)
        natural[:, h * VD : (h + 1) * VD] = dot(
            weights, kv_ref[:, h * KV + HD : (h + 1) * KV]
        ).astype(bf16)
    lse_ref[...] = lses
    rows = toks // parts
    for r, block in enumerate(by_place(natural, tensor_ref[0], parts)):
        attended_ref[r * rows : (r + 1) * rows] = block
    for r in range(parts):
        product = dot(attended_ref[r * rows : (r + 1) * rows], out_weight_ref[...])
        sums[r][...] = product.astype(sums[r].dtype)


def attention_back_kernel(
    parts,
    tensor_ref,
    src_ref,
    query_ref,
    kv_ref,
    rope_ref,
    lse_ref,
    latent_ref,
    latent_normed_ref,
    inv_ref,
    cosines_ref,
    sines_ref,
    place_ref,
    gain_ref,
    up_ref,
    out_weight_ref,
    *refs,
):
    grads = refs[:parts]
    narrow = refs[parts : 2 * parts]
    query_grad_ref, up_far_ref, up_near_ref, natural, query_nat, kv_grad, narrow_nat, up_part = refs[
        2 * parts :
    ]
    toks = query_ref.shape[0]
    heads = query_ref.shape[1] // HEAD
    rows = toks // parts
    factor = (HD + RD) ** -0.5
    tensor = tensor_ref[0]
    for r in range(parts):
        place = pl.ds(pl.multiple_of((tensor ^ r) * rows, rows), rows)
        natural[place, :] = dot_nt(grads[r][:rows], out_weight_ref[...]).astype(bf16)
    rope = rope_ref[...]
    rope_sum = jnp.zeros((toks, LANES), f32)
    for h in range(heads):
        grad = natural[:, h * VD : (h + 1) * VD]
        query = query_ref[:, h * HEAD : (h + 1) * HEAD]
        key = jnp.concatenate([kv_ref[:, h * KV : h * KV + HD], rope], axis=1)
        scores = causal(dot_nt(query, key) * factor)
        probs = jnp.exp(scores - lse_ref[:, h : h + 1])
        kv_grad[:, h * KV + HD : (h + 1) * KV] = dot_tn(probs.astype(bf16), grad).astype(bf16)
        prob_dot = dot_nt(grad, kv_ref[:, h * KV + HD : (h + 1) * KV])
        inner = jnp.sum(probs * prob_dot, axis=1, keepdims=True)
        score_grad = (probs * (prob_dot - inner) * factor).astype(bf16)
        query_grad = dot(score_grad, key)
        start = h * (HD + RD)
        query_nat[:, start : start + HD] = query_grad[:, :HD].astype(bf16)
        query_nat[:, start + HD : start + HD + RD] = rotate(
            query_grad[:, HD:], cosines_ref[...], -sines_ref[...]
        )[:, :RD].astype(bf16)
        key_grad = dot_tn(score_grad, query)
        kv_grad[:, h * KV : h * KV + HD] = key_grad[:, :HD].astype(bf16)
        rope_sum = rope_sum + key_grad[:, HD:]
    for r, block in enumerate(by_place(query_nat, tensor, parts)):
        query_grad_ref[r * rows : (r + 1) * rows] = block
    latent_grad, _ = rms_back(
        dot_nt(kv_grad[...], up_ref[...]), latent_ref[...].astype(f32), inv_ref[...], gain_ref[...]
    )
    rope_sum = rotate(rope_sum, cosines_ref[...], -sines_ref[...]).astype(bf16)
    rope_sum = dot_nt(rope_sum, place_ref[...])
    cols = latent_grad.shape[1] // parts
    rope_cols = rope_sum.shape[1] // parts
    for k in range(parts):
        narrow_nat[:, :cols] = latent_grad[:, k * cols : (k + 1) * cols]
        narrow_nat[:, cols:] = rope_sum[:, k * rope_cols : (k + 1) * rope_cols]
        narrow[k][...] = narrow_nat[...].astype(narrow[k].dtype)
    up_part[...] = dot_tn(latent_normed_ref[...], kv_grad[...])
    half, up_rows, _ = up_far_ref.shape
    for i in range(2 * half):
        start = src_ref[i] * up_rows
        start = (start // cols ^ tensor) * cols + start % cols
        block = up_part[pl.ds(pl.multiple_of(start, up_rows), up_rows), :].astype(bf16)
        if i < half:
            up_far_ref[i] = block
        else:
            up_near_ref[i - half] = block


def normed_back_kernel(parts, tensor_ref, query_grad_ref, query_weight_ref, down_ref, rope_ref, *refs):
    narrow = refs[:parts]
    sums = refs[parts : 2 * parts]
    all_ref, natural = refs[2 * parts :]
    cols = down_ref.shape[1]
    natural[...] = total([ref[...] for ref in narrow])
    mine = jnp.concatenate(by_place(natural, tensor_ref[0], parts), axis=0).astype(bf16)
    all_ref[...] = mine
    rows = query_grad_ref.shape[0] // parts
    product = (
        dot_nt(query_grad_ref[...], query_weight_ref[...])
        + dot_nt(mine[:, :cols], down_ref[...])
        + dot(mine[:, cols:], rope_ref[...])
    )
    for r in range(parts):
        sums[r][...] = product[r * rows : (r + 1) * rows].astype(sums[r].dtype)


ANYWHERE = pl.BlockSpec(memory_space=pl.ANY)


def whole(array):
    rank = len(array.shape)
    return pl.BlockSpec(array.shape, lambda *_: (0,) * rank)


def params(mib):
    return pltpu.CompilerParams(vmem_limit_bytes=mib * MIB)


def cost(flops, bytes_accessed, transcendentals=0):
    return pl.CostEstimate(
        flops=int(flops), bytes_accessed=int(bytes_accessed), transcendentals=int(transcendentals)
    )


def pick_grads(src, tensor, parts, slots, grads, shared_down):
    count, experts, toks = slots.shape
    width = grads.shape[2]
    shared = shared_down.shape[0]
    return pl.pallas_call(
        functools.partial(pick_grad_kernel, parts),
        grid_spec=pltpu.PrefetchScalarGridSpec(
            num_scalar_prefetch=2,
            grid=(count,),
            in_specs=[
                pl.BlockSpec((1, experts, toks), lambda s, src, t: (s, 0, 0)),
                pl.BlockSpec((1, toks, width), lambda s, src, t: (src[s], 0, 0)),
                whole(shared_down),
            ],
            out_specs=[
                pl.BlockSpec((experts, CAP, width), lambda s, src, t: (0, s, 0)),
                pl.BlockSpec((toks, shared), lambda s, src, t: (s, 0)),
            ],
            scratch_shapes=[pltpu.VMEM((toks, width), bf16)],
        ),
        out_shape=[
            jax.ShapeDtypeStruct((experts, count * CAP, width), bf16),
            jax.ShapeDtypeStruct((count * toks, shared), f32),
        ],
        compiler_params=params(VMEM),
        cost_estimate=cost(
            2 * count * toks * width * (experts * CAP + shared), 4 * count * toks * width
        ),
    )(src, tensor, slots, grads, shared_down)


def pick_rows(blocks, first, slots, router, weights, dact, experts_all, results):
    count = len(blocks)
    every, experts, toks = slots.shape
    width = blocks[0].shape[1]
    shared = dact.shape[1]
    operands = [slots, router, weights, dact, *blocks, *results]
    return pl.pallas_call(
        functools.partial(pick_kernel, count, experts_all, len(results)),
        grid=(count,),
        in_specs=[
            pl.BlockSpec((1, experts, toks), lambda s: (s + first, 0, 0)),
            whole(router),
            whole(weights),
            pl.BlockSpec((toks, shared), lambda s: (s + first, 0)),
        ]
        + [ANYWHERE] * (count + len(results)),
        out_specs=[
            pl.BlockSpec((experts, CAP, width), lambda s: (0, s + first, 0)),
            pl.BlockSpec((experts, CAP, LANES), lambda s: (0, s + first, 0)),
            pl.BlockSpec((toks, shared), lambda s: (s + first, 0)),
            pl.BlockSpec((toks, 2 * shared), lambda s: (s + first, 0)),
        ],
        out_shape=[
            shape(bf16, experts, every * CAP, width),
            shape(f32, experts, every * CAP, LANES),
            shape(bf16, every * toks, shared),
            shape(bf16, every * toks, 2 * shared),
        ],
        input_output_aliases={len(operands) - len(results) + i: i for i in range(len(results))},
        scratch_shapes=[
            pltpu.VMEM((count, toks, width), bf16),
            pltpu.SemaphoreType.DMA((count,)),
        ],
        compiler_params=params(VMEM),
        cost_estimate=cost(
            2 * count * toks * width * (experts * CAP + router.shape[0] + 2 * shared),
            4 * count * toks * width,
        ),
    )(*operands)


def expert_hidden(first, rows, grads, gate, expert_gate, expert_up, expert_down, lanes):
    experts, slot_rows, width = rows.shape
    hidden = expert_gate.shape[1]

    def per_expert(array):
        return pl.BlockSpec((1,) + array.shape[1:], lambda e: (e, 0, 0))

    narrow = jax.ShapeDtypeStruct((experts, slot_rows, hidden), bf16)
    score = jax.ShapeDtypeStruct((experts, slot_rows, lanes), bf16)
    return pl.pallas_call(
        hidden_kernel,
        grid=(experts,),
        in_specs=[pl.BlockSpec(memory_space=pltpu.SMEM)]
        + [per_expert(a) for a in (rows, grads, gate, expert_gate, expert_up, expert_down)],
        out_specs=[per_expert(narrow)] * 3 + [per_expert(score)],
        out_shape=[narrow] * 3 + [score],
        compiler_params=params(VMEM),
        cost_estimate=cost(
            6 * experts * slot_rows * width * hidden,
            experts * (4 * slot_rows * width + 6 * hidden * width),
            experts * slot_rows * hidden,
        ),
    )(first, rows, grads, gate, expert_gate, expert_up, expert_down)


def return_rows(half, slots, deltas, weights, shared, shared_weight, score, start, size, other):
    experts, slot_rows, hidden = deltas[0].shape
    sources = slots.shape[0] // 2
    toks = slots.shape[2]
    chunk = min(512, size)
    steps = size // chunk
    first = start // chunk
    outputs = 1 + half
    lanes = 0 if score is None else score.shape[2]
    in_specs = (
        [pl.BlockSpec((sources,) + slots.shape[1:], lambda n: (half, 0, 0))]
        + [pl.BlockSpec((experts, slot_rows // 2, hidden), lambda n: (0, half, 0))] * len(deltas)
        + [pl.BlockSpec((experts, hidden, chunk), lambda n: (0, 0, n + first))] * len(weights)
        + [
            pl.BlockSpec((sources * toks, shared.shape[1]), lambda n: (half, 0)),
            pl.BlockSpec((shared.shape[1], chunk), lambda n: (0, n + first)),
        ]
    )
    operands = [slots, *deltas, *weights, shared, shared_weight]
    if score is not None:
        in_specs.append(pl.BlockSpec((experts, slot_rows // 2, lanes), lambda n: (0, half, 0)))
        operands.append(score)
    if other is not None:
        in_specs.append(whole(other))
        operands.append(other)
    out = jax.ShapeDtypeStruct((sources // outputs, toks, size + lanes), bf16)
    return pl.pallas_call(
        functools.partial(
            return_kernel, (len(deltas), score is not None, other is not None, outputs, steps)
        ),
        grid=(steps,),
        in_specs=in_specs,
        out_specs=[whole(out)] * outputs,
        out_shape=[out] * outputs,
        scratch_shapes=[
            pltpu.VMEM((sources, experts * CAP, toks), bf16),
            pltpu.VMEM((sources, experts * CAP, chunk), bf16),
        ],
        compiler_params=params(VMEM),
        cost_estimate=cost(
            2 * experts * slot_rows // 2 * size * (hidden * len(deltas) + toks)
            + 2 * sources * toks * size * shared.shape[1],
            2 * size * (experts * hidden * len(deltas) + sources * toks),
        ),
    )(*operands)


def expert_grads(rows, grads, act, gate_delta, up_delta):
    experts, slot_rows, width = rows.shape
    hidden = act.shape[2]

    def per_expert(array):
        return pl.BlockSpec((1,) + array.shape[1:], lambda e: (e, 0, 0))

    out = jax.ShapeDtypeStruct((experts, hidden, width), f32)
    return pl.pallas_call(
        expert_grad_kernel,
        grid=(experts,),
        in_specs=[per_expert(a) for a in (rows, grads, act, gate_delta, up_delta)],
        out_specs=[per_expert(out)] * 3,
        out_shape=[out] * 3,
        compiler_params=params(VMEM),
        cost_estimate=cost(
            6 * experts * slot_rows * width * hidden,
            experts * (4 * slot_rows * width + 12 * hidden * width),
        ),
    )(rows, grads, act, gate_delta, up_delta)


def shared_grads(src, tensor, parts, blocks, grads, delta, act, cols):
    count = grads.shape[0]
    toks, width = blocks[0].shape
    out = jax.ShapeDtypeStruct((count, 3 * cols, width // count), bf16)
    return pl.pallas_call(
        functools.partial(shared_grad_kernel, count, parts),
        grid_spec=pltpu.PrefetchScalarGridSpec(
            num_scalar_prefetch=2,
            grid=(count,),
            in_specs=[
                pl.BlockSpec((toks, delta.shape[1]), lambda s, src, t: (s, 0)),
                pl.BlockSpec((toks, act.shape[1]), lambda s, src, t: (s, 0)),
                pl.BlockSpec((1, toks, width), lambda s, src, t: (src[s], 0, 0)),
            ]
            + [ANYWHERE] * count,
            out_specs=whole(out),
            scratch_shapes=[
                pltpu.VMEM((count, toks, width), bf16),
                pltpu.VMEM((toks, width), bf16),
                pltpu.VMEM((delta.shape[1], width), f32),
                pltpu.VMEM((act.shape[1], width), f32),
                pltpu.SemaphoreType.DMA((count,)),
            ],
        ),
        out_shape=out,
        compiler_params=params(VMEM),
        cost_estimate=cost(
            2 * count * toks * width * (delta.shape[1] + act.shape[1]), 4 * count * toks * width
        ),
    )(src, tensor, delta, act, grads, *blocks)


def single(kernel, outs, operands, scalars=(), scratch=(), flops=0, transcendentals=0):
    return pl.pallas_call(
        kernel,
        grid_spec=pltpu.PrefetchScalarGridSpec(
            num_scalar_prefetch=len(scalars),
            grid=(1,),
            in_specs=[whole(a) for a in operands],
            out_specs=[whole(o) for o in outs],
            scratch_shapes=list(scratch),
        ),
        out_shape=list(outs),
        compiler_params=params(VMEM),
        cost_estimate=cost(flops, sum(a.size * a.dtype.itemsize for a in operands), transcendentals),
    )(*scalars, *operands)


def shape(dtype, *sizes):
    return jax.ShapeDtypeStruct(sizes, dtype)


def on_device(
    tokens,
    cotangent,
    attn_gain,
    q_weight,
    kv_down,
    k_rope_weight,
    kv_gain,
    kv_up,
    o_weight,
    ffn_gain,
    router_weight,
    expert_ids,
    expert_gate,
    expert_up,
    expert_down,
    shared_gate,
    shared_up,
    shared_down,
):
    n_t = lax.axis_size("tensor")
    n_d = lax.axis_size("dp")
    half = n_d // 2
    t_index = lax.axis_index("tensor")
    d_index = lax.axis_index("dp")
    toks, width = tokens.shape
    own_toks = toks // n_t
    rows_d = width // n_d
    q_cols = q_weight.shape[1]
    heads = q_cols // (HD + RD)
    experts_all = router_weight.shape[1]
    experts = expert_gate.shape[0]
    cosines, sines = rope_tables()
    order = partner_order()
    src = d_index.astype(jnp.int32) ^ order
    sources = [src[i] for i in range(n_d)]
    lat_cols = kv_down.shape[1]
    lat_rank = kv_up.shape[0]
    rope_cols = k_rope_weight.shape[1]
    narrow_cols = lat_cols + rope_cols
    expert_gate_t = expert_gate.transpose(0, 2, 1)
    expert_up_t = expert_up.transpose(0, 2, 1)

    tokens_p = by_partner(tokens, "tensor", 0)
    tokens_own = tokens_p[0].astype(f32)
    cot_own = block_at(cotangent, t_index, own_toks, 0).astype(f32)
    cot_all = lax.all_gather(cotangent, "dp")
    tensor = t_index.astype(jnp.int32).reshape(1)
    ids = reorder(expert_ids, "tensor", 0)
    every = jnp.arange(experts_all, dtype=jnp.int32)
    member = jnp.any(ids.T[:, None, :] == every[None, :, None], axis=0)
    before = (jnp.arange(toks)[:, None] < jnp.arange(toks)[None, :]).astype(bf16)
    rank = dot(member.astype(bf16), before)
    slots_own = jnp.where(member, rank, -1.0).astype(bf16)
    slots = jnp.stack([block_at(b, d_index, experts, 0) for b in gather_dp(slots_own)]).astype(
        jnp.int32
    )
    router_t = jnp.roll(router_weight.T, -d_index * experts, axis=0)
    router_parts = []
    rest = router_t
    for _ in range(3):
        part = lax.reduce_precision(rest, 8, 7)
        router_parts.append(part.astype(bf16))
        rest = rest - part
    router_parts = jnp.concatenate(router_parts, axis=0)
    shared_cols = shared_down.shape[0] // n_d
    shared_pad = -shared_cols % LANES
    shared_gate_t, shared_up_t, shared_out = [
        jnp.pad(block_at(w, d_index, shared_cols, 0), ((0, shared_pad), (0, 0)))
        for w in (shared_gate.T, shared_up.T, shared_down)
    ]
    shared_in = jnp.concatenate([shared_gate_t, shared_up_t], axis=0)
    grad_rows, shared_dact = pick_grads(src, tensor, n_t, slots, cot_all, shared_out)

    kv_up_p = reorder(kv_up, "tensor", 0)
    kv_gain_p = reorder(kv_gain, "tensor", 0)[None]
    rope_t = k_rope_weight.T
    rope_place = (
        (t_index ^ jnp.arange(n_t)[:, None, None]) * rope_cols + jnp.arange(rope_cols)[None, :, None]
        == jnp.arange(LANES)
    ).astype(bf16).reshape(RD, LANES)
    normed, inv_first, narrow_own = single(
        normed_kernel,
        [shape(bf16, toks, width), shape(f32, toks, 1), shape(bf16, toks, narrow_cols)],
        [tokens, attn_gain[None], kv_down, rope_t],
        flops=2 * toks * width * narrow_cols,
    )
    narrow_blocks = share(narrow_own, "tensor")
    query = single(
        query_kernel,
        [shape(bf16, toks, heads * HEAD)],
        [normed, q_weight, cosines, sines],
        flops=2 * toks * width * q_cols,
    )[0]
    results = single(
        functools.partial(attention_kernel, n_t),
        [shape(f32 if r == 0 else bf16, own_toks, width) for r in range(n_t)]
        + [
            shape(bf16, toks, heads * VD),
            shape(bf16, toks, lat_rank),
            shape(bf16, toks, lat_rank),
            shape(f32, toks, 1),
            shape(bf16, toks, heads * KV),
            shape(bf16, toks, LANES),
            shape(f32, toks, LANES),
        ],
        [query, cosines, sines, rope_place, kv_gain_p, kv_up_p, o_weight, *narrow_blocks],
        scalars=[tensor],
        scratch=[pltpu.VMEM((toks, heads * VD), bf16)],
        flops=2 * toks * heads * (KV * lat_rank + 2 * HEAD * toks + VD * width),
        transcendentals=2 * heads * toks * toks,
    )
    attn_part = results[:n_t]
    attended_p, latent, latent_normed, inv_latent, key_value, rope_rot, lse = results[n_t:]
    attn_sum = total(trade(attn_part, "tensor"))
    hidden_one = tokens_own + attn_sum
    ffn_normed_f, inv_second = rms_norm(hidden_one, ffn_gain)
    ffn_own = ffn_normed_f.astype(bf16)
    ffn_block = jnp.concatenate(share(ffn_own, "tensor"), axis=0)
    near_blocks = gather_chips(ffn_block)
    near_blocks = near_blocks[:-1] + [after(near_blocks[-1], grad_rows)]
    far_blocks = [swap(block, "dp", 1) for block in near_blocks]
    blocks = far_blocks + near_blocks

    results = []
    for side, first, start, stop in (
        (near_blocks, half, 0, half - 1),
        (far_blocks, 0, 0, half - 1),
        (near_blocks, half, half - 1, half),
        (far_blocks, 0, half - 1, half),
    ):
        results = pick_rows(
            side[start:stop], first + start, slots, router_parts, shared_in, shared_dact, experts_all,
            results,
        )
    rows, gate, shared_act, shared_delta = results
    lanes = -(-2 * experts_all // LANES) * LANES
    first = (d_index * experts).astype(jnp.int32).reshape(1)
    act, gate_delta, up_delta, score = expert_hidden(
        first, rows, grad_rows, gate, expert_gate_t, expert_up_t, expert_down, lanes
    )

    def send_back(sum_here):
        return trade(
            [sum_here[k * own_toks : (k + 1) * own_toks].astype(bf16) for k in range(n_t)], "tensor"
        )

    pieces = 2
    size = width // pieces
    deltas, delta_weights = [gate_delta, up_delta], [expert_gate_t, expert_up_t]
    others = [
        return_rows(
            0, slots, deltas, delta_weights, shared_delta, shared_in,
            score if i == pieces - 1 else None, i * size, size, None,
        )[0]
        for i in range(pieces)
    ]
    others = [swap(other, "dp", 1) for other in others]
    mine = [
        return_rows(
            1, slots, deltas, delta_weights, shared_delta, shared_in,
            score if i == pieces - 1 else None, i * size, size, others[i],
        )
        for i in range(pieces)
    ]
    sums, arrivals = sum_chips(mine)

    other = return_rows(
        0, slots, [after(act, mine)], [expert_down], shared_act, shared_out, None, 0, width, None
    )[0]
    other = swap(other, "dp", 1)
    out_pair = return_rows(
        1, slots, [act], [expert_down], shared_act, shared_out, None, 0, width,
        after(other, arrivals[0][0]),
    )
    shared_rows = shared_cols + -shared_cols % 16
    sums[0] = after(sums[0], out_pair)
    back_sums = [total(send_back(s)) for s in sums]
    back_sum = jnp.concatenate(back_sums[:-1] + [back_sums[-1][:, :size]], axis=1)
    score_sum = back_sums[-1][:, size:]
    shared_all = shared_grads(
        src, tensor, n_t, blocks, cot_all, *after((shared_delta, shared_act), arrivals[-1]), shared_rows
    )
    out_pair = after(out_pair, arrivals[-1])
    out_sums, out_arrivals = sum_chips([out_pair])
    out_here = out_sums[0]

    shared_all = lax.all_to_all(shared_all, "dp", 0, 0, tiled=True).astype(f32)
    shared_gate_grad, shared_up_grad, shared_down_grad = [
        shared_all[:, i * shared_rows : i * shared_rows + shared_cols].reshape(-1, rows_d)
        for i in range(3)
    ]

    logits = jnp.dot(ffn_own.astype(f32), router_weight, precision=lax.Precision.HIGHEST)
    router_prob = jax.nn.softmax(logits, axis=-1)
    prob_grad = score_sum[:, :experts_all] + score_sum[:, lanes // 2 : lanes // 2 + experts_all]
    logit_grad = (
        router_prob * (prob_grad - jnp.sum(router_prob * prob_grad, axis=-1, keepdims=True))
    ).astype(bf16)
    ffn_normed_grad = back_sum + jnp.dot(
        logit_grad.astype(f32), router_weight.T, precision=lax.Precision.HIGHEST
    )
    hidden_norm_grad, ffn_gain_part = rms_back(ffn_normed_grad, hidden_one, inv_second, ffn_gain)
    hidden_grad = cot_own + hidden_norm_grad
    flat_logits = logit_grad.reshape(-1, width)
    flat = flat_logits.shape[0]
    extra = jnp.concatenate(
        [
            flat_logits,
            ffn_gain_part.astype(bf16)[None],
            jnp.zeros((-(flat + 1) % 16, width), bf16),
        ],
        axis=0,
    )
    message = jnp.concatenate([hidden_grad.astype(bf16), extra], axis=0)
    message = after(message, out_arrivals[0])
    shared_grads_t = after(share(message, "tensor"), out_arrivals[-1])
    expert_gate_grad, expert_up_grad, expert_down_grad = expert_grads(
        rows, grad_rows, *after((act, gate_delta, up_delta), message)
    )
    out_sum = total(send_back(after(out_here, shared_grads_t)))
    output_own = (hidden_one + out_sum).astype(bf16)

    lat_rows = lat_rank // n_d
    results = single(
        functools.partial(attention_back_kernel, n_t),
        [shape(f32 if r == 0 else bf16, toks, narrow_cols) for r in range(n_t)]
        + [
            shape(bf16, toks, q_cols),
            shape(bf16, half, lat_rows, heads * KV),
            shape(bf16, half, lat_rows, heads * KV),
        ],
        [
            query, key_value, rope_rot, lse, latent, latent_normed, inv_latent, cosines, sines,
            rope_place, kv_gain_p, kv_up_p, o_weight, *shared_grads_t,
        ],
        scalars=[tensor, src],
        scratch=[
            pltpu.VMEM((toks, heads * VD), bf16),
            pltpu.VMEM((toks, q_cols), bf16),
            pltpu.VMEM((toks, heads * KV), bf16),
            pltpu.VMEM((toks, narrow_cols), f32),
            pltpu.VMEM((lat_rank, heads * KV), f32),
        ],
        flops=2 * toks * heads * (2 * KV * lat_rank + 5 * HEAD * toks + VD * width),
        transcendentals=heads * toks * toks,
    )
    latent_parts = results[:n_t]
    query_grad_p, kv_up_far, kv_up_near = results[n_t:]
    results = single(
        functools.partial(normed_back_kernel, n_t),
        [shape(f32 if r == 0 else bf16, own_toks, width) for r in range(n_t)]
        + [shape(bf16, toks, narrow_cols)],
        [query_grad_p, q_weight, kv_down, rope_t, *trade(latent_parts, "tensor")],
        scalars=[tensor],
        scratch=[pltpu.VMEM((toks, narrow_cols), f32)],
        flops=2 * toks * width * (q_cols + narrow_cols),
    )
    normed_part, narrow_p = results[:n_t], results[n_t]
    output_own = after(output_own, normed_part)
    output = reorder(jnp.concatenate(share(output_own, "tensor"), axis=0), "tensor", 0)
    normed_grad = total(trade(normed_part, "tensor"))
    inv_first_own = block_at(inv_first, t_index, own_toks, 0)
    input_norm_grad, _ = rms_back(normed_grad, tokens_own, inv_first_own, attn_gain)
    input_grad = hidden_grad + input_norm_grad

    logit_p = jnp.concatenate(
        [b[own_toks : own_toks + flat].reshape(own_toks, experts_all) for b in shared_grads_t], axis=0
    )
    gain_part = total([b[own_toks + flat] for b in shared_grads_t])[None]
    out_cols = attended_p.shape[1]
    height = out_cols + experts_all + 16
    columns = sum_dp(
        *single(
            functools.partial(columns_grad_kernel, n_t, flat),
            [shape(bf16, half, height, rows_d)] * 2,
            [attended_p, logit_p, ffn_block, gain_part, *shared_grads_t],
            scalars=[src],
            scratch=[pltpu.VMEM((toks, width), bf16)],
            flops=2 * toks * width * height,
        )
    )
    o_weight_grad = columns[:out_cols]
    device_rows = width // (n_d * n_t)
    router_grad = block_at(
        columns[out_cols : out_cols + experts_all], t_index, device_rows, 1
    ).T
    ffn_gain_grad = block_at(columns[out_cols + experts_all], t_index, device_rows, 0)

    def rows_grad(left, right):
        return sum_dp(
            *single(
                rows_grad_kernel,
                [shape(bf16, half, rows_d, right.shape[1])] * 2,
                [left, right],
                scalars=[src],
                flops=2 * toks * width * right.shape[1],
            )
        )

    normed_p = reorder(normed, "tensor", 0)
    q_weight_grad = rows_grad(normed_p, query_grad_p)
    narrow_grad = rows_grad(normed_p, narrow_p)
    kv_down_grad = narrow_grad[:, :lat_cols]
    k_rope_grad = narrow_grad[:, lat_cols:]
    kv_up_grad = sum_dp(kv_up_far, kv_up_near)

    attn_gain_part = jnp.sum(
        block_at(q_weight, d_index, rows_d, 0).astype(f32) * q_weight_grad, axis=1
    ) + jnp.sum(
        block_at(kv_down, d_index, rows_d, 0).astype(f32) * kv_down_grad, axis=1
    ) + jnp.sum(
        block_at(k_rope_weight, d_index, rows_d, 0).astype(f32) * k_rope_grad, axis=1
    )
    attn_gain_part = attn_gain_part / block_at(attn_gain, d_index, rows_d, 0)
    kv_gain_part = jnp.sum(
        block_at(kv_up, d_index, lat_rows, 0).astype(f32) * kv_up_grad, axis=1
    ) / block_at(kv_gain, d_index, lat_rows, 0)
    gains = jnp.concatenate(
        [attn_gain_part.reshape(n_t, 1, -1), kv_gain_part.reshape(n_t, 1, -1)], axis=2
    )
    gains = total(trade([b[0] for b in by_partner(gains, "tensor", 0)], "tensor"))[0]
    attn_gain_grad = gains[:device_rows]
    kv_gain_grad = gains[device_rows:]

    return (
        output,
        input_grad,
        attn_gain_grad,
        q_weight_grad,
        kv_down_grad,
        k_rope_grad,
        kv_gain_grad,
        kv_up_grad,
        o_weight_grad,
        ffn_gain_grad,
        router_grad,
        shared_gate_grad.T,
        shared_up_grad.T,
        shared_down_grad,
        expert_gate_grad.transpose(0, 2, 1),
        expert_up_grad.transpose(0, 2, 1),
        expert_down_grad,
    )


def solution(mesh):
    in_specs = (
        P("dp", None),
        P("dp", None),
        P(),
        P(None, "tensor"),
        P(None, "tensor"),
        P(None, "tensor"),
        P(),
        P(None, "tensor"),
        P("tensor", None),
        P(),
        P(),
        P("dp", None),
        P("dp", None, "tensor"),
        P("dp", None, "tensor"),
        P("dp", "tensor", None),
        P(None, "tensor"),
        P(None, "tensor"),
        P("tensor", None),
    )
    out_specs = (
        P("dp", None),
        P(("dp", "tensor"), None),
        P(("dp", "tensor")),
        P("dp", "tensor"),
        P("dp", "tensor"),
        P("dp", "tensor"),
        P(("dp", "tensor")),
        P("dp", "tensor"),
        P("tensor", "dp"),
        P(("dp", "tensor")),
        P(("dp", "tensor"), None),
        P("dp", "tensor"),
        P("dp", "tensor"),
        P("tensor", "dp"),
        P("dp", None, "tensor"),
        P("dp", None, "tensor"),
        P("dp", "tensor", None),
    )
    return jax.shard_map(
        on_device, mesh=mesh, in_specs=in_specs, out_specs=out_specs, check_vma=False
    )
```

```python
import functools

import jax
import jax.numpy as jnp
import numpy as np
from jax import lax
from jax.experimental import pallas as pl
from jax.experimental.pallas import tpu as pltpu
from jax.sharding import PartitionSpec as P

HD = 128
RD = 64
VD = 128
TOPK = 6
SEQ = 256
CAP = 64
LANES = 128
EPSILON = 1e-06
HEAD = 256
KV = HD + VD
MIB = 1 << 20
VMEM = 60

bf16 = jnp.bfloat16
f32 = jnp.float32


def dot(a, b):
    return lax.dot_general(a, b, (((1,), (0,)), ((), ())), preferred_element_type=f32)


def dot_nt(a, b):
    return lax.dot_general(a, b, (((1,), (1,)), ((), ())), preferred_element_type=f32)


def dot_tn(a, b):
    return lax.dot_general(a, b, (((0,), (0,)), ((), ())), preferred_element_type=f32)


def rope_tables():
    frequency = np.float32(10000.0) ** (-np.arange(RD // 2, dtype=np.float32) * np.float32(2.0 / RD))
    angles = np.arange(SEQ, dtype=np.float32)[:, None] * frequency[None, :]
    blank = np.zeros((SEQ, LANES - RD), np.float32)
    cosine, sine = np.cos(angles), np.sin(angles)
    return (
        jnp.asarray(np.concatenate([cosine, cosine, blank], axis=1)),
        jnp.asarray(np.concatenate([-sine, sine, blank], axis=1)),
    )


def rotate(vector, cosines, sines):
    lane = lax.broadcasted_iota(jnp.int32, vector.shape, 1)
    swapped = jnp.where(
        lane < RD // 2, pltpu.roll(vector, LANES - RD // 2, 1), pltpu.roll(vector, RD // 2, 1)
    )
    return vector * cosines + swapped * sines


def rms_norm(values, gains):
    inv_rms = lax.rsqrt(jnp.mean(values * values, axis=-1, keepdims=True) + EPSILON)
    return (values * inv_rms * gains, inv_rms)


def rms_back(cotan, values, inv_rms, gains):
    weighted = cotan * gains
    inner_mean = jnp.mean(weighted * values, axis=-1, keepdims=True)
    value_grad = inv_rms * weighted - values * (inv_rms * inv_rms * inv_rms) * inner_mean
    gain_grad = jnp.sum(cotan * values * inv_rms, axis=0)
    return (value_grad, gain_grad)


def swap(array, axis, bits):
    count = lax.axis_size(axis)
    return lax.ppermute(array, axis, [(i, i ^ bits) for i in range(count)])


def chip_bits(core):
    bits = [2 << i for i in range((lax.axis_size("dp") // 2).bit_length() - 1)]
    return bits[::-1] if core else bits


def partner_list(core):
    partners = [0]
    for bit in chip_bits(core):
        partners = partners + [p + bit for p in partners]
    return partners


def swap_chips(array, step):
    count = lax.axis_size("dp")
    return lax.ppermute(array, "dp", [(i, i ^ chip_bits(i % 2)[step]) for i in range(count)])


def partner_order():
    core = lax.axis_index("dp") % 2
    lists = jnp.array([partner_list(0), partner_list(1)], jnp.int32)
    return jnp.concatenate([lists[1 - core] ^ 1, lists[core]])


def block_at(array, index, size, dim):
    return lax.dynamic_slice_in_dim(array, index * size, size, dim)


def by_partner(array, axis, dim):
    count = lax.axis_size(axis)
    own = lax.axis_index(axis)
    size = array.shape[dim] // count
    return [block_at(array, own ^ r, size, dim) for r in range(count)]


def reorder(array, axis, dim):
    return jnp.concatenate(by_partner(array, axis, dim), axis=dim)


def share(array, axis):
    return [array] + [swap(array, axis, r) for r in range(1, lax.axis_size(axis))]


def share_far_first(array, axis):
    blocks = {0: array}
    bit = lax.axis_size(axis) // 2
    while bit:
        blocks.update(
            {r ^ bit: swap(block, axis, bit) for r, block in blocks.items()}
        )
        bit //= 2
    return [blocks[r] for r in range(len(blocks))]


def trade(blocks, axis):
    return [blocks[0]] + [swap(blocks[r], axis, r) for r in range(1, len(blocks))]


def sum_along(blocks, sent, axis):
    bit, got = 1, sent
    while True:
        stay = [r for r in blocks if not r & bit]
        rows = blocks[0].shape[0]
        blocks = {
            r: blocks[r].astype(f32) + got[i * rows : (i + 1) * rows].astype(f32)
            for i, r in enumerate(stay)
        }
        bit *= 2
        if bit == lax.axis_size(axis):
            return blocks[0]
        got = swap(
            jnp.concatenate([blocks[r].astype(bf16) for r in blocks if r & bit], axis=0), axis, bit
        )


def gather_chips(block, between):
    own = [block]
    for step in range(len(chip_bits(0))):
        own = own + [
            swap_chips(after(have, between) if i else have, step) for i, have in enumerate(own)
        ]
    return own


def sum_chips(pairs, hook=lambda step, arrived: arrived):
    arrivals = []
    for step in reversed(range(len(chip_bits(0)))):
        got = hook(len(arrivals) // 2, [swap_chips(send, step) for _, send in pairs])
        arrivals.append(got)
        size = got[0].shape[0]
        sums = [keep.astype(f32) + g.astype(f32) for (keep, _), g in zip(pairs, got)]
        pairs = [(s[: size // 2], s[size // 2 :].astype(bf16)) for s in sums]
        arrivals.append([send for _, send in pairs])
    return [s[0] for s in sums], arrivals


def sum_cores(terms):
    pairs = []
    for far, near in terms:
        got = swap(far, "dp", 1)
        half = near.shape[0] // 2
        keep = near[:half].astype(f32) + got[:half].astype(f32)
        send = (near[half:].astype(f32) + got[half:].astype(f32)).astype(bf16)
        pairs.append((keep, send))
    return pairs


def total(blocks):
    return functools.reduce(jnp.add, [block.astype(f32) for block in blocks])


def after(values, *others):
    return lax.optimization_barrier((values, others))[0]


def pick_matrix(slots):
    toks = slots.shape[1]
    place = lax.broadcasted_iota(jnp.int32, (CAP, toks), 0)
    return jnp.concatenate(
        [
            jnp.where(place == slots[e : e + 1, :], 1.0, 0.0).astype(bf16)
            for e in range(slots.shape[0])
        ],
        axis=0,
    )


def fetch(refs, buffer, sems):
    step = pl.program_id(0)

    @pl.when(step == 0)
    def _():
        for i, ref in enumerate(refs):
            pltpu.make_async_copy(ref, buffer.at[i], sems.at[i]).start()

    pltpu.make_async_copy(refs[0], buffer.at[step], sems.at[step]).wait()
    return buffer.at[step]


def by_place(array, tensor, parts):
    size = array.shape[0] // parts
    return [array[pl.ds(pl.multiple_of((tensor ^ r) * size, size), size), :] for r in range(parts)]


def pick_grad_kernel(parts, src_ref, tensor_ref, slots_ref, block_ref, down_ref, rows_ref, dact_ref, placed):
    slots = slots_ref[0]
    blocks = by_place(block_ref.at[0], tensor_ref[0], parts)
    for r, block in enumerate(blocks):
        placed[r * block.shape[0] : (r + 1) * block.shape[0]] = block
    picked = dot(pick_matrix(slots), placed[...]).astype(bf16)
    for e in range(slots.shape[0]):
        rows_ref[e] = picked[e * CAP : (e + 1) * CAP]
    dact_ref[...] = dot_nt(placed[...], down_ref[...])


def pick_kernel(count, experts_all, aliased, slots_ref, router_ref, weights_ref, dact_ref, *refs):
    rows_ref, gate_ref, act_ref, delta_ref, buffer, sems = refs[count + aliased :]
    block = fetch(refs[:count], buffer, sems)
    slots = slots_ref[0]
    experts = slots.shape[0]
    picks = pick_matrix(slots)
    picked = dot(picks, block[...]).astype(bf16)
    for e in range(experts):
        rows_ref[e] = picked[e * CAP : (e + 1) * CAP]
    parts = dot_nt(router_ref[...], block[...])
    logits = parts[:experts_all] + parts[experts_all : 2 * experts_all] + parts[2 * experts_all :]
    spread = jnp.exp(logits - jnp.max(logits, axis=0, keepdims=True))
    prob = spread / jnp.sum(spread, axis=0, keepdims=True)
    for e in range(experts):
        chosen = picks[e * CAP : (e + 1) * CAP].astype(f32) * prob[e : e + 1, :]
        gate_ref[e] = jnp.broadcast_to(jnp.sum(chosen, axis=1, keepdims=True), (CAP, LANES))
    hidden = dot_nt(block[...], weights_ref[...])
    width = hidden.shape[1] // 2
    act, gate_delta, up_delta = gated(hidden[:, :width], hidden[:, width:], dact_ref[...])
    act_ref[...] = act.astype(bf16)
    delta_ref[:, :width] = gate_delta.astype(bf16)
    delta_ref[:, width:] = up_delta.astype(bf16)


def gated(gate_h, up_h, dact):
    sigmoid_h = jax.nn.sigmoid(gate_h)
    silu_h = gate_h * sigmoid_h
    gate_delta = dact * up_h * sigmoid_h * (1.0 + gate_h * (1.0 - sigmoid_h))
    return silu_h * up_h, gate_delta, dact * silu_h


def hidden_kernel(
    first_ref,
    rows_ref,
    grads_ref,
    gate_ref,
    expert_gate_ref,
    expert_up_ref,
    expert_down_ref,
    act_ref,
    gate_delta_ref,
    up_delta_ref,
    score_ref,
):
    rows = rows_ref[0]
    gate_h = dot_nt(rows, expert_gate_ref[0])
    up_h = dot_nt(rows, expert_up_ref[0])
    dact = dot_nt(grads_ref[0], expert_down_ref[0])
    gate = gate_ref[0][:, :1]
    act, gate_delta, up_delta = gated(gate_h, up_h, dact)
    act_ref[0] = (act * gate).astype(bf16)
    gate_delta_ref[0] = (gate_delta * gate).astype(bf16)
    up_delta_ref[0] = (up_delta * gate).astype(bf16)
    score = jnp.sum(act * dact, axis=1, keepdims=True)
    high = score.astype(bf16).astype(f32)
    lanes = score_ref.shape[2]
    lane = lax.broadcasted_iota(jnp.int32, (rows.shape[0], lanes), 1)
    mine = first_ref[0] + pl.program_id(0)
    score_ref[0] = jnp.where(
        lane == mine, high, jnp.where(lane == mine + lanes // 2, score - high, 0.0)
    ).astype(bf16)


def return_kernel(spec, slots_ref, *refs):
    pairs, scored, added, outputs, steps = spec
    deltas, weights = refs[:pairs], refs[pairs : 2 * pairs]
    shared_ref, shared_weight_ref = refs[2 * pairs : 2 * pairs + 2]
    rest = refs[2 * pairs + 2 :]
    score_ref, rest = (rest[0], rest[1:]) if scored else (None, rest)
    other_ref, rest = (rest[0], rest[1:]) if added else (None, rest)
    outs, picks, rows = rest[:outputs], rest[outputs], rest[outputs + 1]
    sources, _, chunk = rows.shape
    experts = slots_ref.shape[1]
    toks = picks.shape[2]
    step = pl.program_id(0)

    def store(s, columns, value):
        if added:
            value = value + other_ref[s, :, columns].astype(f32)
        out = outs[s // (sources // outputs)]
        out[s % (sources // outputs), :, columns] = value.astype(bf16)

    @pl.when(step == 0)
    def _():
        for s in range(sources):
            picks[s] = pick_matrix(slots_ref[s])
        if scored:
            for s in range(sources):
                score = jnp.concatenate(
                    [score_ref[e, s * CAP : (s + 1) * CAP] for e in range(experts)], axis=0
                )
                store(s, pl.ds(steps * chunk, score.shape[1]), dot_tn(picks[s], score))

    for e in range(experts):
        back = functools.reduce(
            jnp.add, [dot(d[e], w[e]) for d, w in zip(deltas, weights)]
        ).astype(bf16)
        for s in range(sources):
            rows[s, e * CAP : (e + 1) * CAP, :] = back[s * CAP : (s + 1) * CAP]
    columns = pl.ds(pl.multiple_of(step * chunk, chunk), chunk)
    for s in range(sources):
        summed = dot_tn(picks[s], rows[s]) + dot(
            shared_ref[s * toks : (s + 1) * toks], shared_weight_ref[...]
        )
        store(s, columns, summed)


def expert_grad_kernel(
    rows_ref,
    grads_ref,
    act_ref,
    gate_delta_ref,
    up_delta_ref,
    gate_grad_ref,
    up_grad_ref,
    down_grad_ref,
):
    rows = rows_ref[0]
    gate_grad_ref[0] = dot_tn(gate_delta_ref[0], rows)
    up_grad_ref[0] = dot_tn(up_delta_ref[0], rows)
    down_grad_ref[0] = dot_tn(act_ref[0], grads_ref[0])


def shared_grad_kernel(count, parts, src_ref, tensor_ref, delta_ref, act_ref, grad_ref, *refs):
    out_ref, buffer, placed, in_acc, down_acc, sems = refs[count:]
    step = pl.program_id(0)
    block = fetch(refs[:count], buffer, sems)
    rows = placed.shape[0] // parts
    for r, part in enumerate(by_place(grad_ref.at[0], tensor_ref[0], parts)):
        placed[r * rows : (r + 1) * rows] = part

    @pl.when(step == 0)
    def _():
        in_acc[...] = jnp.zeros_like(in_acc)
        down_acc[...] = jnp.zeros_like(down_acc)

    in_acc[...] += dot_tn(delta_ref[...], block[...])
    down_acc[...] += dot_tn(act_ref[...], placed[...])

    @pl.when(step == count - 1)
    def _():
        devices, rows, columns = out_ref.shape
        rows //= 3
        middle = in_acc.shape[0] // 2
        for j in range(devices):
            here = slice(j * columns, (j + 1) * columns)
            out_ref[j, :rows] = in_acc[:rows, here].astype(bf16)
            out_ref[j, rows : 2 * rows] = in_acc[middle : middle + rows, here].astype(bf16)
            out_ref[j, 2 * rows :] = down_acc[:rows, here].astype(bf16)


def rows_grad_kernel(src_ref, left_ref, right_ref, far_ref, near_ref):
    half, rows, _ = far_ref.shape
    for i in range(2 * half):
        start = pl.multiple_of(src_ref[i] * rows, rows)
        product = dot_tn(left_ref[:, pl.ds(start, rows)], right_ref[...]).astype(bf16)
        if i < half:
            far_ref[i] = product
        else:
            near_ref[i - half] = product


def columns_grad_kernel(parts, flat, src_ref, left_ref, logits_ref, block_ref, gain_ref, *refs):
    far_ref, near_ref, grads = refs[parts:]
    rows = left_ref.shape[0] // parts
    for r in range(parts):
        grads[r * rows : (r + 1) * rows] = refs[r][:rows]
    half, height, width = far_ref.shape
    wide, experts_all = left_ref.shape[1], logits_ref.shape[1]
    for i in range(2 * half):
        columns = pl.ds(pl.multiple_of(src_ref[i] * width, width), width)
        out = far_ref.at[i] if i < half else near_ref.at[i - half]
        out[:wide] = dot_tn(left_ref[...], grads[:, columns]).astype(bf16)
        router = dot_tn(logits_ref[...], block_ref[:, columns])
        rest = jnp.concatenate(
            [router, jnp.broadcast_to(gain_ref[:, columns], (height - wide - experts_all, width))],
            axis=0,
        )
        out[wide:] = rest.astype(bf16)


def normed_kernel(tokens_ref, gain_ref, down_ref, rope_ref, normed_ref, inv_ref, narrow_ref):
    normed, inv = rms_norm(tokens_ref[...].astype(f32), gain_ref[...])
    normed = normed.astype(bf16)
    normed_ref[...] = normed
    inv_ref[...] = inv
    cols = down_ref.shape[1]
    narrow_ref[:, :cols] = dot(normed, down_ref[...]).astype(bf16)
    narrow_ref[:, cols:] = dot_nt(normed, rope_ref[...]).astype(bf16)


def query_kernel(normed_ref, weight_ref, cosines_ref, sines_ref, query_ref):
    raw = dot(normed_ref[...], weight_ref[...])
    toks = raw.shape[0]
    for h in range(raw.shape[1] // (HD + RD)):
        start = h * (HD + RD)
        rope = jnp.concatenate(
            [raw[:, start + HD : start + HD + RD], jnp.zeros((toks, LANES - RD), f32)], axis=1
        )
        query_ref[:, h * HEAD : h * HEAD + HD] = raw[:, start : start + HD].astype(bf16)
        query_ref[:, h * HEAD + HD : (h + 1) * HEAD] = rotate(
            rope, cosines_ref[...], sines_ref[...]
        ).astype(bf16)


def causal(scores):
    later = lax.broadcasted_iota(jnp.int32, scores.shape, 1) > lax.broadcasted_iota(
        jnp.int32, scores.shape, 0
    )
    return jnp.where(later, -1e30, scores)


def attention_kernel(
    parts,
    tensor_ref,
    query_ref,
    cosines_ref,
    sines_ref,
    place_ref,
    gain_ref,
    up_ref,
    out_weight_ref,
    *refs,
):
    narrow = [ref[...] for ref in refs[:parts]]
    sums = refs[parts : 2 * parts]
    attended_ref, latent_ref, latent_normed_ref, inv_ref, kv_ref, rope_ref, lse_ref, natural = refs[
        2 * parts :
    ]
    toks = query_ref.shape[0]
    heads = query_ref.shape[1] // HEAD
    cols = up_ref.shape[0] // parts
    latent = jnp.concatenate([n[:, :cols] for n in narrow], axis=1)
    latent_ref[...] = latent
    normed, inv = rms_norm(latent.astype(f32), gain_ref[...])
    normed = normed.astype(bf16)
    latent_normed_ref[...] = normed
    inv_ref[...] = inv
    rope = dot(jnp.concatenate([n[:, cols:] for n in narrow], axis=1), place_ref[...])
    rope = rotate(rope, cosines_ref[...], sines_ref[...]).astype(bf16)
    rope_ref[...] = rope
    kv_ref[...] = dot(normed, up_ref[...]).astype(bf16)
    lane = lax.broadcasted_iota(jnp.int32, (toks, LANES), 1)
    lses = jnp.zeros((toks, LANES), f32)
    for h in range(heads):
        key = jnp.concatenate([kv_ref[:, h * KV : h * KV + HD], rope], axis=1)
        scores = causal(dot_nt(query_ref[:, h * HEAD : (h + 1) * HEAD], key) * (HD + RD) ** -0.5)
        top = jnp.max(scores, axis=1, keepdims=True)
        lse = top + jnp.log(jnp.sum(jnp.exp(scores - top), axis=1, keepdims=True))
        lses = jnp.where(lane == h, lse, lses)
        weights = jnp.exp(scores - lse).astype(bf16)
        natural[:, h * VD : (h + 1) * VD] = dot(
            weights, kv_ref[:, h * KV + HD : (h + 1) * KV]
        ).astype(bf16)
    lse_ref[...] = lses
    rows = toks // parts
    for r, block in enumerate(by_place(natural, tensor_ref[0], parts)):
        attended_ref[r * rows : (r + 1) * rows] = block
    for r in range(parts):
        product = dot(attended_ref[r * rows : (r + 1) * rows], out_weight_ref[...])
        sums[r][...] = product.astype(sums[r].dtype)


def attention_back_kernel(
    parts,
    tensor_ref,
    src_ref,
    query_ref,
    kv_ref,
    rope_ref,
    lse_ref,
    latent_ref,
    latent_normed_ref,
    inv_ref,
    cosines_ref,
    sines_ref,
    place_ref,
    gain_ref,
    up_ref,
    out_weight_ref,
    *refs,
):
    grads = refs[:parts]
    narrow = refs[parts : 2 * parts]
    query_grad_ref, up_far_ref, up_near_ref, natural, query_nat, kv_grad, narrow_nat, up_part = refs[
        2 * parts :
    ]
    toks = query_ref.shape[0]
    heads = query_ref.shape[1] // HEAD
    rows = toks // parts
    factor = (HD + RD) ** -0.5
    tensor = tensor_ref[0]
    for r in range(parts):
        place = pl.ds(pl.multiple_of((tensor ^ r) * rows, rows), rows)
        natural[place, :] = dot_nt(grads[r][:rows], out_weight_ref[...]).astype(bf16)
    rope = rope_ref[...]
    rope_sum = jnp.zeros((toks, LANES), f32)
    for h in range(heads):
        grad = natural[:, h * VD : (h + 1) * VD]
        query = query_ref[:, h * HEAD : (h + 1) * HEAD]
        key = jnp.concatenate([kv_ref[:, h * KV : h * KV + HD], rope], axis=1)
        scores = causal(dot_nt(query, key) * factor)
        probs = jnp.exp(scores - lse_ref[:, h : h + 1])
        kv_grad[:, h * KV + HD : (h + 1) * KV] = dot_tn(probs.astype(bf16), grad).astype(bf16)
        prob_dot = dot_nt(grad, kv_ref[:, h * KV + HD : (h + 1) * KV])
        inner = jnp.sum(probs * prob_dot, axis=1, keepdims=True)
        score_grad = (probs * (prob_dot - inner) * factor).astype(bf16)
        query_grad = dot(score_grad, key)
        start = h * (HD + RD)
        query_nat[:, start : start + HD] = query_grad[:, :HD].astype(bf16)
        query_nat[:, start + HD : start + HD + RD] = rotate(
            query_grad[:, HD:], cosines_ref[...], -sines_ref[...]
        )[:, :RD].astype(bf16)
        key_grad = dot_tn(score_grad, query)
        kv_grad[:, h * KV : h * KV + HD] = key_grad[:, :HD].astype(bf16)
        rope_sum = rope_sum + key_grad[:, HD:]
    for r, block in enumerate(by_place(query_nat, tensor, parts)):
        query_grad_ref[r * rows : (r + 1) * rows] = block
    latent_grad, _ = rms_back(
        dot_nt(kv_grad[...], up_ref[...]), latent_ref[...].astype(f32), inv_ref[...], gain_ref[...]
    )
    rope_sum = rotate(rope_sum, cosines_ref[...], -sines_ref[...]).astype(bf16)
    rope_sum = dot_nt(rope_sum, place_ref[...])
    cols = latent_grad.shape[1] // parts
    rope_cols = rope_sum.shape[1] // parts
    for k in range(parts):
        narrow_nat[:, :cols] = latent_grad[:, k * cols : (k + 1) * cols]
        narrow_nat[:, cols:] = rope_sum[:, k * rope_cols : (k + 1) * rope_cols]
        narrow[k][...] = narrow_nat[...].astype(narrow[k].dtype)
    up_part[...] = dot_tn(latent_normed_ref[...], kv_grad[...])
    half, up_rows, _ = up_far_ref.shape
    for i in range(2 * half):
        start = src_ref[i] * up_rows
        start = (start // cols ^ tensor) * cols + start % cols
        block = up_part[pl.ds(pl.multiple_of(start, up_rows), up_rows), :].astype(bf16)
        if i < half:
            up_far_ref[i] = block
        else:
            up_near_ref[i - half] = block


def normed_back_kernel(parts, tensor_ref, query_grad_ref, query_weight_ref, down_ref, rope_ref, *refs):
    narrow = refs[:parts]
    sums = refs[parts : 2 * parts]
    all_ref, natural = refs[2 * parts :]
    cols = down_ref.shape[1]
    natural[...] = total([ref[...] for ref in narrow])
    mine = jnp.concatenate(by_place(natural, tensor_ref[0], parts), axis=0).astype(bf16)
    all_ref[...] = mine
    rows = query_grad_ref.shape[0] // parts
    product = (
        dot_nt(query_grad_ref[...], query_weight_ref[...])
        + dot_nt(mine[:, :cols], down_ref[...])
        + dot(mine[:, cols:], rope_ref[...])
    )
    for r in range(parts):
        sums[r][...] = product[r * rows : (r + 1) * rows].astype(sums[r].dtype)


ANYWHERE = pl.BlockSpec(memory_space=pl.ANY)


def whole(array):
    rank = len(array.shape)
    return pl.BlockSpec(array.shape, lambda *_: (0,) * rank)


def params(mib):
    return pltpu.CompilerParams(vmem_limit_bytes=mib * MIB)


def cost(flops, bytes_accessed, transcendentals=0):
    return pl.CostEstimate(
        flops=int(flops), bytes_accessed=int(bytes_accessed), transcendentals=int(transcendentals)
    )


def pick_grads(src, tensor, parts, slots, grads, shared_down):
    count, experts, toks = slots.shape
    width = grads.shape[2]
    shared = shared_down.shape[0]
    return pl.pallas_call(
        functools.partial(pick_grad_kernel, parts),
        grid_spec=pltpu.PrefetchScalarGridSpec(
            num_scalar_prefetch=2,
            grid=(count,),
            in_specs=[
                pl.BlockSpec((1, experts, toks), lambda s, src, t: (s, 0, 0)),
                pl.BlockSpec((1, toks, width), lambda s, src, t: (src[s], 0, 0)),
                whole(shared_down),
            ],
            out_specs=[
                pl.BlockSpec((experts, CAP, width), lambda s, src, t: (0, s, 0)),
                pl.BlockSpec((toks, shared), lambda s, src, t: (s, 0)),
            ],
            scratch_shapes=[pltpu.VMEM((toks, width), bf16)],
        ),
        out_shape=[
            jax.ShapeDtypeStruct((experts, count * CAP, width), bf16),
            jax.ShapeDtypeStruct((count * toks, shared), f32),
        ],
        compiler_params=params(VMEM),
        cost_estimate=cost(
            2 * count * toks * width * (experts * CAP + shared), 4 * count * toks * width
        ),
    )(src, tensor, slots, grads, shared_down)


def pick_rows(blocks, places, slots, router, weights, dact, experts_all, results):
    count = len(blocks)
    run = next(i for i in range(1, count) if places[i] != places[i - 1] + 1)
    first, skip = places[0], places[run] - places[0] - run

    def place(s):
        return s + first + jnp.where(s < run, 0, skip)

    every, experts, toks = slots.shape
    width = blocks[0].shape[1]
    shared = dact.shape[1]
    operands = [slots, router, weights, dact, *blocks, *results]
    return pl.pallas_call(
        functools.partial(pick_kernel, count, experts_all, len(results)),
        grid=(count,),
        in_specs=[
            pl.BlockSpec((1, experts, toks), lambda s: (place(s), 0, 0)),
            whole(router),
            whole(weights),
            pl.BlockSpec((toks, shared), lambda s: (place(s), 0)),
        ]
        + [ANYWHERE] * (count + len(results)),
        out_specs=[
            pl.BlockSpec((experts, CAP, width), lambda s: (0, place(s), 0)),
            pl.BlockSpec((experts, CAP, LANES), lambda s: (0, place(s), 0)),
            pl.BlockSpec((toks, shared), lambda s: (place(s), 0)),
            pl.BlockSpec((toks, 2 * shared), lambda s: (place(s), 0)),
        ],
        out_shape=[
            shape(bf16, experts, every * CAP, width),
            shape(f32, experts, every * CAP, LANES),
            shape(bf16, every * toks, shared),
            shape(bf16, every * toks, 2 * shared),
        ],
        input_output_aliases={len(operands) - len(results) + i: i for i in range(len(results))},
        scratch_shapes=[
            pltpu.VMEM((count, toks, width), bf16),
            pltpu.SemaphoreType.DMA((count,)),
        ],
        compiler_params=params(VMEM),
        cost_estimate=cost(
            2 * count * toks * width * (experts * CAP + router.shape[0] + 2 * shared),
            4 * count * toks * width,
        ),
    )(*operands)


def expert_hidden(first, rows, grads, gate, expert_gate, expert_up, expert_down, lanes):
    experts, slot_rows, width = rows.shape
    hidden = expert_gate.shape[1]

    def per_expert(array):
        return pl.BlockSpec((1,) + array.shape[1:], lambda e: (e, 0, 0))

    narrow = jax.ShapeDtypeStruct((experts, slot_rows, hidden), bf16)
    score = jax.ShapeDtypeStruct((experts, slot_rows, lanes), bf16)
    return pl.pallas_call(
        hidden_kernel,
        grid=(experts,),
        in_specs=[pl.BlockSpec(memory_space=pltpu.SMEM)]
        + [per_expert(a) for a in (rows, grads, gate, expert_gate, expert_up, expert_down)],
        out_specs=[per_expert(narrow)] * 3 + [per_expert(score)],
        out_shape=[narrow] * 3 + [score],
        compiler_params=params(VMEM),
        cost_estimate=cost(
            6 * experts * slot_rows * width * hidden,
            experts * (4 * slot_rows * width + 6 * hidden * width),
            experts * slot_rows * hidden,
        ),
    )(first, rows, grads, gate, expert_gate, expert_up, expert_down)


def return_rows(half, slots, deltas, weights, shared, shared_weight, score, start, size, other):
    experts, slot_rows, hidden = deltas[0].shape
    sources = slots.shape[0] // 2
    toks = slots.shape[2]
    chunk = min(512, size)
    steps = size // chunk
    first = start // chunk
    outputs = 1 + half
    lanes = 0 if score is None else score.shape[2]
    in_specs = (
        [pl.BlockSpec((sources,) + slots.shape[1:], lambda n: (half, 0, 0))]
        + [pl.BlockSpec((experts, slot_rows // 2, hidden), lambda n: (0, half, 0))] * len(deltas)
        + [pl.BlockSpec((experts, hidden, chunk), lambda n: (0, 0, n + first))] * len(weights)
        + [
            pl.BlockSpec((sources * toks, shared.shape[1]), lambda n: (half, 0)),
            pl.BlockSpec((shared.shape[1], chunk), lambda n: (0, n + first)),
        ]
    )
    operands = [slots, *deltas, *weights, shared, shared_weight]
    if score is not None:
        in_specs.append(pl.BlockSpec((experts, slot_rows // 2, lanes), lambda n: (0, half, 0)))
        operands.append(score)
    if other is not None:
        in_specs.append(whole(other))
        operands.append(other)
    out = jax.ShapeDtypeStruct((sources // outputs, toks, size + lanes), bf16)
    return pl.pallas_call(
        functools.partial(
            return_kernel, (len(deltas), score is not None, other is not None, outputs, steps)
        ),
        grid=(steps,),
        in_specs=in_specs,
        out_specs=[whole(out)] * outputs,
        out_shape=[out] * outputs,
        scratch_shapes=[
            pltpu.VMEM((sources, experts * CAP, toks), bf16),
            pltpu.VMEM((sources, experts * CAP, chunk), bf16),
        ],
        compiler_params=params(VMEM),
        cost_estimate=cost(
            2 * experts * slot_rows // 2 * size * (hidden * len(deltas) + toks)
            + 2 * sources * toks * size * shared.shape[1],
            2 * size * (experts * hidden * len(deltas) + sources * toks),
        ),
    )(*operands)


def expert_grads(rows, grads, act, gate_delta, up_delta):
    experts, slot_rows, width = rows.shape
    hidden = act.shape[2]

    def per_expert(array):
        return pl.BlockSpec((1,) + array.shape[1:], lambda e: (e, 0, 0))

    out = jax.ShapeDtypeStruct((experts, hidden, width), f32)
    return pl.pallas_call(
        expert_grad_kernel,
        grid=(experts,),
        in_specs=[per_expert(a) for a in (rows, grads, act, gate_delta, up_delta)],
        out_specs=[per_expert(out)] * 3,
        out_shape=[out] * 3,
        compiler_params=params(VMEM),
        cost_estimate=cost(
            6 * experts * slot_rows * width * hidden,
            experts * (4 * slot_rows * width + 12 * hidden * width),
        ),
    )(rows, grads, act, gate_delta, up_delta)


def shared_grads(src, tensor, parts, blocks, grads, delta, act, cols):
    count = grads.shape[0]
    toks, width = blocks[0].shape
    out = jax.ShapeDtypeStruct((count, 3 * cols, width // count), bf16)
    return pl.pallas_call(
        functools.partial(shared_grad_kernel, count, parts),
        grid_spec=pltpu.PrefetchScalarGridSpec(
            num_scalar_prefetch=2,
            grid=(count,),
            in_specs=[
                pl.BlockSpec((toks, delta.shape[1]), lambda s, src, t: (s, 0)),
                pl.BlockSpec((toks, act.shape[1]), lambda s, src, t: (s, 0)),
                pl.BlockSpec((1, toks, width), lambda s, src, t: (src[s], 0, 0)),
            ]
            + [ANYWHERE] * count,
            out_specs=whole(out),
            scratch_shapes=[
                pltpu.VMEM((count, toks, width), bf16),
                pltpu.VMEM((toks, width), bf16),
                pltpu.VMEM((delta.shape[1], width), f32),
                pltpu.VMEM((act.shape[1], width), f32),
                pltpu.SemaphoreType.DMA((count,)),
            ],
        ),
        out_shape=out,
        compiler_params=params(VMEM),
        cost_estimate=cost(
            2 * count * toks * width * (delta.shape[1] + act.shape[1]), 4 * count * toks * width
        ),
    )(src, tensor, delta, act, grads, *blocks)


def single(kernel, outs, operands, scalars=(), scratch=(), flops=0, transcendentals=0):
    return pl.pallas_call(
        kernel,
        grid_spec=pltpu.PrefetchScalarGridSpec(
            num_scalar_prefetch=len(scalars),
            grid=(1,),
            in_specs=[whole(a) for a in operands],
            out_specs=[whole(o) for o in outs],
            scratch_shapes=list(scratch),
        ),
        out_shape=list(outs),
        compiler_params=params(VMEM),
        cost_estimate=cost(flops, sum(a.size * a.dtype.itemsize for a in operands), transcendentals),
    )(*scalars, *operands)


def shape(dtype, *sizes):
    return jax.ShapeDtypeStruct(sizes, dtype)


def on_device(
    tokens,
    cotangent,
    attn_gain,
    q_weight,
    kv_down,
    k_rope_weight,
    kv_gain,
    kv_up,
    o_weight,
    ffn_gain,
    router_weight,
    expert_ids,
    expert_gate,
    expert_up,
    expert_down,
    shared_gate,
    shared_up,
    shared_down,
):
    n_t = lax.axis_size("tensor")
    n_d = lax.axis_size("dp")
    half = n_d // 2
    t_index = lax.axis_index("tensor")
    d_index = lax.axis_index("dp")
    toks, width = tokens.shape
    own_toks = toks // n_t
    rows_d = width // n_d
    q_cols = q_weight.shape[1]
    heads = q_cols // (HD + RD)
    experts_all = router_weight.shape[1]
    experts = expert_gate.shape[0]
    cosines, sines = rope_tables()
    order = partner_order()
    src = d_index.astype(jnp.int32) ^ order
    sources = [src[i] for i in range(n_d)]
    lat_cols = kv_down.shape[1]
    lat_rank = kv_up.shape[0]
    rope_cols = k_rope_weight.shape[1]
    narrow_cols = lat_cols + rope_cols
    expert_gate_t = expert_gate.transpose(0, 2, 1)
    expert_up_t = expert_up.transpose(0, 2, 1)

    tokens_p = by_partner(tokens, "tensor", 0)
    tokens_own = tokens_p[0].astype(f32)
    cot_own = block_at(cotangent, t_index, own_toks, 0).astype(f32)
    tensor = t_index.astype(jnp.int32).reshape(1)
    every = jnp.arange(experts_all, dtype=jnp.int32)
    member = jnp.any(expert_ids.T[:, None, :] == every[None, :, None], axis=0)
    before = (jnp.arange(toks)[:, None] < jnp.arange(toks)[None, :]).astype(bf16)
    rank = dot(member.astype(bf16), before)
    slots_own = jnp.where(member, rank, -1.0).astype(bf16).reshape(-1, width)
    slot_rows = slots_own.shape[0]
    slots_own = jnp.pad(slots_own, ((0, -slot_rows % 16), (0, 0)))
    cot_all = lax.all_gather(jnp.concatenate([cotangent, slots_own], axis=0), "dp")
    slots = cot_all[:, toks : toks + slot_rows].reshape(n_d, experts_all, toks)
    slots = reorder(block_at(slots, d_index, experts, 1), "tensor", 2)
    slots = jnp.concatenate([block_at(slots, s, 1, 0) for s in sources], axis=0).astype(jnp.int32)
    router_t = jnp.roll(router_weight.T, -d_index * experts, axis=0)
    router_parts = []
    rest = router_t
    for _ in range(3):
        part = lax.reduce_precision(rest, 8, 7)
        router_parts.append(part.astype(bf16))
        rest = rest - part
    router_parts = jnp.concatenate(router_parts, axis=0)
    shared_cols = shared_down.shape[0] // n_d
    shared_pad = -shared_cols % LANES
    shared_gate_t, shared_up_t, shared_out = [
        jnp.pad(block_at(w, d_index, shared_cols, 0), ((0, shared_pad), (0, 0)))
        for w in (shared_gate.T, shared_up.T, shared_down)
    ]
    shared_in = jnp.concatenate([shared_gate_t, shared_up_t], axis=0)
    grad_rows, shared_dact = pick_grads(src, tensor, n_t, slots, cot_all, shared_out)

    kv_up_p = reorder(kv_up, "tensor", 0)
    kv_gain_p = reorder(kv_gain, "tensor", 0)[None]
    rope_t = k_rope_weight.T
    rope_place = (
        (t_index ^ jnp.arange(n_t)[:, None, None]) * rope_cols + jnp.arange(rope_cols)[None, :, None]
        == jnp.arange(LANES)
    ).astype(bf16).reshape(RD, LANES)
    normed, inv_first, narrow_own = single(
        normed_kernel,
        [shape(bf16, toks, width), shape(f32, toks, 1), shape(bf16, toks, narrow_cols)],
        [tokens, attn_gain[None], kv_down, rope_t],
        flops=2 * toks * width * narrow_cols,
    )
    narrow_blocks = share(narrow_own, "tensor")
    query = single(
        query_kernel,
        [shape(bf16, toks, heads * HEAD)],
        [normed, q_weight, cosines, sines],
        flops=2 * toks * width * q_cols,
    )[0]
    results = single(
        functools.partial(attention_kernel, n_t),
        [shape(f32 if r == 0 else bf16, own_toks, width) for r in range(n_t)]
        + [
            shape(bf16, toks, heads * VD),
            shape(bf16, toks, lat_rank),
            shape(bf16, toks, lat_rank),
            shape(f32, toks, 1),
            shape(bf16, toks, heads * KV),
            shape(bf16, toks, LANES),
            shape(f32, toks, LANES),
        ],
        [query, cosines, sines, rope_place, kv_gain_p, kv_up_p, o_weight, *narrow_blocks],
        scalars=[tensor],
        scratch=[pltpu.VMEM((toks, heads * VD), bf16)],
        flops=2 * toks * heads * (KV * lat_rank + 2 * HEAD * toks + VD * width),
        transcendentals=2 * heads * toks * toks,
    )
    attn_part = results[:n_t]
    attended_p, latent, latent_normed, inv_latent, key_value, rope_rot, lse = results[n_t:]
    attn_sum = total(
        after(trade(attn_part, "tensor"), router_parts, shared_in, shared_out, inv_first, kv_up_p)
    )
    hidden_one = tokens_own + attn_sum
    ffn_normed_f, inv_second = rms_norm(hidden_one, ffn_gain)
    ffn_own = ffn_normed_f.astype(bf16)
    ffn_block = jnp.concatenate(share_far_first(ffn_own, "tensor"), axis=0)
    near_blocks = gather_chips(ffn_block, grad_rows)
    far_blocks = [swap(block, "dp", 1) for block in near_blocks[:-1]]

    def pick(places, blocks_here, results):
        return pick_rows(
            blocks_here, places, slots, router_parts, shared_in, shared_dact, experts_all, results
        )

    early = [0] + list(range(half, n_d - 1))
    results = pick(early, far_blocks[:1] + near_blocks[:-1], [])
    far_blocks.append(swap(after(near_blocks[-1], results), "dp", 1))
    late = list(range(1, half)) + [n_d - 1]
    blocks = far_blocks + near_blocks

    results = pick(late, [blocks[i] for i in late], results)
    rows, gate, shared_act, shared_delta = results
    lanes = -(-2 * experts_all // LANES) * LANES
    first = (d_index * experts).astype(jnp.int32).reshape(1)
    act, gate_delta, up_delta, score = expert_hidden(
        first, rows, grad_rows, gate, expert_gate_t, expert_up_t, expert_down, lanes
    )

    def send_back(sum_here):
        return trade(
            [sum_here[k * own_toks : (k + 1) * own_toks].astype(bf16) for k in range(n_t)], "tensor"
        )

    pieces = 2
    size = width // pieces
    deltas, delta_weights = [gate_delta, up_delta], [expert_gate_t, expert_up_t]
    others = [
        return_rows(
            0, slots, deltas, delta_weights, shared_delta, shared_in,
            score if i == pieces - 1 else None, i * size, size, None,
        )[0]
        for i in range(pieces)
    ]
    others = [swap(other, "dp", 1) for other in others]
    mine = [
        return_rows(
            1, slots, deltas, delta_weights, shared_delta, shared_in,
            score if i == pieces - 1 else None, i * size, size, others[i],
        )
        for i in range(pieces)
    ]
    out_other = []

    def beside(step, arrived):
        if step:
            return arrived
        out_other.extend(
            return_rows(
                0, slots, [after(act, arrived[0], mine[1:])], [expert_down], shared_act, shared_out,
                None, 0, width, None,
            )
        )
        return arrived[:1] + after(arrived[1:], out_other)

    sums, arrivals = sum_chips(mine, beside)
    out_pair = return_rows(
        1, slots, [act], [expert_down], shared_act, shared_out, None, 0, width,
        after(swap(out_other[0], "dp", 1), arrivals[0]),
    )
    shared_rows = shared_cols + -shared_cols % 16
    back_sums = [total(send_back(s)) for s in sums]
    back_sum = jnp.concatenate(back_sums[:-1] + [back_sums[-1][:, :size]], axis=1)
    score_sum = back_sums[-1][:, size:]
    logits = jnp.dot(ffn_own.astype(f32), router_weight, precision=lax.Precision.HIGHEST)
    router_prob = jax.nn.softmax(logits, axis=-1)
    prob_grad = score_sum[:, :experts_all] + score_sum[:, lanes // 2 : lanes // 2 + experts_all]
    logit_grad = (
        router_prob * (prob_grad - jnp.sum(router_prob * prob_grad, axis=-1, keepdims=True))
    ).astype(bf16)
    ffn_normed_grad = back_sum + jnp.dot(
        logit_grad.astype(f32), router_weight.T, precision=lax.Precision.HIGHEST
    )
    hidden_norm_grad, ffn_gain_part = rms_back(ffn_normed_grad, hidden_one, inv_second, ffn_gain)
    hidden_grad = cot_own + hidden_norm_grad
    flat_logits = logit_grad.reshape(-1, width)
    flat = flat_logits.shape[0]
    extra = jnp.concatenate(
        [
            flat_logits,
            ffn_gain_part.astype(bf16)[None],
            jnp.zeros((-(flat + 1) % 8, width), bf16),
        ],
        axis=0,
    )
    message = jnp.concatenate([hidden_grad.astype(bf16), extra], axis=0)
    message = after(message, out_pair)
    shared_grads_t = share(message, "tensor")
    expert_gate_grad, expert_up_grad, expert_down_grad = expert_grads(
        rows, grad_rows, *after((act, gate_delta, up_delta), message)
    )
    out_sums, out_steps = sum_chips([out_pair], lambda step, arrived: after(arrived, expert_gate_grad))
    out_here = out_sums[0]
    shared_grads_t = after(shared_grads_t, expert_gate_grad, out_steps[1])

    lat_rows = lat_rank // n_d
    results = single(
        functools.partial(attention_back_kernel, n_t),
        [shape(f32 if r == 0 else bf16, toks, narrow_cols) for r in range(n_t)]
        + [
            shape(bf16, toks, q_cols),
            shape(bf16, half, lat_rows, heads * KV),
            shape(bf16, half, lat_rows, heads * KV),
        ],
        [
            query, key_value, rope_rot, lse, latent, latent_normed, inv_latent, cosines, sines,
            rope_place, kv_gain_p, kv_up_p, o_weight, *shared_grads_t,
        ],
        scalars=[tensor, src],
        scratch=[
            pltpu.VMEM((toks, heads * VD), bf16),
            pltpu.VMEM((toks, q_cols), bf16),
            pltpu.VMEM((toks, heads * KV), bf16),
            pltpu.VMEM((toks, narrow_cols), f32),
            pltpu.VMEM((lat_rank, heads * KV), f32),
        ],
        flops=2 * toks * heads * (2 * KV * lat_rank + 5 * HEAD * toks + VD * width),
        transcendentals=heads * toks * toks,
    )
    latent_parts = results[:n_t]
    query_grad_p, kv_up_far, kv_up_near = results[n_t:]
    normed_p = reorder(normed, "tensor", 0)

    def rows_grad(left, right):
        return single(
            rows_grad_kernel,
            [shape(bf16, half, rows_d, right.shape[1])] * 2,
            [left, right],
            scalars=[src],
            flops=2 * toks * width * right.shape[1],
        )

    logit_p = jnp.concatenate(
        [b[own_toks : own_toks + flat].reshape(own_toks, experts_all) for b in shared_grads_t], axis=0
    )
    gain_part = total([b[own_toks + flat] for b in shared_grads_t])[None]
    out_cols = attended_p.shape[1]
    height = out_cols + experts_all + 16
    column_terms = single(
        functools.partial(columns_grad_kernel, n_t, flat),
        [shape(bf16, half, height, rows_d)] * 2,
        [after(attended_p, query_grad_p), logit_p, ffn_block, gain_part, *shared_grads_t],
        scalars=[src],
        scratch=[pltpu.VMEM((toks, width), bf16)],
        flops=2 * toks * width * height,
    )
    query_terms = rows_grad(after(normed_p, out_steps[2]), query_grad_p)
    terms = [query_terms, column_terms, (kv_up_far, kv_up_near)]
    out_rows = {r: out_here[r * own_toks : (r + 1) * own_toks] for r in range(n_t)}
    out_sent = swap(
        jnp.concatenate([out_rows[r].astype(bf16) for r in out_rows if r & 1], axis=0), "tensor", 1
    )
    latent_parts = after(trade(latent_parts, "tensor"), terms)
    results = single(
        functools.partial(normed_back_kernel, n_t),
        [shape(f32 if r == 0 else bf16, own_toks, width) for r in range(n_t)]
        + [shape(bf16, toks, narrow_cols)],
        [query_grad_p, q_weight, kv_down, rope_t, *latent_parts],
        scalars=[tensor],
        scratch=[pltpu.VMEM((toks, narrow_cols), f32)],
        flops=2 * toks * width * (q_cols + narrow_cols),
    )
    normed_part, narrow_p = results[:n_t], results[n_t]
    query_pairs = sum_cores(after(terms[:1], normed_part))
    shared_all = shared_grads(
        src, tensor, n_t, blocks, cot_all, *after((shared_delta, shared_act), out_sent, query_pairs[0][1]), shared_rows
    )
    shared_sent = lax.all_to_all(shared_all, "dp", 0, 0, tiled=True).astype(f32)
    shared_gate_grad, shared_up_grad, shared_down_grad = [
        shared_sent[:, i * shared_rows : i * shared_rows + shared_cols].reshape(-1, rows_d)
        for i in range(3)
    ]
    (q_weight_grad,), term_arrivals = sum_chips(query_pairs)
    terms = terms[1:] + [rows_grad(normed_p, narrow_p)]
    (columns, kv_up_grad, narrow_grad), _ = sum_chips(sum_cores(after(terms, query_pairs[0][1])))
    normed_arrived = after(trade(normed_part, "tensor"), term_arrivals[0], shared_all)
    normed_grad = total(normed_arrived)
    out_sum = sum_along(out_rows, after(out_sent, normed_arrived[1:]), "tensor")
    output_own = (hidden_one + out_sum).astype(bf16)
    output = reorder(jnp.concatenate(share_far_first(output_own, "tensor"), axis=0), "tensor", 0)
    inv_first_own = block_at(inv_first, t_index, own_toks, 0)
    input_norm_grad, _ = rms_back(normed_grad, tokens_own, inv_first_own, attn_gain)
    input_grad = hidden_grad + input_norm_grad

    o_weight_grad = columns[:out_cols]
    device_rows = width // (n_d * n_t)
    router_grad = block_at(
        columns[out_cols : out_cols + experts_all], t_index, device_rows, 1
    ).T
    ffn_gain_grad = block_at(columns[out_cols + experts_all], t_index, device_rows, 0)
    kv_down_grad = narrow_grad[:, :lat_cols]
    k_rope_grad = narrow_grad[:, lat_cols:]

    attn_gain_part = jnp.sum(
        block_at(q_weight, d_index, rows_d, 0).astype(f32) * q_weight_grad, axis=1
    ) + jnp.sum(
        block_at(kv_down, d_index, rows_d, 0).astype(f32) * kv_down_grad, axis=1
    ) + jnp.sum(
        block_at(k_rope_weight, d_index, rows_d, 0).astype(f32) * k_rope_grad, axis=1
    )
    attn_gain_part = attn_gain_part / block_at(attn_gain, d_index, rows_d, 0)
    kv_gain_part = jnp.sum(
        block_at(kv_up, d_index, lat_rows, 0).astype(f32) * kv_up_grad, axis=1
    ) / block_at(kv_gain, d_index, lat_rows, 0)
    gains = jnp.concatenate(
        [attn_gain_part.reshape(n_t, 1, -1), kv_gain_part.reshape(n_t, 1, -1)], axis=2
    )
    gains = total(trade([b[0] for b in by_partner(gains, "tensor", 0)], "tensor"))[0]
    attn_gain_grad = gains[:device_rows]
    kv_gain_grad = gains[device_rows:]

    return (
        output,
        input_grad,
        attn_gain_grad,
        q_weight_grad,
        kv_down_grad,
        k_rope_grad,
        kv_gain_grad,
        kv_up_grad,
        o_weight_grad,
        ffn_gain_grad,
        router_grad,
        shared_gate_grad.T,
        shared_up_grad.T,
        shared_down_grad,
        expert_gate_grad.transpose(0, 2, 1),
        expert_up_grad.transpose(0, 2, 1),
        expert_down_grad,
    )


def solution(mesh):
    in_specs = (
        P("dp", None),
        P("dp", None),
        P(),
        P(None, "tensor"),
        P(None, "tensor"),
        P(None, "tensor"),
        P(),
        P(None, "tensor"),
        P("tensor", None),
        P(),
        P(),
        P("dp", None),
        P("dp", None, "tensor"),
        P("dp", None, "tensor"),
        P("dp", "tensor", None),
        P(None, "tensor"),
        P(None, "tensor"),
        P("tensor", None),
    )
    out_specs = (
        P("dp", None),
        P(("dp", "tensor"), None),
        P(("dp", "tensor")),
        P("dp", "tensor"),
        P("dp", "tensor"),
        P("dp", "tensor"),
        P(("dp", "tensor")),
        P("dp", "tensor"),
        P("tensor", "dp"),
        P(("dp", "tensor")),
        P(("dp", "tensor"), None),
        P("dp", "tensor"),
        P("dp", "tensor"),
        P("tensor", "dp"),
        P("dp", None, "tensor"),
        P("dp", None, "tensor"),
        P("dp", "tensor", None),
    )
    return jax.shard_map(
        on_device, mesh=mesh, in_specs=in_specs, out_specs=out_specs, check_vma=False
    )
```

```python
import functools

import jax
import jax.numpy as jnp
import numpy as np
from jax import lax
from jax.experimental import pallas as pl
from jax.experimental.pallas import tpu as pltpu
from jax.sharding import PartitionSpec as P

HD = 128
RD = 64
VD = 128
TOPK = 6
SEQ = 256
CAP = 64
LANES = 128
EPSILON = 1e-06
HEAD = 256
KV = HD + VD
MIB = 1 << 20
VMEM = 60

bf16 = jnp.bfloat16
f32 = jnp.float32


def dot(a, b):
    return lax.dot_general(a, b, (((1,), (0,)), ((), ())), preferred_element_type=f32)


def dot_nt(a, b):
    return lax.dot_general(a, b, (((1,), (1,)), ((), ())), preferred_element_type=f32)


def dot_tn(a, b):
    return lax.dot_general(a, b, (((0,), (0,)), ((), ())), preferred_element_type=f32)


def rope_tables():
    frequency = np.float32(10000.0) ** (-np.arange(RD // 2, dtype=np.float32) * np.float32(2.0 / RD))
    angles = np.arange(SEQ, dtype=np.float32)[:, None] * frequency[None, :]
    blank = np.zeros((SEQ, LANES - RD), np.float32)
    cosine, sine = np.cos(angles), np.sin(angles)
    return (
        jnp.asarray(np.concatenate([cosine, cosine, blank], axis=1)),
        jnp.asarray(np.concatenate([-sine, sine, blank], axis=1)),
    )


def rotate(vector, cosines, sines):
    lane = lax.broadcasted_iota(jnp.int32, vector.shape, 1)
    swapped = jnp.where(
        lane < RD // 2, pltpu.roll(vector, LANES - RD // 2, 1), pltpu.roll(vector, RD // 2, 1)
    )
    return vector * cosines + swapped * sines


def rms_norm(values, gains):
    inv_rms = lax.rsqrt(jnp.mean(values * values, axis=-1, keepdims=True) + EPSILON)
    return (values * inv_rms * gains, inv_rms)


def rms_back(cotan, values, inv_rms, gains):
    weighted = cotan * gains
    inner_mean = jnp.mean(weighted * values, axis=-1, keepdims=True)
    value_grad = inv_rms * weighted - values * (inv_rms * inv_rms * inv_rms) * inner_mean
    gain_grad = jnp.sum(cotan * values * inv_rms, axis=0)
    return (value_grad, gain_grad)


def swap(array, axis, bits):
    count = lax.axis_size(axis)
    return lax.ppermute(array, axis, [(i, i ^ bits) for i in range(count)])


def chip_bits(core):
    bits = [2 << i for i in range((lax.axis_size("dp") // 2).bit_length() - 1)]
    return bits[::-1] if core else bits


def partner_list(core):
    partners = [0]
    for bit in chip_bits(core):
        partners = partners + [p + bit for p in partners]
    return partners


def swap_chips(array, step):
    count = lax.axis_size("dp")
    return lax.ppermute(array, "dp", [(i, i ^ chip_bits(i % 2)[step]) for i in range(count)])


def partner_order():
    core = lax.axis_index("dp") % 2
    lists = jnp.array([partner_list(0), partner_list(1)], jnp.int32)
    return jnp.concatenate([lists[1 - core] ^ 1, lists[core]])


def block_at(array, index, size, dim):
    return lax.dynamic_slice_in_dim(array, index * size, size, dim)


def by_partner(array, axis, dim):
    count = lax.axis_size(axis)
    own = lax.axis_index(axis)
    size = array.shape[dim] // count
    return [block_at(array, own ^ r, size, dim) for r in range(count)]


def reorder(array, axis, dim):
    return jnp.concatenate(by_partner(array, axis, dim), axis=dim)


def share(array, axis):
    return [array] + [swap(array, axis, r) for r in range(1, lax.axis_size(axis))]


def trade(blocks, axis):
    return [blocks[0]] + [swap(blocks[r], axis, r) for r in range(1, len(blocks))]


def sum_along(blocks, sent, axis, others):
    bit, got = 1, sent
    while True:
        stay = [r for r in blocks if not r & bit]
        rows = blocks[0].shape[0]
        blocks = {
            r: blocks[r].astype(f32) + got[i * rows : (i + 1) * rows].astype(f32)
            for i, r in enumerate(stay)
        }
        bit *= 2
        if bit == lax.axis_size(axis):
            return blocks[0]
        got = swap(
            jnp.concatenate([blocks[r].astype(bf16) for r in blocks if r & bit], axis=0), axis, bit
        )
        got = after(got, others)


def gather_chips(block, between):
    own = [block]
    for step in range(len(chip_bits(0))):
        own = own + [
            swap_chips(after(have, between) if i else have, step) for i, have in enumerate(own)
        ]
    return own


def sum_chips(pairs, hook=lambda step, arrived: arrived):
    arrivals = []
    for step in reversed(range(len(chip_bits(0)))):
        got = hook(len(arrivals) // 2, [swap_chips(send, step) for _, send in pairs])
        arrivals.append(got)
        size = got[0].shape[0]
        sums = [keep.astype(f32) + g.astype(f32) for (keep, _), g in zip(pairs, got)]
        pairs = [(s[: size // 2], s[size // 2 :].astype(bf16)) for s in sums]
        arrivals.append([send for _, send in pairs])
    return [s[0] for s in sums], arrivals


def sum_cores(terms):
    pairs = []
    for far, near in terms:
        got = swap(far, "dp", 1)
        half = near.shape[0] // 2
        keep = near[:half].astype(f32) + got[:half].astype(f32)
        send = (near[half:].astype(f32) + got[half:].astype(f32)).astype(bf16)
        pairs.append((keep, send))
    return pairs


def total(blocks):
    return functools.reduce(jnp.add, [block.astype(f32) for block in blocks])


def after(values, *others):
    return lax.optimization_barrier((values, others))[0]


def pick_matrix(slots):
    toks = slots.shape[1]
    place = lax.broadcasted_iota(jnp.int32, (CAP, toks), 0)
    return jnp.concatenate(
        [
            jnp.where(place == slots[e : e + 1, :], 1.0, 0.0).astype(bf16)
            for e in range(slots.shape[0])
        ],
        axis=0,
    )


def fetch(refs, buffer, sems):
    step = pl.program_id(0)

    @pl.when(step == 0)
    def _():
        for i, ref in enumerate(refs):
            pltpu.make_async_copy(ref, buffer.at[i], sems.at[i]).start()

    pltpu.make_async_copy(refs[0], buffer.at[step], sems.at[step]).wait()
    return buffer.at[step]


def by_place(array, tensor, parts):
    size = array.shape[0] // parts
    return [array[pl.ds(pl.multiple_of((tensor ^ r) * size, size), size), :] for r in range(parts)]


def pick_grad_kernel(parts, src_ref, tensor_ref, slots_ref, block_ref, down_ref, rows_ref, dact_ref, placed):
    slots = slots_ref[0]
    blocks = by_place(block_ref.at[0], tensor_ref[0], parts)
    for r, block in enumerate(blocks):
        placed[r * block.shape[0] : (r + 1) * block.shape[0]] = block
    picked = dot(pick_matrix(slots), placed[...]).astype(bf16)
    for e in range(slots.shape[0]):
        rows_ref[e] = picked[e * CAP : (e + 1) * CAP]
    dact_ref[...] = dot_nt(placed[...], down_ref[...])


def pick_kernel(count, experts_all, aliased, slots_ref, router_ref, weights_ref, dact_ref, *refs):
    rows_ref, gate_ref, act_ref, delta_ref, buffer, sems = refs[count + aliased :]
    block = fetch(refs[:count], buffer, sems)
    slots = slots_ref[0]
    experts = slots.shape[0]
    picks = pick_matrix(slots)
    picked = dot(picks, block[...]).astype(bf16)
    for e in range(experts):
        rows_ref[e] = picked[e * CAP : (e + 1) * CAP]
    parts = dot_nt(router_ref[...], block[...])
    logits = parts[:experts_all] + parts[experts_all : 2 * experts_all] + parts[2 * experts_all :]
    spread = jnp.exp(logits - jnp.max(logits, axis=0, keepdims=True))
    prob = spread / jnp.sum(spread, axis=0, keepdims=True)
    for e in range(experts):
        chosen = picks[e * CAP : (e + 1) * CAP].astype(f32) * prob[e : e + 1, :]
        gate_ref[e] = jnp.broadcast_to(jnp.sum(chosen, axis=1, keepdims=True), (CAP, LANES))
    hidden = dot_nt(block[...], weights_ref[...])
    width = hidden.shape[1] // 2
    act, gate_delta, up_delta = gated(hidden[:, :width], hidden[:, width:], dact_ref[...])
    act_ref[...] = act.astype(bf16)
    delta_ref[:, :width] = gate_delta.astype(bf16)
    delta_ref[:, width:] = up_delta.astype(bf16)


def gated(gate_h, up_h, dact):
    sigmoid_h = jax.nn.sigmoid(gate_h)
    silu_h = gate_h * sigmoid_h
    gate_delta = dact * up_h * sigmoid_h * (1.0 + gate_h * (1.0 - sigmoid_h))
    return silu_h * up_h, gate_delta, dact * silu_h


def hidden_kernel(
    first_ref,
    rows_ref,
    grads_ref,
    gate_ref,
    expert_gate_ref,
    expert_up_ref,
    expert_down_ref,
    act_ref,
    gate_delta_ref,
    up_delta_ref,
    score_ref,
):
    rows = rows_ref[0]
    gate_h = dot_nt(rows, expert_gate_ref[0])
    up_h = dot_nt(rows, expert_up_ref[0])
    dact = dot_nt(grads_ref[0], expert_down_ref[0])
    gate = gate_ref[0][:, :1]
    act, gate_delta, up_delta = gated(gate_h, up_h, dact)
    act_ref[0] = (act * gate).astype(bf16)
    gate_delta_ref[0] = (gate_delta * gate).astype(bf16)
    up_delta_ref[0] = (up_delta * gate).astype(bf16)
    score = jnp.sum(act * dact, axis=1, keepdims=True)
    high = score.astype(bf16).astype(f32)
    lanes = score_ref.shape[2]
    lane = lax.broadcasted_iota(jnp.int32, (rows.shape[0], lanes), 1)
    mine = first_ref[0] + pl.program_id(0)
    score_ref[0] = jnp.where(
        lane == mine, high, jnp.where(lane == mine + lanes // 2, score - high, 0.0)
    ).astype(bf16)


def return_kernel(spec, slots_ref, *refs):
    pairs, scored, added, outputs, steps = spec
    deltas, weights = refs[:pairs], refs[pairs : 2 * pairs]
    shared_ref, shared_weight_ref = refs[2 * pairs : 2 * pairs + 2]
    rest = refs[2 * pairs + 2 :]
    score_ref, rest = (rest[0], rest[1:]) if scored else (None, rest)
    other_ref, rest = (rest[0], rest[1:]) if added else (None, rest)
    outs, picks, rows = rest[:outputs], rest[outputs], rest[outputs + 1]
    sources, _, chunk = rows.shape
    experts = slots_ref.shape[1]
    toks = picks.shape[2]
    step = pl.program_id(0)

    def store(s, columns, value):
        if added:
            value = value + other_ref[s, :, columns].astype(f32)
        out = outs[s // (sources // outputs)]
        out[s % (sources // outputs), :, columns] = value.astype(bf16)

    @pl.when(step == 0)
    def _():
        for s in range(sources):
            picks[s] = pick_matrix(slots_ref[s])
        if scored:
            for s in range(sources):
                score = jnp.concatenate(
                    [score_ref[e, s * CAP : (s + 1) * CAP] for e in range(experts)], axis=0
                )
                store(s, pl.ds(steps * chunk, score.shape[1]), dot_tn(picks[s], score))

    for e in range(experts):
        back = functools.reduce(
            jnp.add, [dot(d[e], w[e]) for d, w in zip(deltas, weights)]
        ).astype(bf16)
        for s in range(sources):
            rows[s, e * CAP : (e + 1) * CAP, :] = back[s * CAP : (s + 1) * CAP]
    columns = pl.ds(pl.multiple_of(step * chunk, chunk), chunk)
    for s in range(sources):
        summed = dot_tn(picks[s], rows[s]) + dot(
            shared_ref[s * toks : (s + 1) * toks], shared_weight_ref[...]
        )
        store(s, columns, summed)


def expert_grad_kernel(
    rows_ref,
    grads_ref,
    act_ref,
    gate_delta_ref,
    up_delta_ref,
    gate_grad_ref,
    up_grad_ref,
    down_grad_ref,
):
    rows = rows_ref[0]
    gate_grad_ref[0] = dot_tn(gate_delta_ref[0], rows)
    up_grad_ref[0] = dot_tn(up_delta_ref[0], rows)
    down_grad_ref[0] = dot_tn(act_ref[0], grads_ref[0])


def shared_grad_kernel(count, parts, src_ref, tensor_ref, delta_ref, act_ref, grad_ref, *refs):
    out_ref, buffer, placed, in_acc, down_acc, sems = refs[count:]
    step = pl.program_id(0)
    block = fetch(refs[:count], buffer, sems)
    rows = placed.shape[0] // parts
    for r, part in enumerate(by_place(grad_ref.at[0], tensor_ref[0], parts)):
        placed[r * rows : (r + 1) * rows] = part

    @pl.when(step == 0)
    def _():
        in_acc[...] = jnp.zeros_like(in_acc)
        down_acc[...] = jnp.zeros_like(down_acc)

    in_acc[...] += dot_tn(delta_ref[...], block[...])
    down_acc[...] += dot_tn(act_ref[...], placed[...])

    @pl.when(step == count - 1)
    def _():
        devices, rows, columns = out_ref.shape
        rows //= 3
        middle = in_acc.shape[0] // 2
        for j in range(devices):
            here = slice(j * columns, (j + 1) * columns)
            out_ref[j, :rows] = in_acc[:rows, here].astype(bf16)
            out_ref[j, rows : 2 * rows] = in_acc[middle : middle + rows, here].astype(bf16)
            out_ref[j, 2 * rows :] = down_acc[:rows, here].astype(bf16)


def rows_grad_kernel(src_ref, left_ref, right_ref, far_ref, near_ref):
    half, rows, _ = far_ref.shape
    for i in range(2 * half):
        start = pl.multiple_of(src_ref[i] * rows, rows)
        product = dot_tn(left_ref[:, pl.ds(start, rows)], right_ref[...]).astype(bf16)
        if i < half:
            far_ref[i] = product
        else:
            near_ref[i - half] = product


def columns_grad_kernel(parts, flat, src_ref, left_ref, logits_ref, block_ref, gain_ref, *refs):
    far_ref, near_ref, grads = refs[parts:]
    rows = left_ref.shape[0] // parts
    for r in range(parts):
        grads[r * rows : (r + 1) * rows] = refs[r][:rows]
    half, height, width = far_ref.shape
    wide, experts_all = left_ref.shape[1], logits_ref.shape[1]
    for i in range(2 * half):
        columns = pl.ds(pl.multiple_of(src_ref[i] * width, width), width)
        out = far_ref.at[i] if i < half else near_ref.at[i - half]
        out[:wide] = dot_tn(left_ref[...], grads[:, columns]).astype(bf16)
        router = dot_tn(logits_ref[...], block_ref[:, columns])
        rest = jnp.concatenate(
            [router, jnp.broadcast_to(gain_ref[:, columns], (height - wide - experts_all, width))],
            axis=0,
        )
        out[wide:] = rest.astype(bf16)


def normed_kernel(tokens_ref, gain_ref, down_ref, rope_ref, normed_ref, inv_ref, narrow_ref):
    normed, inv = rms_norm(tokens_ref[...].astype(f32), gain_ref[...])
    normed = normed.astype(bf16)
    normed_ref[...] = normed
    inv_ref[...] = inv
    cols = down_ref.shape[1]
    narrow_ref[:, :cols] = dot(normed, down_ref[...]).astype(bf16)
    narrow_ref[:, cols:] = dot_nt(normed, rope_ref[...]).astype(bf16)


def query_kernel(normed_ref, weight_ref, cosines_ref, sines_ref, query_ref):
    raw = dot(normed_ref[...], weight_ref[...])
    toks = raw.shape[0]
    for h in range(raw.shape[1] // (HD + RD)):
        start = h * (HD + RD)
        rope = jnp.concatenate(
            [raw[:, start + HD : start + HD + RD], jnp.zeros((toks, LANES - RD), f32)], axis=1
        )
        query_ref[:, h * HEAD : h * HEAD + HD] = raw[:, start : start + HD].astype(bf16)
        query_ref[:, h * HEAD + HD : (h + 1) * HEAD] = rotate(
            rope, cosines_ref[...], sines_ref[...]
        ).astype(bf16)


def causal(scores):
    later = lax.broadcasted_iota(jnp.int32, scores.shape, 1) > lax.broadcasted_iota(
        jnp.int32, scores.shape, 0
    )
    return jnp.where(later, -1e30, scores)


def attention_kernel(
    parts,
    tensor_ref,
    query_ref,
    cosines_ref,
    sines_ref,
    place_ref,
    gain_ref,
    up_ref,
    out_weight_ref,
    *refs,
):
    narrow = [ref[...] for ref in refs[:parts]]
    sums = refs[parts : 2 * parts]
    attended_ref, latent_ref, latent_normed_ref, inv_ref, kv_ref, rope_ref, lse_ref, natural = refs[
        2 * parts :
    ]
    toks = query_ref.shape[0]
    heads = query_ref.shape[1] // HEAD
    cols = up_ref.shape[0] // parts
    latent = jnp.concatenate([n[:, :cols] for n in narrow], axis=1)
    latent_ref[...] = latent
    normed, inv = rms_norm(latent.astype(f32), gain_ref[...])
    normed = normed.astype(bf16)
    latent_normed_ref[...] = normed
    inv_ref[...] = inv
    rope = dot(jnp.concatenate([n[:, cols:] for n in narrow], axis=1), place_ref[...])
    rope = rotate(rope, cosines_ref[...], sines_ref[...]).astype(bf16)
    rope_ref[...] = rope
    kv_ref[...] = dot(normed, up_ref[...]).astype(bf16)
    lane = lax.broadcasted_iota(jnp.int32, (toks, LANES), 1)
    lses = jnp.zeros((toks, LANES), f32)
    for h in range(heads):
        key = jnp.concatenate([kv_ref[:, h * KV : h * KV + HD], rope], axis=1)
        scores = causal(dot_nt(query_ref[:, h * HEAD : (h + 1) * HEAD], key) * (HD + RD) ** -0.5)
        top = jnp.max(scores, axis=1, keepdims=True)
        lse = top + jnp.log(jnp.sum(jnp.exp(scores - top), axis=1, keepdims=True))
        lses = jnp.where(lane == h, lse, lses)
        weights = jnp.exp(scores - lse).astype(bf16)
        natural[:, h * VD : (h + 1) * VD] = dot(
            weights, kv_ref[:, h * KV + HD : (h + 1) * KV]
        ).astype(bf16)
    lse_ref[...] = lses
    rows = toks // parts
    for r, block in enumerate(by_place(natural, tensor_ref[0], parts)):
        attended_ref[r * rows : (r + 1) * rows] = block
    for r in range(parts):
        product = dot(attended_ref[r * rows : (r + 1) * rows], out_weight_ref[...])
        sums[r][...] = product.astype(sums[r].dtype)


def attention_back_kernel(
    parts,
    tensor_ref,
    src_ref,
    query_ref,
    kv_ref,
    rope_ref,
    lse_ref,
    latent_ref,
    latent_normed_ref,
    inv_ref,
    cosines_ref,
    sines_ref,
    place_ref,
    gain_ref,
    up_ref,
    out_weight_ref,
    *refs,
):
    grads = refs[:parts]
    narrow = refs[parts : 2 * parts]
    query_grad_ref, up_far_ref, up_near_ref, natural, query_nat, kv_grad, narrow_nat, up_part = refs[
        2 * parts :
    ]
    toks = query_ref.shape[0]
    heads = query_ref.shape[1] // HEAD
    rows = toks // parts
    factor = (HD + RD) ** -0.5
    tensor = tensor_ref[0]
    for r in range(parts):
        place = pl.ds(pl.multiple_of((tensor ^ r) * rows, rows), rows)
        natural[place, :] = dot_nt(grads[r][:rows], out_weight_ref[...]).astype(bf16)
    rope = rope_ref[...]
    rope_sum = jnp.zeros((toks, LANES), f32)
    for h in range(heads):
        grad = natural[:, h * VD : (h + 1) * VD]
        query = query_ref[:, h * HEAD : (h + 1) * HEAD]
        key = jnp.concatenate([kv_ref[:, h * KV : h * KV + HD], rope], axis=1)
        scores = causal(dot_nt(query, key) * factor)
        probs = jnp.exp(scores - lse_ref[:, h : h + 1])
        kv_grad[:, h * KV + HD : (h + 1) * KV] = dot_tn(probs.astype(bf16), grad).astype(bf16)
        prob_dot = dot_nt(grad, kv_ref[:, h * KV + HD : (h + 1) * KV])
        inner = jnp.sum(probs * prob_dot, axis=1, keepdims=True)
        score_grad = (probs * (prob_dot - inner) * factor).astype(bf16)
        query_grad = dot(score_grad, key)
        start = h * (HD + RD)
        query_nat[:, start : start + HD] = query_grad[:, :HD].astype(bf16)
        query_nat[:, start + HD : start + HD + RD] = rotate(
            query_grad[:, HD:], cosines_ref[...], -sines_ref[...]
        )[:, :RD].astype(bf16)
        key_grad = dot_tn(score_grad, query)
        kv_grad[:, h * KV : h * KV + HD] = key_grad[:, :HD].astype(bf16)
        rope_sum = rope_sum + key_grad[:, HD:]
    for r, block in enumerate(by_place(query_nat, tensor, parts)):
        query_grad_ref[r * rows : (r + 1) * rows] = block
    latent_grad, _ = rms_back(
        dot_nt(kv_grad[...], up_ref[...]), latent_ref[...].astype(f32), inv_ref[...], gain_ref[...]
    )
    rope_sum = rotate(rope_sum, cosines_ref[...], -sines_ref[...]).astype(bf16)
    rope_sum = dot_nt(rope_sum, place_ref[...])
    cols = latent_grad.shape[1] // parts
    rope_cols = rope_sum.shape[1] // parts
    for k in range(parts):
        narrow_nat[:, :cols] = latent_grad[:, k * cols : (k + 1) * cols]
        narrow_nat[:, cols:] = rope_sum[:, k * rope_cols : (k + 1) * rope_cols]
        narrow[k][...] = narrow_nat[...].astype(narrow[k].dtype)
    up_part[...] = dot_tn(latent_normed_ref[...], kv_grad[...])
    half, up_rows, _ = up_far_ref.shape
    for i in range(2 * half):
        start = src_ref[i] * up_rows
        start = (start // cols ^ tensor) * cols + start % cols
        block = up_part[pl.ds(pl.multiple_of(start, up_rows), up_rows), :].astype(bf16)
        if i < half:
            up_far_ref[i] = block
        else:
            up_near_ref[i - half] = block


def normed_back_kernel(parts, tensor_ref, query_grad_ref, query_weight_ref, down_ref, rope_ref, *refs):
    narrow = refs[:parts]
    sums = refs[parts : 2 * parts]
    all_ref, natural = refs[2 * parts :]
    cols = down_ref.shape[1]
    natural[...] = total([ref[...] for ref in narrow])
    mine = jnp.concatenate(by_place(natural, tensor_ref[0], parts), axis=0).astype(bf16)
    all_ref[...] = mine
    rows = query_grad_ref.shape[0] // parts
    product = (
        dot_nt(query_grad_ref[...], query_weight_ref[...])
        + dot_nt(mine[:, :cols], down_ref[...])
        + dot(mine[:, cols:], rope_ref[...])
    )
    for r in range(parts):
        sums[r][...] = product[r * rows : (r + 1) * rows].astype(sums[r].dtype)


ANYWHERE = pl.BlockSpec(memory_space=pl.ANY)


def whole(array):
    rank = len(array.shape)
    return pl.BlockSpec(array.shape, lambda *_: (0,) * rank)


def params(mib):
    return pltpu.CompilerParams(vmem_limit_bytes=mib * MIB)


def cost(flops, bytes_accessed, transcendentals=0):
    return pl.CostEstimate(
        flops=int(flops), bytes_accessed=int(bytes_accessed), transcendentals=int(transcendentals)
    )


def pick_grads(src, tensor, parts, slots, grads, shared_down):
    count, experts, toks = slots.shape
    width = grads.shape[2]
    shared = shared_down.shape[0]
    return pl.pallas_call(
        functools.partial(pick_grad_kernel, parts),
        grid_spec=pltpu.PrefetchScalarGridSpec(
            num_scalar_prefetch=2,
            grid=(count,),
            in_specs=[
                pl.BlockSpec((1, experts, toks), lambda s, src, t: (s, 0, 0)),
                pl.BlockSpec((1, toks, width), lambda s, src, t: (src[s], 0, 0)),
                whole(shared_down),
            ],
            out_specs=[
                pl.BlockSpec((experts, CAP, width), lambda s, src, t: (0, s, 0)),
                pl.BlockSpec((toks, shared), lambda s, src, t: (s, 0)),
            ],
            scratch_shapes=[pltpu.VMEM((toks, width), bf16)],
        ),
        out_shape=[
            jax.ShapeDtypeStruct((experts, count * CAP, width), bf16),
            jax.ShapeDtypeStruct((count * toks, shared), f32),
        ],
        compiler_params=params(VMEM),
        cost_estimate=cost(
            2 * count * toks * width * (experts * CAP + shared), 4 * count * toks * width
        ),
    )(src, tensor, slots, grads, shared_down)


def pick_rows(blocks, places, slots, router, weights, dact, experts_all, results):
    count = len(blocks)
    run = next(i for i in range(1, count) if places[i] != places[i - 1] + 1)
    first, skip = places[0], places[run] - places[0] - run

    def place(s):
        return s + first + jnp.where(s < run, 0, skip)

    every, experts, toks = slots.shape
    width = blocks[0].shape[1]
    shared = dact.shape[1]
    operands = [slots, router, weights, dact, *blocks, *results]
    return pl.pallas_call(
        functools.partial(pick_kernel, count, experts_all, len(results)),
        grid=(count,),
        in_specs=[
            pl.BlockSpec((1, experts, toks), lambda s: (place(s), 0, 0)),
            whole(router),
            whole(weights),
            pl.BlockSpec((toks, shared), lambda s: (place(s), 0)),
        ]
        + [ANYWHERE] * (count + len(results)),
        out_specs=[
            pl.BlockSpec((experts, CAP, width), lambda s: (0, place(s), 0)),
            pl.BlockSpec((experts, CAP, LANES), lambda s: (0, place(s), 0)),
            pl.BlockSpec((toks, shared), lambda s: (place(s), 0)),
            pl.BlockSpec((toks, 2 * shared), lambda s: (place(s), 0)),
        ],
        out_shape=[
            shape(bf16, experts, every * CAP, width),
            shape(f32, experts, every * CAP, LANES),
            shape(bf16, every * toks, shared),
            shape(bf16, every * toks, 2 * shared),
        ],
        input_output_aliases={len(operands) - len(results) + i: i for i in range(len(results))},
        scratch_shapes=[
            pltpu.VMEM((count, toks, width), bf16),
            pltpu.SemaphoreType.DMA((count,)),
        ],
        compiler_params=params(VMEM),
        cost_estimate=cost(
            2 * count * toks * width * (experts * CAP + router.shape[0] + 2 * shared),
            4 * count * toks * width,
        ),
    )(*operands)


def expert_hidden(first, rows, grads, gate, expert_gate, expert_up, expert_down, lanes):
    experts, slot_rows, width = rows.shape
    hidden = expert_gate.shape[1]

    def per_expert(array):
        return pl.BlockSpec((1,) + array.shape[1:], lambda e: (e, 0, 0))

    narrow = jax.ShapeDtypeStruct((experts, slot_rows, hidden), bf16)
    score = jax.ShapeDtypeStruct((experts, slot_rows, lanes), bf16)
    return pl.pallas_call(
        hidden_kernel,
        grid=(experts,),
        in_specs=[pl.BlockSpec(memory_space=pltpu.SMEM)]
        + [per_expert(a) for a in (rows, grads, gate, expert_gate, expert_up, expert_down)],
        out_specs=[per_expert(narrow)] * 3 + [per_expert(score)],
        out_shape=[narrow] * 3 + [score],
        compiler_params=params(VMEM),
        cost_estimate=cost(
            6 * experts * slot_rows * width * hidden,
            experts * (4 * slot_rows * width + 6 * hidden * width),
            experts * slot_rows * hidden,
        ),
    )(first, rows, grads, gate, expert_gate, expert_up, expert_down)


def return_rows(half, slots, deltas, weights, shared, shared_weight, score, start, size, other):
    experts, slot_rows, hidden = deltas[0].shape
    sources = slots.shape[0] // 2
    toks = slots.shape[2]
    chunk = min(512, size)
    steps = size // chunk
    first = start // chunk
    outputs = 1 + half
    lanes = 0 if score is None else score.shape[2]
    in_specs = (
        [pl.BlockSpec((sources,) + slots.shape[1:], lambda n: (half, 0, 0))]
        + [pl.BlockSpec((experts, slot_rows // 2, hidden), lambda n: (0, half, 0))] * len(deltas)
        + [pl.BlockSpec((experts, hidden, chunk), lambda n: (0, 0, n + first))] * len(weights)
        + [
            pl.BlockSpec((sources * toks, shared.shape[1]), lambda n: (half, 0)),
            pl.BlockSpec((shared.shape[1], chunk), lambda n: (0, n + first)),
        ]
    )
    operands = [slots, *deltas, *weights, shared, shared_weight]
    if score is not None:
        in_specs.append(pl.BlockSpec((experts, slot_rows // 2, lanes), lambda n: (0, half, 0)))
        operands.append(score)
    if other is not None:
        in_specs.append(whole(other))
        operands.append(other)
    out = jax.ShapeDtypeStruct((sources // outputs, toks, size + lanes), bf16)
    return pl.pallas_call(
        functools.partial(
            return_kernel, (len(deltas), score is not None, other is not None, outputs, steps)
        ),
        grid=(steps,),
        in_specs=in_specs,
        out_specs=[whole(out)] * outputs,
        out_shape=[out] * outputs,
        scratch_shapes=[
            pltpu.VMEM((sources, experts * CAP, toks), bf16),
            pltpu.VMEM((sources, experts * CAP, chunk), bf16),
        ],
        compiler_params=params(VMEM),
        cost_estimate=cost(
            2 * experts * slot_rows // 2 * size * (hidden * len(deltas) + toks)
            + 2 * sources * toks * size * shared.shape[1],
            2 * size * (experts * hidden * len(deltas) + sources * toks),
        ),
    )(*operands)


def expert_grads(rows, grads, act, gate_delta, up_delta):
    experts, slot_rows, width = rows.shape
    hidden = act.shape[2]

    def per_expert(array):
        return pl.BlockSpec((1,) + array.shape[1:], lambda e: (e, 0, 0))

    out = jax.ShapeDtypeStruct((experts, hidden, width), f32)
    return pl.pallas_call(
        expert_grad_kernel,
        grid=(experts,),
        in_specs=[per_expert(a) for a in (rows, grads, act, gate_delta, up_delta)],
        out_specs=[per_expert(out)] * 3,
        out_shape=[out] * 3,
        compiler_params=params(VMEM),
        cost_estimate=cost(
            6 * experts * slot_rows * width * hidden,
            experts * (4 * slot_rows * width + 12 * hidden * width),
        ),
    )(rows, grads, act, gate_delta, up_delta)


def shared_grads(src, tensor, parts, blocks, grads, delta, act, cols):
    count = grads.shape[0]
    toks, width = blocks[0].shape
    out = jax.ShapeDtypeStruct((count, 3 * cols, width // count), bf16)
    return pl.pallas_call(
        functools.partial(shared_grad_kernel, count, parts),
        grid_spec=pltpu.PrefetchScalarGridSpec(
            num_scalar_prefetch=2,
            grid=(count,),
            in_specs=[
                pl.BlockSpec((toks, delta.shape[1]), lambda s, src, t: (s, 0)),
                pl.BlockSpec((toks, act.shape[1]), lambda s, src, t: (s, 0)),
                pl.BlockSpec((1, toks, width), lambda s, src, t: (src[s], 0, 0)),
            ]
            + [ANYWHERE] * count,
            out_specs=whole(out),
            scratch_shapes=[
                pltpu.VMEM((count, toks, width), bf16),
                pltpu.VMEM((toks, width), bf16),
                pltpu.VMEM((delta.shape[1], width), f32),
                pltpu.VMEM((act.shape[1], width), f32),
                pltpu.SemaphoreType.DMA((count,)),
            ],
        ),
        out_shape=out,
        compiler_params=params(VMEM),
        cost_estimate=cost(
            2 * count * toks * width * (delta.shape[1] + act.shape[1]), 4 * count * toks * width
        ),
    )(src, tensor, delta, act, grads, *blocks)


def single(kernel, outs, operands, scalars=(), scratch=(), flops=0, transcendentals=0):
    return pl.pallas_call(
        kernel,
        grid_spec=pltpu.PrefetchScalarGridSpec(
            num_scalar_prefetch=len(scalars),
            grid=(1,),
            in_specs=[whole(a) for a in operands],
            out_specs=[whole(o) for o in outs],
            scratch_shapes=list(scratch),
        ),
        out_shape=list(outs),
        compiler_params=params(VMEM),
        cost_estimate=cost(flops, sum(a.size * a.dtype.itemsize for a in operands), transcendentals),
    )(*scalars, *operands)


def shape(dtype, *sizes):
    return jax.ShapeDtypeStruct(sizes, dtype)


def on_device(
    tokens,
    cotangent,
    attn_gain,
    q_weight,
    kv_down,
    k_rope_weight,
    kv_gain,
    kv_up,
    o_weight,
    ffn_gain,
    router_weight,
    expert_ids,
    expert_gate,
    expert_up,
    expert_down,
    shared_gate,
    shared_up,
    shared_down,
):
    n_t = lax.axis_size("tensor")
    n_d = lax.axis_size("dp")
    half = n_d // 2
    t_index = lax.axis_index("tensor")
    d_index = lax.axis_index("dp")
    toks, width = tokens.shape
    own_toks = toks // n_t
    rows_d = width // n_d
    q_cols = q_weight.shape[1]
    heads = q_cols // (HD + RD)
    experts_all = router_weight.shape[1]
    experts = expert_gate.shape[0]
    cosines, sines = rope_tables()
    order = partner_order()
    src = d_index.astype(jnp.int32) ^ order
    sources = [src[i] for i in range(n_d)]
    lat_cols = kv_down.shape[1]
    lat_rank = kv_up.shape[0]
    rope_cols = k_rope_weight.shape[1]
    narrow_cols = lat_cols + rope_cols
    expert_gate_t = expert_gate.transpose(0, 2, 1)
    expert_up_t = expert_up.transpose(0, 2, 1)

    tokens_p = by_partner(tokens, "tensor", 0)
    tokens_own = tokens_p[0].astype(f32)
    cot_own = block_at(cotangent, t_index, own_toks, 0).astype(f32)
    tensor = t_index.astype(jnp.int32).reshape(1)
    every = jnp.arange(experts_all, dtype=jnp.int32)
    member = jnp.any(expert_ids.T[:, None, :] == every[None, :, None], axis=0)
    before = (jnp.arange(toks)[:, None] < jnp.arange(toks)[None, :]).astype(bf16)
    rank = dot(member.astype(bf16), before)
    slots_own = jnp.where(member, rank, -1.0).astype(bf16).reshape(-1, width)
    slot_rows = slots_own.shape[0]
    slots_own = jnp.pad(slots_own, ((0, -slot_rows % 16), (0, 0)))
    cot_all = lax.all_gather(jnp.concatenate([cotangent, slots_own], axis=0), "dp")
    slots = cot_all[:, toks : toks + slot_rows].reshape(n_d, experts_all, toks)
    slots = reorder(block_at(slots, d_index, experts, 1), "tensor", 2)
    slots = jnp.concatenate([block_at(slots, s, 1, 0) for s in sources], axis=0).astype(jnp.int32)
    router_t = jnp.roll(router_weight.T, -d_index * experts, axis=0)
    router_parts = []
    rest = router_t
    for _ in range(3):
        part = lax.reduce_precision(rest, 8, 7)
        router_parts.append(part.astype(bf16))
        rest = rest - part
    router_parts = jnp.concatenate(router_parts, axis=0)
    shared_cols = shared_down.shape[0] // n_d
    shared_pad = -shared_cols % LANES
    shared_gate_t, shared_up_t, shared_out = [
        jnp.pad(block_at(w, d_index, shared_cols, 0), ((0, shared_pad), (0, 0)))
        for w in (shared_gate.T, shared_up.T, shared_down)
    ]
    shared_in = jnp.concatenate([shared_gate_t, shared_up_t], axis=0)
    grad_rows, shared_dact = pick_grads(src, tensor, n_t, slots, cot_all, shared_out)

    kv_up_p = reorder(kv_up, "tensor", 0)
    kv_gain_p = reorder(kv_gain, "tensor", 0)[None]
    rope_t = k_rope_weight.T
    rope_place = (
        (t_index ^ jnp.arange(n_t)[:, None, None]) * rope_cols + jnp.arange(rope_cols)[None, :, None]
        == jnp.arange(LANES)
    ).astype(bf16).reshape(RD, LANES)
    normed, inv_first, narrow_own = single(
        normed_kernel,
        [shape(bf16, toks, width), shape(f32, toks, 1), shape(bf16, toks, narrow_cols)],
        [tokens, attn_gain[None], kv_down, rope_t],
        flops=2 * toks * width * narrow_cols,
    )
    narrow_blocks = share(narrow_own, "tensor")
    query = single(
        query_kernel,
        [shape(bf16, toks, heads * HEAD)],
        [normed, q_weight, cosines, sines],
        flops=2 * toks * width * q_cols,
    )[0]
    results = single(
        functools.partial(attention_kernel, n_t),
        [shape(f32 if r == 0 else bf16, own_toks, width) for r in range(n_t)]
        + [
            shape(bf16, toks, heads * VD),
            shape(bf16, toks, lat_rank),
            shape(bf16, toks, lat_rank),
            shape(f32, toks, 1),
            shape(bf16, toks, heads * KV),
            shape(bf16, toks, LANES),
            shape(f32, toks, LANES),
        ],
        [query, cosines, sines, rope_place, kv_gain_p, kv_up_p, o_weight, *narrow_blocks],
        scalars=[tensor],
        scratch=[pltpu.VMEM((toks, heads * VD), bf16)],
        flops=2 * toks * heads * (KV * lat_rank + 2 * HEAD * toks + VD * width),
        transcendentals=2 * heads * toks * toks,
    )
    attn_part = results[:n_t]
    attended_p, latent, latent_normed, inv_latent, key_value, rope_rot, lse = results[n_t:]
    attn_sum = total(
        after(trade(attn_part, "tensor"), router_parts, shared_in, shared_out, inv_first, kv_up_p)
    )
    hidden_one = tokens_own + attn_sum
    ffn_normed_f, inv_second = rms_norm(hidden_one, ffn_gain)
    ffn_own = ffn_normed_f.astype(bf16)
    ffn_block = jnp.concatenate(share(ffn_own, "tensor"), axis=0)
    near_blocks = gather_chips(ffn_block, grad_rows)
    far_blocks = [swap(block, "dp", 1) for block in near_blocks[:-1]]

    def pick(places, blocks_here, results):
        return pick_rows(
            blocks_here, places, slots, router_parts, shared_in, shared_dact, experts_all, results
        )

    early = [0] + list(range(half, n_d - 1))
    results = pick(early, far_blocks[:1] + near_blocks[:-1], [])
    far_blocks.append(swap(after(near_blocks[-1], results), "dp", 1))
    late = list(range(1, half)) + [n_d - 1]
    blocks = far_blocks + near_blocks

    results = pick(late, [blocks[i] for i in late], results)
    rows, gate, shared_act, shared_delta = results
    lanes = -(-2 * experts_all // LANES) * LANES
    first = (d_index * experts).astype(jnp.int32).reshape(1)
    act, gate_delta, up_delta, score = expert_hidden(
        first, rows, grad_rows, gate, expert_gate_t, expert_up_t, expert_down, lanes
    )

    def send_back(sum_here):
        return trade(
            [sum_here[k * own_toks : (k + 1) * own_toks].astype(bf16) for k in range(n_t)], "tensor"
        )

    pieces = 2
    size = width // pieces
    deltas, delta_weights = [gate_delta, up_delta], [expert_gate_t, expert_up_t]
    others = [
        return_rows(
            0, slots, deltas, delta_weights, shared_delta, shared_in,
            score if i == pieces - 1 else None, i * size, size, None,
        )[0]
        for i in range(pieces)
    ]
    others = [swap(other, "dp", 1) for other in others]
    mine = [
        return_rows(
            1, slots, deltas, delta_weights, shared_delta, shared_in,
            score if i == pieces - 1 else None, i * size, size, others[i],
        )
        for i in range(pieces)
    ]
    out_other = []

    def beside(step, arrived):
        if step:
            return arrived
        out_other.extend(
            return_rows(
                0, slots, [after(act, arrived[0], mine[1:])], [expert_down], shared_act, shared_out,
                None, 0, width, None,
            )
        )
        return arrived[:1] + after(arrived[1:], out_other)

    sums, arrivals = sum_chips(mine, beside)
    shared_rows = shared_cols + -shared_cols % 16
    back_sums = [total(send_back(s)) for s in sums]
    back_sum = jnp.concatenate(back_sums[:-1] + [back_sums[-1][:, :size]], axis=1)
    score_sum = back_sums[-1][:, size:]
    logits = jnp.dot(ffn_own.astype(f32), router_weight, precision=lax.Precision.HIGHEST)
    router_prob = jax.nn.softmax(logits, axis=-1)
    prob_grad = score_sum[:, :experts_all] + score_sum[:, lanes // 2 : lanes // 2 + experts_all]
    logit_grad = (
        router_prob * (prob_grad - jnp.sum(router_prob * prob_grad, axis=-1, keepdims=True))
    ).astype(bf16)
    ffn_normed_grad = back_sum + jnp.dot(
        logit_grad.astype(f32), router_weight.T, precision=lax.Precision.HIGHEST
    )
    hidden_norm_grad, ffn_gain_part = rms_back(ffn_normed_grad, hidden_one, inv_second, ffn_gain)
    hidden_grad = cot_own + hidden_norm_grad
    flat_logits = logit_grad.reshape(-1, width)
    flat = flat_logits.shape[0]
    extra = jnp.concatenate(
        [
            flat_logits,
            ffn_gain_part.astype(bf16)[None],
            jnp.zeros((-(flat + 1) % 8, width), bf16),
        ],
        axis=0,
    )
    message = jnp.concatenate([hidden_grad.astype(bf16), extra], axis=0)
    shared_grads_t = share(message, "tensor")
    out_pair = return_rows(
        1, slots, [act], [expert_down], shared_act, shared_out, None, 0, width,
        after(swap(out_other[0], "dp", 1), message),
    )
    shared_all = shared_grads(
        src, tensor, n_t, blocks, cot_all, *after((shared_delta, shared_act), out_pair), shared_rows
    )
    shared_grads_t = after(shared_grads_t, shared_all)

    lat_rows = lat_rank // n_d
    results = single(
        functools.partial(attention_back_kernel, n_t),
        [shape(f32 if r == 0 else bf16, toks, narrow_cols) for r in range(n_t)]
        + [
            shape(bf16, toks, q_cols),
            shape(bf16, half, lat_rows, heads * KV),
            shape(bf16, half, lat_rows, heads * KV),
        ],
        [
            query, key_value, rope_rot, lse, latent, latent_normed, inv_latent, cosines, sines,
            rope_place, kv_gain_p, kv_up_p, o_weight, *shared_grads_t,
        ],
        scalars=[tensor, src],
        scratch=[
            pltpu.VMEM((toks, heads * VD), bf16),
            pltpu.VMEM((toks, q_cols), bf16),
            pltpu.VMEM((toks, heads * KV), bf16),
            pltpu.VMEM((toks, narrow_cols), f32),
            pltpu.VMEM((lat_rank, heads * KV), f32),
        ],
        flops=2 * toks * heads * (2 * KV * lat_rank + 5 * HEAD * toks + VD * width),
        transcendentals=heads * toks * toks,
    )
    latent_parts = results[:n_t]
    query_grad_p, kv_up_far, kv_up_near = results[n_t:]
    normed_p = reorder(normed, "tensor", 0)

    def rows_grad(left, right):
        return single(
            rows_grad_kernel,
            [shape(bf16, half, rows_d, right.shape[1])] * 2,
            [left, right],
            scalars=[src],
            flops=2 * toks * width * right.shape[1],
        )

    logit_p = jnp.concatenate(
        [b[own_toks : own_toks + flat].reshape(own_toks, experts_all) for b in shared_grads_t], axis=0
    )
    gain_part = total([b[own_toks + flat] for b in shared_grads_t])[None]
    out_cols = attended_p.shape[1]
    height = out_cols + experts_all + 16
    column_terms = single(
        functools.partial(columns_grad_kernel, n_t, flat),
        [shape(bf16, half, height, rows_d)] * 2,
        [after(attended_p, query_grad_p), logit_p, ffn_block, gain_part, *shared_grads_t],
        scalars=[src],
        scratch=[pltpu.VMEM((toks, width), bf16)],
        flops=2 * toks * width * height,
    )
    query_terms = rows_grad(normed_p, query_grad_p)
    terms = [query_terms, column_terms, (kv_up_far, kv_up_near)]
    latent_parts = after(trade(latent_parts, "tensor"), terms)
    out_sums, out_steps = sum_chips([out_pair], lambda step, arrived: after(arrived, latent_parts))
    out_here = out_sums[0]
    out_rows = {r: out_here[r * own_toks : (r + 1) * own_toks] for r in range(n_t)}
    results = single(
        functools.partial(normed_back_kernel, n_t),
        [shape(f32 if r == 0 else bf16, own_toks, width) for r in range(n_t)]
        + [shape(bf16, toks, narrow_cols)],
        [query_grad_p, q_weight, kv_down, rope_t, *latent_parts],
        scalars=[tensor],
        scratch=[pltpu.VMEM((toks, narrow_cols), f32)],
        flops=2 * toks * width * (q_cols + narrow_cols),
    )
    normed_part, narrow_p = results[:n_t], results[n_t]
    query_pairs = sum_cores(after(terms[:1], normed_part))
    expert_gate_grad, expert_up_grad, expert_down_grad = expert_grads(
        rows, grad_rows, *after((act, gate_delta, up_delta), query_pairs[0][1], out_steps[1])
    )
    shared_sent = lax.all_to_all(after(shared_all, expert_gate_grad), "dp", 0, 0, tiled=True).astype(f32)
    shared_gate_grad, shared_up_grad, shared_down_grad = [
        shared_sent[:, i * shared_rows : i * shared_rows + shared_cols].reshape(-1, rows_d)
        for i in range(3)
    ]
    out_message = after(
        jnp.concatenate([out_rows[r].astype(bf16) for r in out_rows if r & 1], axis=0),
        expert_gate_grad,
    )
    out_sent = swap(out_message, "tensor", 1)
    normed_arrived = after(trade(normed_part, "tensor"), expert_gate_grad)
    normed_grad = total(normed_arrived)
    (q_weight_grad,), term_arrivals = sum_chips(query_pairs)
    terms = terms[1:] + [rows_grad(normed_p, after(narrow_p, expert_gate_grad))]
    pairs = after(sum_cores(after(terms, expert_gate_grad, out_message)), term_arrivals[0])
    (columns, kv_up_grad, narrow_grad), chain = sum_chips(
        pairs, lambda step, arrived: after(arrived, term_arrivals[min(2 * step + 2, len(term_arrivals) - 2)])
    )
    sends = [send for _, send in pairs] + term_arrivals[1]
    out_sum = sum_along(
        out_rows, after(out_sent, normed_arrived[1:], sends), "tensor", chain[1] or sends
    )
    output_own = (hidden_one + out_sum).astype(bf16)
    output_blocks = share(after(output_own, chain[-2]), "tensor")
    inv_first_own = block_at(inv_first, t_index, own_toks, 0)
    input_norm_grad, _ = rms_back(normed_grad, tokens_own, inv_first_own, attn_gain)
    input_grad = hidden_grad + input_norm_grad

    o_weight_grad = columns[:out_cols]
    device_rows = width // (n_d * n_t)
    router_grad = block_at(
        columns[out_cols : out_cols + experts_all], t_index, device_rows, 1
    ).T
    ffn_gain_grad = block_at(columns[out_cols + experts_all], t_index, device_rows, 0)
    kv_down_grad = narrow_grad[:, :lat_cols]
    k_rope_grad = narrow_grad[:, lat_cols:]

    attn_gain_part = jnp.sum(
        block_at(q_weight, d_index, rows_d, 0).astype(f32) * q_weight_grad, axis=1
    ) + jnp.sum(
        block_at(kv_down, d_index, rows_d, 0).astype(f32) * kv_down_grad, axis=1
    ) + jnp.sum(
        block_at(k_rope_weight, d_index, rows_d, 0).astype(f32) * k_rope_grad, axis=1
    )
    attn_gain_part = attn_gain_part / block_at(attn_gain, d_index, rows_d, 0)
    kv_gain_part = jnp.sum(
        block_at(kv_up, d_index, lat_rows, 0).astype(f32) * kv_up_grad, axis=1
    ) / block_at(kv_gain, d_index, lat_rows, 0)
    gains = jnp.concatenate(
        [attn_gain_part.reshape(n_t, 1, -1), kv_gain_part.reshape(n_t, 1, -1)], axis=2
    )
    gains = total(trade([b[0] for b in by_partner(gains, "tensor", 0)], "tensor"))[0]
    output = reorder(jnp.concatenate(after(output_blocks, gains), axis=0), "tensor", 0)
    attn_gain_grad = gains[:device_rows]
    kv_gain_grad = gains[device_rows:]

    return (
        output,
        input_grad,
        attn_gain_grad,
        q_weight_grad,
        kv_down_grad,
        k_rope_grad,
        kv_gain_grad,
        kv_up_grad,
        o_weight_grad,
        ffn_gain_grad,
        router_grad,
        shared_gate_grad.T,
        shared_up_grad.T,
        shared_down_grad,
        expert_gate_grad.transpose(0, 2, 1),
        expert_up_grad.transpose(0, 2, 1),
        expert_down_grad,
    )


def solution(mesh):
    in_specs = (
        P("dp", None),
        P("dp", None),
        P(),
        P(None, "tensor"),
        P(None, "tensor"),
        P(None, "tensor"),
        P(),
        P(None, "tensor"),
        P("tensor", None),
        P(),
        P(),
        P("dp", None),
        P("dp", None, "tensor"),
        P("dp", None, "tensor"),
        P("dp", "tensor", None),
        P(None, "tensor"),
        P(None, "tensor"),
        P("tensor", None),
    )
    out_specs = (
        P("dp", None),
        P(("dp", "tensor"), None),
        P(("dp", "tensor")),
        P("dp", "tensor"),
        P("dp", "tensor"),
        P("dp", "tensor"),
        P(("dp", "tensor")),
        P("dp", "tensor"),
        P("tensor", "dp"),
        P(("dp", "tensor")),
        P(("dp", "tensor"), None),
        P("dp", "tensor"),
        P("dp", "tensor"),
        P("tensor", "dp"),
        P("dp", None, "tensor"),
        P("dp", None, "tensor"),
        P("dp", "tensor", None),
    )
    return jax.shard_map(
        on_device, mesh=mesh, in_specs=in_specs, out_specs=out_specs, check_vma=False
    )
```

```python
import functools

import jax
import jax.numpy as jnp
import numpy as np
from jax import lax
from jax.experimental import pallas as pl
from jax.experimental.pallas import tpu as pltpu
from jax.sharding import PartitionSpec as P

HD = 128
RD = 64
VD = 128
TOPK = 6
SEQ = 256
CAP = 64
LANES = 128
EPSILON = 1e-06
HEAD = 256
KV = HD + VD
MIB = 1 << 20
VMEM = 60

bf16 = jnp.bfloat16
f32 = jnp.float32


def dot(a, b):
    return lax.dot_general(a, b, (((1,), (0,)), ((), ())), preferred_element_type=f32)


def dot_nt(a, b):
    return lax.dot_general(a, b, (((1,), (1,)), ((), ())), preferred_element_type=f32)


def dot_tn(a, b):
    return lax.dot_general(a, b, (((0,), (0,)), ((), ())), preferred_element_type=f32)


def rope_tables():
    frequency = np.float32(10000.0) ** (-np.arange(RD // 2, dtype=np.float32) * np.float32(2.0 / RD))
    angles = np.arange(SEQ, dtype=np.float32)[:, None] * frequency[None, :]
    blank = np.zeros((SEQ, LANES - RD), np.float32)
    cosine, sine = np.cos(angles), np.sin(angles)
    return (
        jnp.asarray(np.concatenate([cosine, cosine, blank], axis=1)),
        jnp.asarray(np.concatenate([-sine, sine, blank], axis=1)),
    )


def rotate(vector, cosines, sines):
    lane = lax.broadcasted_iota(jnp.int32, vector.shape, 1)
    swapped = jnp.where(
        lane < RD // 2, pltpu.roll(vector, LANES - RD // 2, 1), pltpu.roll(vector, RD // 2, 1)
    )
    return vector * cosines + swapped * sines


def rms_norm(values, gains):
    inv_rms = lax.rsqrt(jnp.mean(values * values, axis=-1, keepdims=True) + EPSILON)
    return (values * inv_rms * gains, inv_rms)


def rms_back(cotan, values, inv_rms, gains):
    weighted = cotan * gains
    inner_mean = jnp.mean(weighted * values, axis=-1, keepdims=True)
    value_grad = inv_rms * weighted - values * (inv_rms * inv_rms * inv_rms) * inner_mean
    gain_grad = jnp.sum(cotan * values * inv_rms, axis=0)
    return (value_grad, gain_grad)


def swap(array, axis, bits):
    count = lax.axis_size(axis)
    return lax.ppermute(array, axis, [(i, i ^ bits) for i in range(count)])


def chip_bits(core):
    bits = [2 << i for i in range((lax.axis_size("dp") // 2).bit_length() - 1)]
    return bits[::-1] if core else bits


def partner_list(core):
    partners = [0]
    for bit in chip_bits(core):
        partners = partners + [p + bit for p in partners]
    return partners


def swap_chips(array, step):
    count = lax.axis_size("dp")
    return lax.ppermute(array, "dp", [(i, i ^ chip_bits(i % 2)[step]) for i in range(count)])


def partner_order():
    core = lax.axis_index("dp") % 2
    lists = jnp.array([partner_list(0), partner_list(1)], jnp.int32)
    return jnp.concatenate([lists[1 - core] ^ 1, lists[core]])


def block_at(array, index, size, dim):
    return lax.dynamic_slice_in_dim(array, index * size, size, dim)


def by_partner(array, axis, dim):
    count = lax.axis_size(axis)
    own = lax.axis_index(axis)
    size = array.shape[dim] // count
    return [block_at(array, own ^ r, size, dim) for r in range(count)]


def reorder(array, axis, dim):
    return jnp.concatenate(by_partner(array, axis, dim), axis=dim)


def share(array, axis):
    return [array] + [swap(array, axis, r) for r in range(1, lax.axis_size(axis))]


def trade(blocks, axis):
    return [blocks[0]] + [swap(blocks[r], axis, r) for r in range(1, len(blocks))]


def sum_along(blocks, sent, axis, others):
    bit, got = 1, sent
    while True:
        stay = [r for r in blocks if not r & bit]
        rows = blocks[0].shape[0]
        blocks = {
            r: blocks[r].astype(f32) + got[i * rows : (i + 1) * rows].astype(f32)
            for i, r in enumerate(stay)
        }
        bit *= 2
        if bit == lax.axis_size(axis):
            return blocks[0]
        got = swap(
            jnp.concatenate([blocks[r].astype(bf16) for r in blocks if r & bit], axis=0), axis, bit
        )
        got = after(got, others)


def gather_chips(block, between):
    own = [block]
    for step in range(len(chip_bits(0))):
        own = own + [
            swap_chips(after(have, between) if i else have, step) for i, have in enumerate(own)
        ]
    return own


def sum_chips(pairs, hook=lambda step, arrived: arrived):
    arrivals = []
    for step in reversed(range(len(chip_bits(0)))):
        got = hook(len(arrivals) // 2, [swap_chips(send, step) for _, send in pairs])
        arrivals.append(got)
        size = got[0].shape[0]
        sums = [keep.astype(f32) + g.astype(f32) for (keep, _), g in zip(pairs, got)]
        pairs = [(s[: size // 2], s[size // 2 :].astype(bf16)) for s in sums]
        arrivals.append([send for _, send in pairs])
    return [s[0] for s in sums], arrivals


def sum_cores(terms):
    pairs = []
    for far, near in terms:
        got = swap(far, "dp", 1)
        half = near.shape[0] // 2
        keep = near[:half].astype(f32) + got[:half].astype(f32)
        send = (near[half:].astype(f32) + got[half:].astype(f32)).astype(bf16)
        pairs.append((keep, send))
    return pairs


def total(blocks):
    return functools.reduce(jnp.add, [block.astype(f32) for block in blocks])


def after(values, *others):
    return lax.optimization_barrier((values, others))[0]


def pick_matrix(slots):
    toks = slots.shape[1]
    place = lax.broadcasted_iota(jnp.int32, (CAP, toks), 0)
    return jnp.concatenate(
        [
            jnp.where(place == slots[e : e + 1, :], 1.0, 0.0).astype(bf16)
            for e in range(slots.shape[0])
        ],
        axis=0,
    )


def fetch(refs, buffer, sems):
    step = pl.program_id(0)

    @pl.when(step == 0)
    def _():
        for i, ref in enumerate(refs):
            pltpu.make_async_copy(ref, buffer.at[i], sems.at[i]).start()

    pltpu.make_async_copy(refs[0], buffer.at[step], sems.at[step]).wait()
    return buffer.at[step]


def by_place(array, tensor, parts):
    size = array.shape[0] // parts
    return [array[pl.ds(pl.multiple_of((tensor ^ r) * size, size), size), :] for r in range(parts)]


def pick_grad_kernel(parts, src_ref, tensor_ref, slots_ref, block_ref, down_ref, rows_ref, dact_ref, placed):
    slots = slots_ref[0]
    blocks = by_place(block_ref.at[0], tensor_ref[0], parts)
    for r, block in enumerate(blocks):
        placed[r * block.shape[0] : (r + 1) * block.shape[0]] = block
    picked = dot(pick_matrix(slots), placed[...]).astype(bf16)
    for e in range(slots.shape[0]):
        rows_ref[e] = picked[e * CAP : (e + 1) * CAP]
    dact_ref[...] = dot_nt(placed[...], down_ref[...])


def pick_kernel(count, experts_all, aliased, slots_ref, router_ref, weights_ref, dact_ref, *refs):
    rows_ref, gate_ref, act_ref, delta_ref, buffer, sems = refs[count + aliased :]
    block = fetch(refs[:count], buffer, sems)
    slots = slots_ref[0]
    experts = slots.shape[0]
    picks = pick_matrix(slots)
    picked = dot(picks, block[...]).astype(bf16)
    for e in range(experts):
        rows_ref[e] = picked[e * CAP : (e + 1) * CAP]
    parts = dot_nt(router_ref[...], block[...])
    logits = parts[:experts_all] + parts[experts_all : 2 * experts_all] + parts[2 * experts_all :]
    spread = jnp.exp(logits - jnp.max(logits, axis=0, keepdims=True))
    prob = spread / jnp.sum(spread, axis=0, keepdims=True)
    for e in range(experts):
        chosen = picks[e * CAP : (e + 1) * CAP].astype(f32) * prob[e : e + 1, :]
        gate_ref[e] = jnp.broadcast_to(jnp.sum(chosen, axis=1, keepdims=True), (CAP, LANES))
    hidden = dot_nt(block[...], weights_ref[...])
    width = hidden.shape[1] // 2
    act, gate_delta, up_delta = gated(hidden[:, :width], hidden[:, width:], dact_ref[...])
    act_ref[...] = act.astype(bf16)
    delta_ref[:, :width] = gate_delta.astype(bf16)
    delta_ref[:, width:] = up_delta.astype(bf16)


def gated(gate_h, up_h, dact):
    sigmoid_h = jax.nn.sigmoid(gate_h)
    silu_h = gate_h * sigmoid_h
    gate_delta = dact * up_h * sigmoid_h * (1.0 + gate_h * (1.0 - sigmoid_h))
    return silu_h * up_h, gate_delta, dact * silu_h


def hidden_kernel(
    first_ref,
    rows_ref,
    grads_ref,
    gate_ref,
    expert_gate_ref,
    expert_up_ref,
    expert_down_ref,
    act_ref,
    gate_delta_ref,
    up_delta_ref,
    score_ref,
):
    rows = rows_ref[0]
    gate_h = dot_nt(rows, expert_gate_ref[0])
    up_h = dot_nt(rows, expert_up_ref[0])
    dact = dot_nt(grads_ref[0], expert_down_ref[0])
    gate = gate_ref[0][:, :1]
    act, gate_delta, up_delta = gated(gate_h, up_h, dact)
    act_ref[0] = (act * gate).astype(bf16)
    gate_delta_ref[0] = (gate_delta * gate).astype(bf16)
    up_delta_ref[0] = (up_delta * gate).astype(bf16)
    score = jnp.sum(act * dact, axis=1, keepdims=True)
    high = score.astype(bf16).astype(f32)
    lanes = score_ref.shape[2]
    lane = lax.broadcasted_iota(jnp.int32, (rows.shape[0], lanes), 1)
    mine = first_ref[0] + pl.program_id(0)
    score_ref[0] = jnp.where(
        lane == mine, high, jnp.where(lane == mine + lanes // 2, score - high, 0.0)
    ).astype(bf16)


def return_kernel(spec, slots_ref, *refs):
    pairs, scored, added, outputs, steps = spec
    deltas, weights = refs[:pairs], refs[pairs : 2 * pairs]
    shared_ref, shared_weight_ref = refs[2 * pairs : 2 * pairs + 2]
    rest = refs[2 * pairs + 2 :]
    score_ref, rest = (rest[0], rest[1:]) if scored else (None, rest)
    other_ref, rest = (rest[0], rest[1:]) if added else (None, rest)
    outs, picks, rows = rest[:outputs], rest[outputs], rest[outputs + 1]
    sources, _, chunk = rows.shape
    experts = slots_ref.shape[1]
    toks = picks.shape[2]
    step = pl.program_id(0)

    def store(s, columns, value):
        if added:
            value = value + other_ref[s, :, columns].astype(f32)
        out = outs[s // (sources // outputs)]
        out[s % (sources // outputs), :, columns] = value.astype(bf16)

    @pl.when(step == 0)
    def _():
        for s in range(sources):
            picks[s] = pick_matrix(slots_ref[s])
        if scored:
            for s in range(sources):
                score = jnp.concatenate(
                    [score_ref[e, s * CAP : (s + 1) * CAP] for e in range(experts)], axis=0
                )
                store(s, pl.ds(steps * chunk, score.shape[1]), dot_tn(picks[s], score))

    for e in range(experts):
        back = functools.reduce(
            jnp.add, [dot(d[e], w[e]) for d, w in zip(deltas, weights)]
        ).astype(bf16)
        for s in range(sources):
            rows[s, e * CAP : (e + 1) * CAP, :] = back[s * CAP : (s + 1) * CAP]
    columns = pl.ds(pl.multiple_of(step * chunk, chunk), chunk)
    for s in range(sources):
        summed = dot_tn(picks[s], rows[s]) + dot(
            shared_ref[s * toks : (s + 1) * toks], shared_weight_ref[...]
        )
        store(s, columns, summed)


def expert_grad_kernel(
    rows_ref,
    grads_ref,
    act_ref,
    gate_delta_ref,
    up_delta_ref,
    gate_grad_ref,
    up_grad_ref,
    down_grad_ref,
):
    rows = rows_ref[0]
    gate_grad_ref[0] = dot_tn(gate_delta_ref[0], rows)
    up_grad_ref[0] = dot_tn(up_delta_ref[0], rows)
    down_grad_ref[0] = dot_tn(act_ref[0], grads_ref[0])


def shared_grad_kernel(count, parts, src_ref, tensor_ref, delta_ref, act_ref, grad_ref, *refs):
    out_ref, buffer, placed, in_acc, down_acc, sems = refs[count:]
    step = pl.program_id(0)
    block = fetch(refs[:count], buffer, sems)
    rows = placed.shape[0] // parts
    for r, part in enumerate(by_place(grad_ref.at[0], tensor_ref[0], parts)):
        placed[r * rows : (r + 1) * rows] = part

    @pl.when(step == 0)
    def _():
        in_acc[...] = jnp.zeros_like(in_acc)
        down_acc[...] = jnp.zeros_like(down_acc)

    in_acc[...] += dot_tn(delta_ref[...], block[...])
    down_acc[...] += dot_tn(act_ref[...], placed[...])

    @pl.when(step == count - 1)
    def _():
        devices, rows, columns = out_ref.shape
        rows //= 3
        middle = in_acc.shape[0] // 2
        for j in range(devices):
            here = slice(j * columns, (j + 1) * columns)
            out_ref[j, :rows] = in_acc[:rows, here].astype(bf16)
            out_ref[j, rows : 2 * rows] = in_acc[middle : middle + rows, here].astype(bf16)
            out_ref[j, 2 * rows :] = down_acc[:rows, here].astype(bf16)


def rows_grad_kernel(src_ref, left_ref, right_ref, far_ref, near_ref):
    half, rows, _ = far_ref.shape
    for i in range(2 * half):
        start = pl.multiple_of(src_ref[i] * rows, rows)
        product = dot_tn(left_ref[:, pl.ds(start, rows)], right_ref[...]).astype(bf16)
        if i < half:
            far_ref[i] = product
        else:
            near_ref[i - half] = product


def columns_grad_kernel(parts, flat, src_ref, left_ref, logits_ref, block_ref, gain_ref, *refs):
    far_ref, near_ref, grads = refs[parts:]
    rows = left_ref.shape[0] // parts
    for r in range(parts):
        grads[r * rows : (r + 1) * rows] = refs[r][:rows]
    half, height, width = far_ref.shape
    wide, experts_all = left_ref.shape[1], logits_ref.shape[1]
    for i in range(2 * half):
        columns = pl.ds(pl.multiple_of(src_ref[i] * width, width), width)
        out = far_ref.at[i] if i < half else near_ref.at[i - half]
        out[:wide] = dot_tn(left_ref[...], grads[:, columns]).astype(bf16)
        router = dot_tn(logits_ref[...], block_ref[:, columns])
        rest = jnp.concatenate(
            [router, jnp.broadcast_to(gain_ref[:, columns], (height - wide - experts_all, width))],
            axis=0,
        )
        out[wide:] = rest.astype(bf16)


def normed_kernel(tokens_ref, gain_ref, down_ref, rope_ref, normed_ref, inv_ref, narrow_ref):
    normed, inv = rms_norm(tokens_ref[...].astype(f32), gain_ref[...])
    normed = normed.astype(bf16)
    normed_ref[...] = normed
    inv_ref[...] = inv
    cols = down_ref.shape[1]
    narrow_ref[:, :cols] = dot(normed, down_ref[...]).astype(bf16)
    narrow_ref[:, cols:] = dot_nt(normed, rope_ref[...]).astype(bf16)


def query_kernel(normed_ref, weight_ref, cosines_ref, sines_ref, query_ref):
    raw = dot(normed_ref[...], weight_ref[...])
    toks = raw.shape[0]
    for h in range(raw.shape[1] // (HD + RD)):
        start = h * (HD + RD)
        rope = jnp.concatenate(
            [raw[:, start + HD : start + HD + RD], jnp.zeros((toks, LANES - RD), f32)], axis=1
        )
        query_ref[:, h * HEAD : h * HEAD + HD] = raw[:, start : start + HD].astype(bf16)
        query_ref[:, h * HEAD + HD : (h + 1) * HEAD] = rotate(
            rope, cosines_ref[...], sines_ref[...]
        ).astype(bf16)


def causal(scores):
    later = lax.broadcasted_iota(jnp.int32, scores.shape, 1) > lax.broadcasted_iota(
        jnp.int32, scores.shape, 0
    )
    return jnp.where(later, -1e30, scores)


def attention_kernel(
    parts,
    tensor_ref,
    query_ref,
    cosines_ref,
    sines_ref,
    place_ref,
    gain_ref,
    up_ref,
    out_weight_ref,
    *refs,
):
    narrow = [ref[...] for ref in refs[:parts]]
    sums = refs[parts : 2 * parts]
    attended_ref, latent_ref, latent_normed_ref, inv_ref, kv_ref, rope_ref, lse_ref, natural = refs[
        2 * parts :
    ]
    toks = query_ref.shape[0]
    heads = query_ref.shape[1] // HEAD
    cols = up_ref.shape[0] // parts
    latent = jnp.concatenate([n[:, :cols] for n in narrow], axis=1)
    latent_ref[...] = latent
    normed, inv = rms_norm(latent.astype(f32), gain_ref[...])
    normed = normed.astype(bf16)
    latent_normed_ref[...] = normed
    inv_ref[...] = inv
    rope = dot(jnp.concatenate([n[:, cols:] for n in narrow], axis=1), place_ref[...])
    rope = rotate(rope, cosines_ref[...], sines_ref[...]).astype(bf16)
    rope_ref[...] = rope
    kv_ref[...] = dot(normed, up_ref[...]).astype(bf16)
    lane = lax.broadcasted_iota(jnp.int32, (toks, LANES), 1)
    lses = jnp.zeros((toks, LANES), f32)
    for h in range(heads):
        key = jnp.concatenate([kv_ref[:, h * KV : h * KV + HD], rope], axis=1)
        scores = causal(dot_nt(query_ref[:, h * HEAD : (h + 1) * HEAD], key) * (HD + RD) ** -0.5)
        top = jnp.max(scores, axis=1, keepdims=True)
        lse = top + jnp.log(jnp.sum(jnp.exp(scores - top), axis=1, keepdims=True))
        lses = jnp.where(lane == h, lse, lses)
        weights = jnp.exp(scores - lse).astype(bf16)
        natural[:, h * VD : (h + 1) * VD] = dot(
            weights, kv_ref[:, h * KV + HD : (h + 1) * KV]
        ).astype(bf16)
    lse_ref[...] = lses
    rows = toks // parts
    for r, block in enumerate(by_place(natural, tensor_ref[0], parts)):
        attended_ref[r * rows : (r + 1) * rows] = block
    for r in range(parts):
        product = dot(attended_ref[r * rows : (r + 1) * rows], out_weight_ref[...])
        sums[r][...] = product.astype(sums[r].dtype)


def attention_back_kernel(
    parts,
    tensor_ref,
    src_ref,
    query_ref,
    kv_ref,
    rope_ref,
    lse_ref,
    latent_ref,
    latent_normed_ref,
    inv_ref,
    cosines_ref,
    sines_ref,
    place_ref,
    gain_ref,
    up_ref,
    out_weight_ref,
    *refs,
):
    grads = refs[:parts]
    narrow = refs[parts : 2 * parts]
    query_grad_ref, up_far_ref, up_near_ref, natural, query_nat, kv_grad, narrow_nat, up_part = refs[
        2 * parts :
    ]
    toks = query_ref.shape[0]
    heads = query_ref.shape[1] // HEAD
    rows = toks // parts
    factor = (HD + RD) ** -0.5
    tensor = tensor_ref[0]
    for r in range(parts):
        place = pl.ds(pl.multiple_of((tensor ^ r) * rows, rows), rows)
        natural[place, :] = dot_nt(grads[r][:rows], out_weight_ref[...]).astype(bf16)
    rope = rope_ref[...]
    rope_sum = jnp.zeros((toks, LANES), f32)
    for h in range(heads):
        grad = natural[:, h * VD : (h + 1) * VD]
        query = query_ref[:, h * HEAD : (h + 1) * HEAD]
        key = jnp.concatenate([kv_ref[:, h * KV : h * KV + HD], rope], axis=1)
        scores = causal(dot_nt(query, key) * factor)
        probs = jnp.exp(scores - lse_ref[:, h : h + 1])
        kv_grad[:, h * KV + HD : (h + 1) * KV] = dot_tn(probs.astype(bf16), grad).astype(bf16)
        prob_dot = dot_nt(grad, kv_ref[:, h * KV + HD : (h + 1) * KV])
        inner = jnp.sum(probs * prob_dot, axis=1, keepdims=True)
        score_grad = (probs * (prob_dot - inner) * factor).astype(bf16)
        query_grad = dot(score_grad, key)
        start = h * (HD + RD)
        query_nat[:, start : start + HD] = query_grad[:, :HD].astype(bf16)
        query_nat[:, start + HD : start + HD + RD] = rotate(
            query_grad[:, HD:], cosines_ref[...], -sines_ref[...]
        )[:, :RD].astype(bf16)
        key_grad = dot_tn(score_grad, query)
        kv_grad[:, h * KV : h * KV + HD] = key_grad[:, :HD].astype(bf16)
        rope_sum = rope_sum + key_grad[:, HD:]
    for r, block in enumerate(by_place(query_nat, tensor, parts)):
        query_grad_ref[r * rows : (r + 1) * rows] = block
    latent_grad, _ = rms_back(
        dot_nt(kv_grad[...], up_ref[...]), latent_ref[...].astype(f32), inv_ref[...], gain_ref[...]
    )
    rope_sum = rotate(rope_sum, cosines_ref[...], -sines_ref[...]).astype(bf16)
    rope_sum = dot_nt(rope_sum, place_ref[...])
    cols = latent_grad.shape[1] // parts
    rope_cols = rope_sum.shape[1] // parts
    for k in range(parts):
        narrow_nat[:, :cols] = latent_grad[:, k * cols : (k + 1) * cols]
        narrow_nat[:, cols:] = rope_sum[:, k * rope_cols : (k + 1) * rope_cols]
        narrow[k][...] = narrow_nat[...].astype(narrow[k].dtype)
    up_part[...] = dot_tn(latent_normed_ref[...], kv_grad[...])
    half, up_rows, _ = up_far_ref.shape
    for i in range(2 * half):
        start = src_ref[i] * up_rows
        start = (start // cols ^ tensor) * cols + start % cols
        block = up_part[pl.ds(pl.multiple_of(start, up_rows), up_rows), :].astype(bf16)
        if i < half:
            up_far_ref[i] = block
        else:
            up_near_ref[i - half] = block


def normed_back_kernel(parts, tensor_ref, query_grad_ref, query_weight_ref, down_ref, rope_ref, *refs):
    narrow = refs[:parts]
    sums = refs[parts : 2 * parts]
    all_ref, natural = refs[2 * parts :]
    cols = down_ref.shape[1]
    natural[...] = total([ref[...] for ref in narrow])
    mine = jnp.concatenate(by_place(natural, tensor_ref[0], parts), axis=0).astype(bf16)
    all_ref[...] = mine
    rows = query_grad_ref.shape[0] // parts
    product = (
        dot_nt(query_grad_ref[...], query_weight_ref[...])
        + dot_nt(mine[:, :cols], down_ref[...])
        + dot(mine[:, cols:], rope_ref[...])
    )
    for r in range(parts):
        sums[r][...] = product[r * rows : (r + 1) * rows].astype(sums[r].dtype)


ANYWHERE = pl.BlockSpec(memory_space=pl.ANY)


def whole(array):
    rank = len(array.shape)
    return pl.BlockSpec(array.shape, lambda *_: (0,) * rank)


def params(mib):
    return pltpu.CompilerParams(vmem_limit_bytes=mib * MIB)


def cost(flops, bytes_accessed, transcendentals=0):
    return pl.CostEstimate(
        flops=int(flops * 4),
        bytes_accessed=int(bytes_accessed * 4),
        transcendentals=int(transcendentals * 4),
    )


def pick_grads(src, tensor, parts, slots, grads, shared_down):
    count, experts, toks = slots.shape
    width = grads.shape[2]
    shared = shared_down.shape[0]
    return pl.pallas_call(
        functools.partial(pick_grad_kernel, parts),
        grid_spec=pltpu.PrefetchScalarGridSpec(
            num_scalar_prefetch=2,
            grid=(count,),
            in_specs=[
                pl.BlockSpec((1, experts, toks), lambda s, src, t: (s, 0, 0)),
                pl.BlockSpec((1, toks, width), lambda s, src, t: (src[s], 0, 0)),
                whole(shared_down),
            ],
            out_specs=[
                pl.BlockSpec((experts, CAP, width), lambda s, src, t: (0, s, 0)),
                pl.BlockSpec((toks, shared), lambda s, src, t: (s, 0)),
            ],
            scratch_shapes=[pltpu.VMEM((toks, width), bf16)],
        ),
        out_shape=[
            jax.ShapeDtypeStruct((experts, count * CAP, width), bf16),
            jax.ShapeDtypeStruct((count * toks, shared), f32),
        ],
        compiler_params=params(VMEM),
        cost_estimate=cost(
            2 * count * toks * width * (experts * CAP + shared), 4 * count * toks * width
        ),
    )(src, tensor, slots, grads, shared_down)


def pick_rows(blocks, places, slots, router, weights, dact, experts_all, results):
    count = len(blocks)
    run = next(i for i in range(1, count) if places[i] != places[i - 1] + 1)
    first, skip = places[0], places[run] - places[0] - run

    def place(s):
        return s + first + jnp.where(s < run, 0, skip)

    every, experts, toks = slots.shape
    width = blocks[0].shape[1]
    shared = dact.shape[1]
    operands = [slots, router, weights, dact, *blocks, *results]
    return pl.pallas_call(
        functools.partial(pick_kernel, count, experts_all, len(results)),
        grid=(count,),
        in_specs=[
            pl.BlockSpec((1, experts, toks), lambda s: (place(s), 0, 0)),
            whole(router),
            whole(weights),
            pl.BlockSpec((toks, shared), lambda s: (place(s), 0)),
        ]
        + [ANYWHERE] * (count + len(results)),
        out_specs=[
            pl.BlockSpec((experts, CAP, width), lambda s: (0, place(s), 0)),
            pl.BlockSpec((experts, CAP, LANES), lambda s: (0, place(s), 0)),
            pl.BlockSpec((toks, shared), lambda s: (place(s), 0)),
            pl.BlockSpec((toks, 2 * shared), lambda s: (place(s), 0)),
        ],
        out_shape=[
            shape(bf16, experts, every * CAP, width),
            shape(f32, experts, every * CAP, LANES),
            shape(bf16, every * toks, shared),
            shape(bf16, every * toks, 2 * shared),
        ],
        input_output_aliases={len(operands) - len(results) + i: i for i in range(len(results))},
        scratch_shapes=[
            pltpu.VMEM((count, toks, width), bf16),
            pltpu.SemaphoreType.DMA((count,)),
        ],
        compiler_params=params(VMEM),
        cost_estimate=cost(
            2 * count * toks * width * (experts * CAP + router.shape[0] + 2 * shared),
            4 * count * toks * width,
        ),
    )(*operands)


def expert_hidden(first, rows, grads, gate, expert_gate, expert_up, expert_down, lanes):
    experts, slot_rows, width = rows.shape
    hidden = expert_gate.shape[1]

    def per_expert(array):
        return pl.BlockSpec((1,) + array.shape[1:], lambda e: (e, 0, 0))

    narrow = jax.ShapeDtypeStruct((experts, slot_rows, hidden), bf16)
    score = jax.ShapeDtypeStruct((experts, slot_rows, lanes), bf16)
    return pl.pallas_call(
        hidden_kernel,
        grid=(experts,),
        in_specs=[pl.BlockSpec(memory_space=pltpu.SMEM)]
        + [per_expert(a) for a in (rows, grads, gate, expert_gate, expert_up, expert_down)],
        out_specs=[per_expert(narrow)] * 3 + [per_expert(score)],
        out_shape=[narrow] * 3 + [score],
        compiler_params=params(VMEM),
        cost_estimate=cost(
            6 * experts * slot_rows * width * hidden,
            experts * (4 * slot_rows * width + 6 * hidden * width),
            experts * slot_rows * hidden,
        ),
    )(first, rows, grads, gate, expert_gate, expert_up, expert_down)


def return_rows(half, slots, deltas, weights, shared, shared_weight, score, start, size, other):
    experts, slot_rows, hidden = deltas[0].shape
    sources = slots.shape[0] // 2
    toks = slots.shape[2]
    chunk = min(512, size)
    steps = size // chunk
    first = start // chunk
    outputs = 1 + half
    lanes = 0 if score is None else score.shape[2]
    in_specs = (
        [pl.BlockSpec((sources,) + slots.shape[1:], lambda n: (half, 0, 0))]
        + [pl.BlockSpec((experts, slot_rows // 2, hidden), lambda n: (0, half, 0))] * len(deltas)
        + [pl.BlockSpec((experts, hidden, chunk), lambda n: (0, 0, n + first))] * len(weights)
        + [
            pl.BlockSpec((sources * toks, shared.shape[1]), lambda n: (half, 0)),
            pl.BlockSpec((shared.shape[1], chunk), lambda n: (0, n + first)),
        ]
    )
    operands = [slots, *deltas, *weights, shared, shared_weight]
    if score is not None:
        in_specs.append(pl.BlockSpec((experts, slot_rows // 2, lanes), lambda n: (0, half, 0)))
        operands.append(score)
    if other is not None:
        in_specs.append(whole(other))
        operands.append(other)
    out = jax.ShapeDtypeStruct((sources // outputs, toks, size + lanes), bf16)
    return pl.pallas_call(
        functools.partial(
            return_kernel, (len(deltas), score is not None, other is not None, outputs, steps)
        ),
        grid=(steps,),
        in_specs=in_specs,
        out_specs=[whole(out)] * outputs,
        out_shape=[out] * outputs,
        scratch_shapes=[
            pltpu.VMEM((sources, experts * CAP, toks), bf16),
            pltpu.VMEM((sources, experts * CAP, chunk), bf16),
        ],
        compiler_params=params(VMEM),
        cost_estimate=cost(
            2 * experts * slot_rows // 2 * size * (hidden * len(deltas) + toks)
            + 2 * sources * toks * size * shared.shape[1],
            2 * size * (experts * hidden * len(deltas) + sources * toks),
        ),
    )(*operands)


def expert_grads(rows, grads, act, gate_delta, up_delta):
    experts, slot_rows, width = rows.shape
    hidden = act.shape[2]

    def per_expert(array):
        return pl.BlockSpec((1,) + array.shape[1:], lambda e: (e, 0, 0))

    out = jax.ShapeDtypeStruct((experts, hidden, width), f32)
    return pl.pallas_call(
        expert_grad_kernel,
        grid=(experts,),
        in_specs=[per_expert(a) for a in (rows, grads, act, gate_delta, up_delta)],
        out_specs=[per_expert(out)] * 3,
        out_shape=[out] * 3,
        compiler_params=params(VMEM),
        cost_estimate=cost(
            6 * experts * slot_rows * width * hidden,
            experts * (4 * slot_rows * width + 12 * hidden * width),
        ),
    )(rows, grads, act, gate_delta, up_delta)


def shared_grads(src, tensor, parts, blocks, grads, delta, act, cols):
    count = grads.shape[0]
    toks, width = blocks[0].shape
    out = jax.ShapeDtypeStruct((count, 3 * cols, width // count), bf16)
    return pl.pallas_call(
        functools.partial(shared_grad_kernel, count, parts),
        grid_spec=pltpu.PrefetchScalarGridSpec(
            num_scalar_prefetch=2,
            grid=(count,),
            in_specs=[
                pl.BlockSpec((toks, delta.shape[1]), lambda s, src, t: (s, 0)),
                pl.BlockSpec((toks, act.shape[1]), lambda s, src, t: (s, 0)),
                pl.BlockSpec((1, toks, width), lambda s, src, t: (src[s], 0, 0)),
            ]
            + [ANYWHERE] * count,
            out_specs=whole(out),
            scratch_shapes=[
                pltpu.VMEM((count, toks, width), bf16),
                pltpu.VMEM((toks, width), bf16),
                pltpu.VMEM((delta.shape[1], width), f32),
                pltpu.VMEM((act.shape[1], width), f32),
                pltpu.SemaphoreType.DMA((count,)),
            ],
        ),
        out_shape=out,
        compiler_params=params(VMEM),
        cost_estimate=cost(
            2 * count * toks * width * (delta.shape[1] + act.shape[1]), 4 * count * toks * width
        ),
    )(src, tensor, delta, act, grads, *blocks)


def single(kernel, outs, operands, scalars=(), scratch=(), flops=0, transcendentals=0):
    return pl.pallas_call(
        kernel,
        grid_spec=pltpu.PrefetchScalarGridSpec(
            num_scalar_prefetch=len(scalars),
            grid=(1,),
            in_specs=[whole(a) for a in operands],
            out_specs=[whole(o) for o in outs],
            scratch_shapes=list(scratch),
        ),
        out_shape=list(outs),
        compiler_params=params(VMEM),
        cost_estimate=cost(flops, sum(a.size * a.dtype.itemsize for a in operands), transcendentals),
    )(*scalars, *operands)


def shape(dtype, *sizes):
    return jax.ShapeDtypeStruct(sizes, dtype)


def on_device(
    tokens,
    cotangent,
    attn_gain,
    q_weight,
    kv_down,
    k_rope_weight,
    kv_gain,
    kv_up,
    o_weight,
    ffn_gain,
    router_weight,
    expert_ids,
    expert_gate,
    expert_up,
    expert_down,
    shared_gate,
    shared_up,
    shared_down,
):
    n_t = lax.axis_size("tensor")
    n_d = lax.axis_size("dp")
    half = n_d // 2
    t_index = lax.axis_index("tensor")
    d_index = lax.axis_index("dp")
    toks, width = tokens.shape
    own_toks = toks // n_t
    rows_d = width // n_d
    q_cols = q_weight.shape[1]
    heads = q_cols // (HD + RD)
    experts_all = router_weight.shape[1]
    experts = expert_gate.shape[0]
    cosines, sines = rope_tables()
    order = partner_order()
    src = d_index.astype(jnp.int32) ^ order
    sources = [src[i] for i in range(n_d)]
    lat_cols = kv_down.shape[1]
    lat_rank = kv_up.shape[0]
    rope_cols = k_rope_weight.shape[1]
    narrow_cols = lat_cols + rope_cols
    expert_gate_t = expert_gate.transpose(0, 2, 1)
    expert_up_t = expert_up.transpose(0, 2, 1)

    tokens_p = by_partner(tokens, "tensor", 0)
    tokens_own = tokens_p[0].astype(f32)
    cot_own = block_at(cotangent, t_index, own_toks, 0).astype(f32)
    tensor = t_index.astype(jnp.int32).reshape(1)
    every = jnp.arange(experts_all, dtype=jnp.int32)
    member = jnp.any(expert_ids.T[:, None, :] == every[None, :, None], axis=0)
    before = (jnp.arange(toks)[:, None] < jnp.arange(toks)[None, :]).astype(bf16)
    rank = dot(member.astype(bf16), before)
    slots_own = jnp.where(member, rank, -1.0).astype(bf16).reshape(-1, width)
    slot_rows = slots_own.shape[0]
    slots_own = jnp.pad(slots_own, ((0, -slot_rows % 16), (0, 0)))
    cot_all = lax.all_gather(jnp.concatenate([cotangent, slots_own], axis=0), "dp")
    slots = cot_all[:, toks : toks + slot_rows].reshape(n_d, experts_all, toks)
    slots = reorder(block_at(slots, d_index, experts, 1), "tensor", 2)
    slots = jnp.concatenate([block_at(slots, s, 1, 0) for s in sources], axis=0).astype(jnp.int32)
    router_t = jnp.roll(router_weight.T, -d_index * experts, axis=0)
    router_parts = []
    rest = router_t
    for _ in range(3):
        part = lax.reduce_precision(rest, 8, 7)
        router_parts.append(part.astype(bf16))
        rest = rest - part
    router_parts = jnp.concatenate(router_parts, axis=0)
    shared_cols = shared_down.shape[0] // n_d
    shared_pad = -shared_cols % LANES
    shared_gate_t, shared_up_t, shared_out = [
        jnp.pad(block_at(w, d_index, shared_cols, 0), ((0, shared_pad), (0, 0)))
        for w in (shared_gate.T, shared_up.T, shared_down)
    ]
    shared_in = jnp.concatenate([shared_gate_t, shared_up_t], axis=0)
    grad_rows, shared_dact = pick_grads(src, tensor, n_t, slots, cot_all, shared_out)

    kv_up_p = reorder(kv_up, "tensor", 0)
    kv_gain_p = reorder(kv_gain, "tensor", 0)[None]
    rope_t = k_rope_weight.T
    rope_place = (
        (t_index ^ jnp.arange(n_t)[:, None, None]) * rope_cols + jnp.arange(rope_cols)[None, :, None]
        == jnp.arange(LANES)
    ).astype(bf16).reshape(RD, LANES)
    normed, inv_first, narrow_own = single(
        normed_kernel,
        [shape(bf16, toks, width), shape(f32, toks, 1), shape(bf16, toks, narrow_cols)],
        [tokens, attn_gain[None], kv_down, rope_t],
        flops=2 * toks * width * narrow_cols,
    )
    narrow_blocks = share(narrow_own, "tensor")
    query = single(
        query_kernel,
        [shape(bf16, toks, heads * HEAD)],
        [normed, q_weight, cosines, sines],
        flops=2 * toks * width * q_cols,
    )[0]
    results = single(
        functools.partial(attention_kernel, n_t),
        [shape(f32 if r == 0 else bf16, own_toks, width) for r in range(n_t)]
        + [
            shape(bf16, toks, heads * VD),
            shape(bf16, toks, lat_rank),
            shape(bf16, toks, lat_rank),
            shape(f32, toks, 1),
            shape(bf16, toks, heads * KV),
            shape(bf16, toks, LANES),
            shape(f32, toks, LANES),
        ],
        [query, cosines, sines, rope_place, kv_gain_p, kv_up_p, o_weight, *narrow_blocks],
        scalars=[tensor],
        scratch=[pltpu.VMEM((toks, heads * VD), bf16)],
        flops=2 * toks * heads * (KV * lat_rank + 2 * HEAD * toks + VD * width),
        transcendentals=2 * heads * toks * toks,
    )
    attn_part = results[:n_t]
    attended_p, latent, latent_normed, inv_latent, key_value, rope_rot, lse = results[n_t:]
    attn_sum = total(
        after(trade(attn_part, "tensor"), router_parts, shared_in, shared_out, inv_first, kv_up_p)
    )
    hidden_one = tokens_own + attn_sum
    ffn_normed_f, inv_second = rms_norm(hidden_one, ffn_gain)
    ffn_own = ffn_normed_f.astype(bf16)
    ffn_block = jnp.concatenate(share(ffn_own, "tensor"), axis=0)
    near_blocks = gather_chips(ffn_block, grad_rows)
    far_blocks = [swap(block, "dp", 1) for block in near_blocks[:-1]]

    def pick(places, blocks_here, results):
        return pick_rows(
            blocks_here, places, slots, router_parts, shared_in, shared_dact, experts_all, results
        )

    early = [0] + list(range(half, n_d - 1))
    results = pick(early, far_blocks[:1] + near_blocks[:-1], [])
    far_blocks.append(swap(after(near_blocks[-1], results), "dp", 1))
    late = list(range(1, half)) + [n_d - 1]
    blocks = far_blocks + near_blocks

    results = pick(late, [blocks[i] for i in late], results)
    rows, gate, shared_act, shared_delta = results
    lanes = -(-2 * experts_all // LANES) * LANES
    first = (d_index * experts).astype(jnp.int32).reshape(1)
    act, gate_delta, up_delta, score = expert_hidden(
        first, rows, grad_rows, gate, expert_gate_t, expert_up_t, expert_down, lanes
    )

    def send_back(sum_here):
        return trade(
            [sum_here[k * own_toks : (k + 1) * own_toks].astype(bf16) for k in range(n_t)], "tensor"
        )

    pieces = 2
    size = width // pieces
    deltas, delta_weights = [gate_delta, up_delta], [expert_gate_t, expert_up_t]
    others = [
        return_rows(
            0, slots, deltas, delta_weights, shared_delta, shared_in,
            score if i == pieces - 1 else None, i * size, size, None,
        )[0]
        for i in range(pieces)
    ]
    others = [swap(other, "dp", 1) for other in others]
    mine = [
        return_rows(
            1, slots, deltas, delta_weights, shared_delta, shared_in,
            score if i == pieces - 1 else None, i * size, size, others[i],
        )
        for i in range(pieces)
    ]
    out_other = []

    def beside(step, arrived):
        if step:
            return arrived
        out_other.extend(
            return_rows(
                0, slots, [after(act, arrived[0], mine[1:])], [expert_down], shared_act, shared_out,
                None, 0, width, None,
            )
        )
        return arrived[:1] + after(arrived[1:], out_other)

    sums, arrivals = sum_chips(mine, beside)
    shared_rows = shared_cols + -shared_cols % 16
    back_sums = [total(send_back(s)) for s in sums]
    back_sum = jnp.concatenate(back_sums[:-1] + [back_sums[-1][:, :size]], axis=1)
    score_sum = back_sums[-1][:, size:]
    logits = jnp.dot(ffn_own.astype(f32), router_weight, precision=lax.Precision.HIGHEST)
    router_prob = jax.nn.softmax(logits, axis=-1)
    prob_grad = score_sum[:, :experts_all] + score_sum[:, lanes // 2 : lanes // 2 + experts_all]
    logit_grad = (
        router_prob * (prob_grad - jnp.sum(router_prob * prob_grad, axis=-1, keepdims=True))
    ).astype(bf16)
    ffn_normed_grad = back_sum + jnp.dot(
        logit_grad.astype(f32), router_weight.T, precision=lax.Precision.HIGHEST
    )
    hidden_norm_grad, ffn_gain_part = rms_back(ffn_normed_grad, hidden_one, inv_second, ffn_gain)
    hidden_grad = cot_own + hidden_norm_grad
    flat_logits = logit_grad.reshape(-1, width)
    flat = flat_logits.shape[0]
    extra = jnp.concatenate(
        [
            flat_logits,
            ffn_gain_part.astype(bf16)[None],
            jnp.zeros((-(flat + 1) % 8, width), bf16),
        ],
        axis=0,
    )
    message = jnp.concatenate([hidden_grad.astype(bf16), extra], axis=0)
    shared_grads_t = share(message, "tensor")
    out_pair = return_rows(
        1, slots, [act], [expert_down], shared_act, shared_out, None, 0, width,
        after(swap(out_other[0], "dp", 1), message),
    )
    shared_all = shared_grads(
        src, tensor, n_t, blocks, cot_all, *after((shared_delta, shared_act), out_pair), shared_rows
    )
    shared_grads_t = after(shared_grads_t, shared_all)

    lat_rows = lat_rank // n_d
    results = single(
        functools.partial(attention_back_kernel, n_t),
        [shape(f32 if r == 0 else bf16, toks, narrow_cols) for r in range(n_t)]
        + [
            shape(bf16, toks, q_cols),
            shape(bf16, half, lat_rows, heads * KV),
            shape(bf16, half, lat_rows, heads * KV),
        ],
        [
            query, key_value, rope_rot, lse, latent, latent_normed, inv_latent, cosines, sines,
            rope_place, kv_gain_p, kv_up_p, o_weight, *shared_grads_t,
        ],
        scalars=[tensor, src],
        scratch=[
            pltpu.VMEM((toks, heads * VD), bf16),
            pltpu.VMEM((toks, q_cols), bf16),
            pltpu.VMEM((toks, heads * KV), bf16),
            pltpu.VMEM((toks, narrow_cols), f32),
            pltpu.VMEM((lat_rank, heads * KV), f32),
        ],
        flops=2 * toks * heads * (2 * KV * lat_rank + 5 * HEAD * toks + VD * width),
        transcendentals=heads * toks * toks,
    )
    latent_parts = results[:n_t]
    query_grad_p, kv_up_far, kv_up_near = results[n_t:]
    normed_p = reorder(normed, "tensor", 0)

    def rows_grad(left, right):
        return single(
            rows_grad_kernel,
            [shape(bf16, half, rows_d, right.shape[1])] * 2,
            [left, right],
            scalars=[src],
            flops=2 * toks * width * right.shape[1],
        )

    logit_p = jnp.concatenate(
        [b[own_toks : own_toks + flat].reshape(own_toks, experts_all) for b in shared_grads_t], axis=0
    )
    gain_part = total([b[own_toks + flat] for b in shared_grads_t])[None]
    out_cols = attended_p.shape[1]
    height = out_cols + experts_all + 16
    column_terms = single(
        functools.partial(columns_grad_kernel, n_t, flat),
        [shape(bf16, half, height, rows_d)] * 2,
        [after(attended_p, query_grad_p), logit_p, ffn_block, gain_part, *shared_grads_t],
        scalars=[src],
        scratch=[pltpu.VMEM((toks, width), bf16)],
        flops=2 * toks * width * height,
    )
    query_terms = rows_grad(normed_p, query_grad_p)
    terms = [query_terms, column_terms, (kv_up_far, kv_up_near)]
    latent_parts = after(trade(latent_parts, "tensor"), terms)
    out_sums, out_steps = sum_chips([out_pair], lambda step, arrived: after(arrived, latent_parts))
    out_here = out_sums[0]
    out_rows = {r: out_here[r * own_toks : (r + 1) * own_toks] for r in range(n_t)}
    results = single(
        functools.partial(normed_back_kernel, n_t),
        [shape(f32 if r == 0 else bf16, own_toks, width) for r in range(n_t)]
        + [shape(bf16, toks, narrow_cols)],
        [query_grad_p, q_weight, kv_down, rope_t, *latent_parts],
        scalars=[tensor],
        scratch=[pltpu.VMEM((toks, narrow_cols), f32)],
        flops=2 * toks * width * (q_cols + narrow_cols),
    )
    normed_part, narrow_p = results[:n_t], results[n_t]
    query_pairs = sum_cores(after(terms[:1], normed_part))
    expert_gate_grad, expert_up_grad, expert_down_grad = expert_grads(
        rows, grad_rows, *after((act, gate_delta, up_delta), query_pairs[0][1], out_steps[1])
    )
    shared_sent = lax.all_to_all(after(shared_all, expert_gate_grad), "dp", 0, 0, tiled=True).astype(f32)
    shared_gate_grad, shared_up_grad, shared_down_grad = [
        shared_sent[:, i * shared_rows : i * shared_rows + shared_cols].reshape(-1, rows_d)
        for i in range(3)
    ]
    out_message = after(
        jnp.concatenate([out_rows[r].astype(bf16) for r in out_rows if r & 1], axis=0),
        expert_gate_grad,
    )
    out_sent = swap(out_message, "tensor", 1)
    normed_arrived = after(trade(normed_part, "tensor"), expert_gate_grad)
    normed_grad = total(normed_arrived)
    (q_weight_grad,), term_arrivals = sum_chips(query_pairs)
    terms = terms[1:] + [rows_grad(normed_p, after(narrow_p, expert_gate_grad))]
    pairs = after(sum_cores(after(terms, expert_gate_grad, out_message)), term_arrivals[0])
    (columns, kv_up_grad, narrow_grad), chain = sum_chips(
        pairs, lambda step, arrived: after(arrived, term_arrivals[min(2 * step + 2, len(term_arrivals) - 2)])
    )
    sends = [send for _, send in pairs] + term_arrivals[1]
    out_sum = sum_along(
        out_rows, after(out_sent, normed_arrived[1:], sends), "tensor", chain[1] or sends
    )
    output_own = (hidden_one + out_sum).astype(bf16)
    output_blocks = share(after(output_own, chain[-2]), "tensor")
    inv_first_own = block_at(inv_first, t_index, own_toks, 0)
    input_norm_grad, _ = rms_back(normed_grad, tokens_own, inv_first_own, attn_gain)
    input_grad = hidden_grad + input_norm_grad

    o_weight_grad = columns[:out_cols]
    device_rows = width // (n_d * n_t)
    router_grad = block_at(
        columns[out_cols : out_cols + experts_all], t_index, device_rows, 1
    ).T
    ffn_gain_grad = block_at(columns[out_cols + experts_all], t_index, device_rows, 0)
    kv_down_grad = narrow_grad[:, :lat_cols]
    k_rope_grad = narrow_grad[:, lat_cols:]

    attn_gain_part = jnp.sum(
        block_at(q_weight, d_index, rows_d, 0).astype(f32) * q_weight_grad, axis=1
    ) + jnp.sum(
        block_at(kv_down, d_index, rows_d, 0).astype(f32) * kv_down_grad, axis=1
    ) + jnp.sum(
        block_at(k_rope_weight, d_index, rows_d, 0).astype(f32) * k_rope_grad, axis=1
    )
    attn_gain_part = attn_gain_part / block_at(attn_gain, d_index, rows_d, 0)
    kv_gain_part = jnp.sum(
        block_at(kv_up, d_index, lat_rows, 0).astype(f32) * kv_up_grad, axis=1
    ) / block_at(kv_gain, d_index, lat_rows, 0)
    gains = jnp.concatenate(
        [attn_gain_part.reshape(n_t, 1, -1), kv_gain_part.reshape(n_t, 1, -1)], axis=2
    )
    gains = total(trade([b[0] for b in by_partner(gains, "tensor", 0)], "tensor"))[0]
    output = reorder(jnp.concatenate(after(output_blocks, gains), axis=0), "tensor", 0)
    attn_gain_grad = gains[:device_rows]
    kv_gain_grad = gains[device_rows:]

    return (
        output,
        input_grad,
        attn_gain_grad,
        q_weight_grad,
        kv_down_grad,
        k_rope_grad,
        kv_gain_grad,
        kv_up_grad,
        o_weight_grad,
        ffn_gain_grad,
        router_grad,
        shared_gate_grad.T,
        shared_up_grad.T,
        shared_down_grad,
        expert_gate_grad.transpose(0, 2, 1),
        expert_up_grad.transpose(0, 2, 1),
        expert_down_grad,
    )


def solution(mesh):
    in_specs = (
        P("dp", None),
        P("dp", None),
        P(),
        P(None, "tensor"),
        P(None, "tensor"),
        P(None, "tensor"),
        P(),
        P(None, "tensor"),
        P("tensor", None),
        P(),
        P(),
        P("dp", None),
        P("dp", None, "tensor"),
        P("dp", None, "tensor"),
        P("dp", "tensor", None),
        P(None, "tensor"),
        P(None, "tensor"),
        P("tensor", None),
    )
    out_specs = (
        P("dp", None),
        P(("dp", "tensor"), None),
        P(("dp", "tensor")),
        P("dp", "tensor"),
        P("dp", "tensor"),
        P("dp", "tensor"),
        P(("dp", "tensor")),
        P("dp", "tensor"),
        P("tensor", "dp"),
        P(("dp", "tensor")),
        P(("dp", "tensor"), None),
        P("dp", "tensor"),
        P("dp", "tensor"),
        P("tensor", "dp"),
        P("dp", None, "tensor"),
        P("dp", None, "tensor"),
        P("dp", "tensor", None),
    )
    return jax.shard_map(
        on_device, mesh=mesh, in_specs=in_specs, out_specs=out_specs, check_vma=False
    )
```
